32 devices in a mesh: fsdp: 4 (over z), ctx: 2 (over x), tp: 4 (over y, core).
Axes of the slice: x: 2, y: 2, z: 4, core: 2. Of those that a mesh axis runs over, the one named last changes fastest.
Arguments:
- tokens: bfloat16 [4, 1024, 1024], P('fsdp', 'ctx'), may hold values from -16 to 16
- segments: int32 [4, 1024], P('fsdp'), may hold values from 0 to 1023, as said below
- w_qkv: bfloat16 [1024, 3, 1024], P(('fsdp', 'ctx'), None, 'tp'), may hold values from -0.1875 to 0.1875
- b_qv: bfloat16 [2, 16, 64], P(None, 'tp', ('fsdp', 'ctx')), may hold values from -0.59765625 to 0.59765625
- w_out: bfloat16 [1024, 1024], P('tp', ('fsdp', 'ctx')), may hold values from -0.75 to 0.75
- b_out: bfloat16 [1024], P(('fsdp', 'ctx')), may hold values from -3 to 3
- w_up: bfloat16 [1024, 4096], P(('fsdp', 'ctx'), 'tp'), may hold values from -0.1875 to 0.1875
- b_up: bfloat16 [64, 64], P('tp', ('fsdp', 'ctx')), may hold values from -3 to 3
- w_down: bfloat16 [4096, 1024], P('tp', ('fsdp', 'ctx')), may hold values from -0.09375 to 0.09375
- b_down: bfloat16 [1024], P(('fsdp', 'ctx')), may hold values from -3 to 3
- attngain: bfloat16 [1024], P(('fsdp', 'ctx')), may hold values from 0.5 to 1.5
- attnshift: bfloat16 [1024], P(('fsdp', 'ctx')), may hold values from -3 to 3
- mlpgain: bfloat16 [1024], P(('fsdp', 'ctx')), may hold values from 0.5 to 1.5
- mlpshift: bfloat16 [1024], P(('fsdp', 'ctx')), may hold values from -3 to 3
- cotangent: bfloat16 [4, 1024, 1024], P('fsdp', 'ctx'), may hold values from -6 to 6
Outputs:
- block_out: bfloat16 [4, 1024, 1024], P('fsdp', 'ctx')
- grad_tokens: float32 [4, 1024, 1024], P('fsdp', 'ctx')
- grad_wqkv: float32 [1024, 3, 1024], P(('fsdp', 'ctx'), None, 'tp')
- grad_bqv: float32 [2, 16, 64], P(None, 'tp', ('fsdp', 'ctx'))
- grad_wout: float32 [1024, 1024], P('tp', ('fsdp', 'ctx'))
- grad_bout: float32 [1024], P(('fsdp', 'ctx'))
- grad_wup: float32 [1024, 4096], P(('fsdp', 'ctx'), 'tp')
- grad_bup: float32 [64, 64], P('tp', ('fsdp', 'ctx'))
- grad_wdown: float32 [4096, 1024], P('tp', ('fsdp', 'ctx'))
- grad_bdown: float32 [1024], P(('fsdp', 'ctx'))
- grad_attngain: float32 [1024], P(('fsdp', 'ctx'))
- grad_attnshift: float32 [1024], P(('fsdp', 'ctx'))
- grad_mlpgain: float32 [1024], P(('fsdp', 'ctx'))
- grad_mlpshift: float32 [1024], P(('fsdp', 'ctx'))
The draws below stay inside these ranges and needn't reach their ends.
Inputs may be any that keep to these rules, and one draw needn't show every extreme that they name: `segments`: in each sequence the numbers start at 0 and never fall along it; equal numbers mark one document; the last document of every sequence has the number 1024 - 1.
All inputs are finite; a program needn't handle non-finite values.
Results may differ from the reference program's by a relative error of at most 0.018.
Values may be sent and summed in bfloat16 or wider, within the bound.
No kernel may reach another device: no remote copies, remote signals or barrier semaphores. Data moves between devices by JAX's collectives and lax.ppermute only.
A program may use at most 128 MiB of HBM per device.

```python
import jax
import jax.numpy as jnp
from jax import lax

D = 1024
HEADS = 16
HD = 64
FF = 4096
LEN = 1024
BLOCK = 512
SEQS = 4


def draw_tokens(key, part):
    key = jax.random.fold_in(key, 11)
    key_one, key_two = jax.random.split(key, 2)
    columns = jnp.exp(jax.random.uniform(key_one, (D,), jnp.float32, -1.1512925, 1.1512925))
    noise_vals = jnp.clip(jax.random.normal(key_two, (SEQS, LEN, D), jnp.float32), -5.0, 5.0)
    return (noise_vals * columns).astype(jnp.bfloat16)


def draw_segments(key, part):
    key = jax.random.fold_in(key, 7)
    key_one, key_two, key_three = jax.random.split(key, 3)
    doc_begin = jax.random.randint(key_one, (SEQS, 1), 1, BLOCK)
    finish = jax.random.randint(key_two, (SEQS, 1), LEN - BLOCK + 1, LEN)
    spot_index = jnp.arange(LEN, dtype=jnp.int32)[None, :]
    coin_flips = jax.random.randint(key_three, (SEQS, LEN), 0, 160)
    starts = jnp.where((coin_flips == 0) & (spot_index < doc_begin), 1, 0)
    starts = jnp.where((spot_index == doc_begin) | (spot_index == finish) | (spot_index == 0), 1, starts)
    numbers = jnp.cumsum(starts, axis=1) - 1
    numbers = jnp.where(spot_index >= finish, LEN - 1, numbers)
    return numbers.astype(jnp.int32)


def shard_levels(key, extent, cuts, least, largest):
    def one(position, blocks):
        steps = jax.random.uniform(jax.random.fold_in(jax.random.fold_in(key, 6), position), (blocks,), jnp.float32, least / len(cuts), largest / len(cuts))
        return jnp.repeat(jnp.exp(steps), extent[position] // blocks).reshape((-1,) + (1,) * (len(extent) - position - 1))

    gain = one(*cuts[0])
    for cut in cuts[1:]:
        gain = gain * one(*cut)
    return gain


def gaussian(own_key, dims, scale, limit, pieces=(), held_as=jnp.bfloat16):
    entries = jax.random.normal(own_key, dims, jnp.float32) * scale
    if len(pieces) > 0:
        entries = shard_levels(own_key, dims, pieces, -0.22, 0.18) * entries
    return jnp.clip(entries, min=-limit, max=limit).astype(held_as)


def setup_inputs(seed: int = 0) -> dict:
    splits = jax.random.split(jax.random.key(seed), 16)
    tokens = draw_tokens(jax.random.fold_in(splits[15], 71), 0)
    segments = draw_segments(jax.random.fold_in(splits[15], 71), 0)
    w_qkv = gaussian(splits[2], (D, 3, D), D ** -0.5, 0.1875, ((0, 8), (2, 4)))
    b_qv = gaussian(splits[3], (2, HEADS, HD), 0.1, 0.59765625, ((1, 4), (2, 8)))
    w_out = gaussian(splits[4], (D, D), (D // 16) ** -0.5, 0.75, ((0, 4), (1, 8)))
    b_out = gaussian(splits[5], (D,), 0.5, 3.0, ((0, 8),))
    w_up = gaussian(splits[6], (D, FF), D ** -0.5, 0.1875, ((0, 8), (1, 4)))
    b_up = gaussian(splits[7], (FF // HD, HD), 0.5, 3.0, ((0, 4), (1, 8)))
    w_down = gaussian(splits[8], (FF, D), FF ** -0.5, 0.09375, ((0, 4), (1, 8)))
    b_down = gaussian(splits[9], (D,), 0.5, 3.0, ((0, 8),))
    attngain = jnp.clip(1.0 + 0.1 * jax.random.normal(splits[10], (D,), jnp.float32), 0.5, 1.5).astype(jnp.bfloat16)
    attnshift = gaussian(splits[11], (D,), 0.5, 3.0, ((0, 8),))
    mlpgain = jnp.clip(1.0 + 0.1 * jax.random.normal(splits[12], (D,), jnp.float32), 0.5, 1.5).astype(jnp.bfloat16)
    mlpshift = gaussian(splits[13], (D,), 0.5, 3.0, ((0, 8),))
    cotangent = gaussian(splits[14], (SEQS, LEN, D), 1.0, 6.0, ((0, 4), (1, 2)))
    return {"tokens": tokens, "segments": segments, "w_qkv": w_qkv, "b_qv": b_qv, "w_out": w_out, "b_out": b_out, "w_up": w_up, "b_up": b_up, "w_down": w_down, "b_down": b_down, "attngain": attngain, "attnshift": attnshift, "mlpgain": mlpgain, "mlpshift": mlpshift, "cotangent": cotangent}


@jax.custom_vjp
def low(v):
    return lax.optimization_barrier(v.astype(jnp.bfloat16)).astype(jnp.float32)

@jax.custom_vjp
def low_back(v):
    return v

def low_keep(v):
    return (low(v), None)

def low_pass(kept, grad):
    return (grad,)

def back_keep(v):
    return (v, None)

def back_low(kept, grad):
    return (low(grad),)
low.defvjp(low_keep, low_pass)
low_back.defvjp(back_keep, back_low)
epsilon = 1e-05
negative = -1e+30

def normalize(matrix, factor, offset):
    average = lax.optimization_barrier(jnp.mean(matrix, axis=-1, keepdims=True))
    centered = matrix - average
    spread = lax.optimization_barrier(jnp.mean(centered * centered, axis=-1, keepdims=True))
    return centered * lax.rsqrt(spread + epsilon) * factor + offset

def gelu_tanh(inputs):
    cubed_vals = inputs * inputs * inputs
    return 0.5 * inputs * (1.0 + jnp.tanh(0.7978845608028654 * (inputs + 0.044715 * cubed_vals)))

def block_layer(inputs, seg_ids, w_qkv, b_qv, w_out, b_out, w_up, b_up, w_down, b_down, attngain, attnshift, mlpgain, mlpshift):
    highest = lax.Precision.HIGHEST
    normed_one = low(normalize(inputs, attngain, attnshift))
    projected = jnp.einsum('td,dje->tje', normed_one, w_qkv, precision=highest)
    qv_flat = b_qv.reshape(2, D)
    queries = low_back(low(projected[:, 0] + qv_flat[0]))
    key_rows = low_back(low(projected[:, 1]))
    value_rows = low_back(low(projected[:, 2] + qv_flat[1]))
    shape_heads = (LEN, HEADS, HD)
    raw_scores = jnp.einsum('qhd,khd->hqk', queries.reshape(shape_heads), key_rows.reshape(shape_heads), precision=highest)
    scores = low_back(raw_scores * (1.0 / HD ** 0.5))
    positions = jnp.arange(LEN)
    allowed = (seg_ids[:, None] == seg_ids[None, :]) & (positions[None, :] <= positions[:, None])
    scores = jnp.where(allowed[None], scores, negative)
    row_max = lax.optimization_barrier(jnp.max(scores, axis=-1, keepdims=True))
    exp_scores = jnp.exp(scores - row_max)
    soft_probs = low(exp_scores / lax.optimization_barrier(jnp.sum(exp_scores, axis=-1, keepdims=True)))
    attended = jnp.einsum('hqk,khd->qhd', soft_probs, value_rows.reshape(shape_heads), precision=highest)
    attended = low_back(low(attended.reshape(LEN, D)))
    branch_one = low_back(jnp.dot(attended, w_out, precision=highest) + b_out)
    middle = inputs + branch_one
    normed_two = low(normalize(middle, mlpgain, mlpshift))
    hidden_pre = low_back(jnp.dot(normed_two, w_up, precision=highest) + b_up.reshape(FF))
    activated = low(gelu_tanh(hidden_pre))
    branch_two = low_back(jnp.dot(activated, w_down, precision=highest) + b_down)
    return middle + branch_two

def reference(tokens, segments, w_qkv, b_qv, w_out, b_out, w_up, b_up, w_down, b_down, attngain, attnshift, mlpgain, mlpshift, cotangent):
    weights = tuple((array_in.astype(jnp.float32) for array_in in (w_qkv, b_qv, w_out, b_out, w_up, b_up, w_down, b_down, attngain, attnshift, mlpgain, mlpshift)))

    def one_sequence(running, slices):
        rows_in, seg_ids, rows_grad = slices

        def forward(inputs, p_qkv, p_qv, p_out, p_bout, p_up, p_bup, p_down, p_bdown, p_gone, p_sone, p_gtwo, p_stwo):
            return block_layer(inputs, seg_ids, p_qkv, p_qv, p_out, p_bout, p_up, p_bup, p_down, p_bdown, p_gone, p_sone, p_gtwo, p_stwo)
        result, pullback = jax.vjp(forward, rows_in.astype(jnp.float32), *weights)
        gradients = pullback(rows_grad.astype(jnp.float32))
        running = tuple((before + added for before, added in zip(running, gradients[1:])))
        return (running, (result.astype(jnp.bfloat16), gradients[0]))
    zero_sums = tuple((jnp.zeros(array_in.shape, jnp.float32) for array_in in weights))
    totals, (block_out, grad_tokens) = lax.scan(one_sequence, zero_sums, (tokens, segments, cotangent))
    return (block_out, grad_tokens, totals[0], totals[1], totals[2], totals[3], totals[4], totals[5], totals[6], totals[7], totals[8], totals[9], totals[10], totals[11])
```

```python
import jax
import jax.numpy as jnp
from jax import lax
from jax.sharding import PartitionSpec as P

HD = 64
LANES = 128
CORE = 1
CHIP = 2

epsilon = 1e-05
negative = -1e30


def swap(array, axis, mask=1):
    devices = lax.axis_size(axis)
    return lax.ppermute(array, axis, [(i, i ^ mask) for i in range(devices)])


def ordered(place, own, other):
    return jnp.where(place == 0, own, other), jnp.where(place == 0, other, own)


def gather_fsdp(block):
    devices = lax.axis_size("fsdp")
    return lax.all_to_all(
        jnp.broadcast_to(block[None], (devices,) + block.shape), "fsdp", 0, 0, tiled=True
    )


def gather_rows(block, ctx_place):
    own = gather_fsdp(block)
    other = swap(own, "ctx")
    first, second = ordered(ctx_place, own, other)
    return jnp.stack([first, second], axis=1).reshape(-1, block.shape[1])


def sum_tp(part_of, rows, core_place):
    half = rows // 2
    sent = swap(part_of((1 - core_place) * half, half).astype(jnp.bfloat16), "tp", CORE)
    kept = part_of(core_place * half, half)
    chip_sum = (kept + sent.astype(jnp.float32)).astype(jnp.bfloat16)
    across = swap(chip_sum, "tp", CHIP)
    total = (chip_sum.astype(jnp.float32) + across.astype(jnp.float32)).astype(jnp.bfloat16)
    return jnp.concatenate(ordered(core_place, total, swap(total, "tp", CORE)), axis=0)


def scatter_rows(wide, narrow, ctx_place):
    devices = lax.axis_size("fsdp")
    tokens, width = wide.shape
    rows = width // (devices * 2)
    split = wide.reshape(tokens, devices, 2, rows)
    first, second = split[:, :, 0], split[:, :, 1]

    def product(part):
        return jnp.einsum(
            "tzd,tn->zdn", part, narrow, preferred_element_type=jnp.float32
        )

    sent = swap(
        product(jnp.where(ctx_place == 0, second, first)).astype(jnp.bfloat16), "ctx"
    )
    kept = product(jnp.where(ctx_place == 0, first, second))
    pair_sum = (kept + sent.astype(jnp.float32)).astype(jnp.bfloat16)
    parts = lax.all_to_all(pair_sum, "fsdp", 0, 0, tiled=True)
    return jnp.sum(parts.astype(jnp.float32), axis=0)


def normalize(matrix, factor, offset):
    average = jnp.mean(matrix, axis=-1, keepdims=True)
    centered = matrix - average
    spread = jnp.mean(centered * centered, axis=-1, keepdims=True)
    return centered * lax.rsqrt(spread + epsilon) * factor + offset


def normalize_back(matrix, factor, grad):
    average = jnp.mean(matrix, axis=-1, keepdims=True)
    centered = matrix - average
    spread = jnp.mean(centered * centered, axis=-1, keepdims=True)
    inverse = lax.rsqrt(spread + epsilon)
    xhat = centered * inverse
    scaled = grad * factor
    mean_scaled = jnp.mean(scaled, axis=-1, keepdims=True)
    mean_product = jnp.mean(scaled * xhat, axis=-1, keepdims=True)
    grad_in = inverse * (scaled - mean_scaled - xhat * mean_product)
    return grad_in, jnp.sum(grad * xhat, axis=0), jnp.sum(grad, axis=0)


def gelu_tanh(inputs):
    cubed_vals = inputs * inputs * inputs
    return 0.5 * inputs * (1.0 + jnp.tanh(0.7978845608028654 * (inputs + 0.044715 * cubed_vals)))


def dot(left, right, left_dim, right_dim):
    return lax.dot_general(
        left, right, (((left_dim,), (right_dim,)), ((), ())), preferred_element_type=jnp.float32
    )


def local(
    tokens,
    segments,
    w_qkv,
    b_qv,
    w_out,
    b_out,
    w_up,
    b_up,
    w_down,
    b_down,
    attngain,
    attnshift,
    mlpgain,
    mlpshift,
    cotangent,
):
    fsdp = lax.axis_size("fsdp")
    owners = fsdp * 2
    ctx_place = lax.axis_index("ctx")
    core_place = lax.axis_index("tp") % 2
    block_len, width = tokens.shape[1:]
    length = segments.shape[1]
    local_width = w_qkv.shape[2]
    part_width = local_width // 2
    part_heads = part_width // HD
    heads_local = local_width // HD
    drow = w_qkv.shape[0]
    hrow = b_qv.shape[2]
    score_scale = 1.0 / HD**0.5

    by_kind = jnp.transpose(w_qkv, (1, 0, 2))
    weight_rows = 3 * drow * part_width // LANES
    own_weight = lax.dynamic_slice_in_dim(by_kind, ctx_place * part_width, part_width, 2)
    sent_weight = lax.dynamic_slice_in_dim(by_kind, (1 - ctx_place) * part_width, part_width, 2)
    small = jnp.concatenate(
        [
            b_out,
            b_down,
            attngain,
            attnshift,
            mlpgain,
            mlpshift,
            b_up.reshape(-1),
            b_qv.reshape(-1),
        ]
    )
    small_rows = 16 * (-(-small.shape[0] // (16 * LANES)))
    small_size = small.shape[0]
    small = jnp.pad(small, (0, small_rows * LANES - small_size)).reshape(small_rows, LANES)
    own_pack = jnp.concatenate([own_weight.reshape(weight_rows, LANES), small])
    other_pack = swap(
        jnp.concatenate([sent_weight.reshape(weight_rows, LANES), small]), "ctx"
    )
    packs = gather_fsdp(jnp.stack(ordered(ctx_place, own_pack, other_pack)))
    qkv_part = (
        packs[:, :, :weight_rows]
        .reshape(fsdp, 2, 3, drow, part_width)
        .transpose(0, 1, 3, 2, 4)
        .reshape(width, 3 * part_width)
    )
    smalls = packs[:, :, weight_rows:].reshape(owners, -1)[:, :small_size]
    vectors = smalls[:, : 6 * drow].reshape(owners, 6, drow).transpose(1, 0, 2).reshape(6, width)
    out_bias, down_bias, gain_one, shift_one, gain_two, shift_two = vectors.astype(jnp.float32)
    up_size = b_up.shape[0] * hrow
    up_bias = (
        smalls[:, 6 * drow : 6 * drow + up_size]
        .reshape(owners, b_up.shape[0], hrow)
        .transpose(1, 0, 2)
        .reshape(-1)
        .astype(jnp.float32)
    )
    qv_bias = (
        smalls[:, 6 * drow + up_size :]
        .reshape(owners, 2, heads_local, hrow)
        .transpose(1, 2, 0, 3)
        .reshape(2, local_width)
        .astype(jnp.float32)
    )
    qv_bias_part = lax.dynamic_slice_in_dim(qv_bias, ctx_place * part_width, part_width, 1)

    own_tokens = tokens[0]
    half = block_len // 2
    got = swap(lax.dynamic_slice_in_dim(own_tokens, core_place * half, half, 0), "ctx")
    other_tokens = jnp.concatenate(ordered(core_place, got, swap(got, "tp", CORE)))
    all_tokens = jnp.concatenate(ordered(ctx_place, own_tokens, other_tokens))

    out_full = gather_rows(w_out.T, ctx_place)
    up_full = gather_rows(w_up, ctx_place)
    down_full = gather_rows(w_down.T, ctx_place)

    normed_all = normalize(all_tokens.astype(jnp.float32), gain_one, shift_one).astype(jnp.bfloat16)
    projected = dot(normed_all, qkv_part, 1, 0)
    queries = (projected[:, :part_width] + qv_bias_part[0]).astype(jnp.bfloat16)
    key_rows = projected[:, part_width : 2 * part_width].astype(jnp.bfloat16)
    value_rows = (projected[:, 2 * part_width :] + qv_bias_part[1]).astype(jnp.bfloat16)
    query_heads = queries.reshape(length, part_heads, HD)
    key_heads = key_rows.reshape(length, part_heads, HD)
    value_heads = value_rows.reshape(length, part_heads, HD)
    places = jnp.arange(length, dtype=jnp.int32)
    allowed = (segments[0][:, None] == segments[0][None, :]) & (
        places[None, :] <= places[:, None]
    )
    scores = (
        jnp.einsum("qhd,khd->hqk", query_heads, key_heads, preferred_element_type=jnp.float32)
        * score_scale
    )
    scores = jnp.where(allowed[None], scores, negative)
    row_max = jnp.max(scores, axis=-1, keepdims=True)
    exp_scores = jnp.exp(scores - row_max)
    row_totals = jnp.sum(exp_scores, axis=-1, keepdims=True)
    soft_probs = exp_scores / row_totals
    probs_low = soft_probs.astype(jnp.bfloat16)
    attended_part = (
        jnp.einsum("hqk,khd->qhd", probs_low, value_heads, preferred_element_type=jnp.float32)
        .reshape(length, part_width)
        .astype(jnp.bfloat16)
    )

    def to_tokens(array):
        kept = lax.dynamic_slice_in_dim(array, ctx_place * block_len, block_len, 0)
        sent = swap(
            lax.dynamic_slice_in_dim(array, (1 - ctx_place) * block_len, block_len, 0), "ctx"
        )
        return ordered(ctx_place, kept, sent)

    attended = jnp.concatenate(to_tokens(attended_part), axis=1)
    inputs = own_tokens.astype(jnp.float32)

    def out_part(start, count):
        return dot(lax.dynamic_slice_in_dim(attended, start, count, 0), out_full, 1, 1)

    middle = inputs + (sum_tp(out_part, block_len, core_place).astype(jnp.float32) + out_bias)
    normed_two = normalize(middle, gain_two, shift_two).astype(jnp.bfloat16)
    hidden_pre = dot(normed_two, up_full, 1, 0) + up_bias
    activated = gelu_tanh(hidden_pre).astype(jnp.bfloat16)

    def down_part(start, count):
        return dot(lax.dynamic_slice_in_dim(activated, start, count, 0), down_full, 1, 1)

    finished = middle + (
        sum_tp(down_part, block_len, core_place).astype(jnp.float32) + down_bias
    )

    grad_out_low = cotangent[0]
    grad_out = grad_out_low.astype(jnp.float32)
    grad_down_bias = jnp.sum(grad_out, axis=0)
    grad_activated = dot(grad_out_low, down_full, 1, 0)
    unused, gelu_pull = jax.vjp(gelu_tanh, hidden_pre)
    grad_hidden_low = gelu_pull(grad_activated)[0].astype(jnp.bfloat16)
    grad_up_bias = jnp.sum(grad_hidden_low.astype(jnp.float32), axis=0)

    def up_part(start, count):
        return dot(lax.dynamic_slice_in_dim(grad_hidden_low, start, count, 0), up_full, 1, 1)

    grad_normed_two = sum_tp(up_part, block_len, core_place).astype(jnp.float32)
    grad_down = scatter_rows(grad_out_low, activated, ctx_place).T
    grad_up = scatter_rows(normed_two, grad_hidden_low, ctx_place)
    grad_middle_norm, grad_gain_two, grad_shift_two = normalize_back(
        middle, gain_two, grad_normed_two
    )
    grad_middle = grad_out + grad_middle_norm
    grad_branch_low = grad_middle.astype(jnp.bfloat16)
    grad_out_bias = jnp.sum(grad_branch_low.astype(jnp.float32), axis=0)
    grad_attended_low = dot(grad_branch_low, out_full, 1, 0).astype(jnp.bfloat16)
    grad_out_weight = scatter_rows(grad_branch_low, attended, ctx_place).T

    own_cols = lax.dynamic_slice_in_dim(grad_attended_low, ctx_place * part_width, part_width, 1)
    sent_cols = swap(
        lax.dynamic_slice_in_dim(grad_attended_low, (1 - ctx_place) * part_width, part_width, 1),
        "ctx",
    )
    grad_heads = jnp.concatenate(ordered(ctx_place, own_cols, sent_cols)).reshape(
        length, part_heads, HD
    )
    grad_values = jnp.einsum(
        "hqk,qhd->khd", probs_low, grad_heads, preferred_element_type=jnp.float32
    )
    grad_probs = jnp.einsum(
        "qhd,khd->hqk", grad_heads, value_heads, preferred_element_type=jnp.float32
    )
    row_inner = jnp.sum(soft_probs * grad_probs, axis=-1, keepdims=True)
    grad_scores = (soft_probs * (grad_probs - row_inner)).astype(jnp.bfloat16)
    grad_queries = (
        jnp.einsum("hqk,khd->qhd", grad_scores, key_heads, preferred_element_type=jnp.float32)
        * score_scale
    )
    grad_keys = (
        jnp.einsum("hqk,qhd->khd", grad_scores, query_heads, preferred_element_type=jnp.float32)
        * score_scale
    )
    grad_qkv_part = jnp.concatenate(
        [
            grad.reshape(length, part_width).astype(jnp.bfloat16)
            for grad in (grad_queries, grad_keys, grad_values)
        ],
        axis=1,
    )
    grad_qkv_weight = dot(normed_all, grad_qkv_part, 0, 0).astype(jnp.bfloat16)
    grad_qkv_sum = jnp.sum(
        lax.all_to_all(
            grad_qkv_weight.reshape(fsdp, 2 * drow, 3 * part_width), "fsdp", 0, 0, tiled=True
        ).astype(jnp.float32),
        axis=0,
    )
    own_rows = lax.dynamic_slice_in_dim(grad_qkv_sum, ctx_place * drow, drow, 0)
    sent_rows = swap(
        lax.dynamic_slice_in_dim(grad_qkv_sum, (1 - ctx_place) * drow, drow, 0).astype(
            jnp.bfloat16
        ),
        "ctx",
    ).astype(jnp.float32)
    grad_qkv_out = jnp.concatenate(
        [
            part.reshape(drow, 3, part_width)
            for part in ordered(ctx_place, own_rows, sent_rows)
        ],
        axis=2,
    )
    bias_sums = jnp.sum(grad_qkv_part.astype(jnp.float32), axis=0).reshape(3, part_width)
    bias_sums = jnp.stack([bias_sums[0], bias_sums[2]])
    nothing = jnp.zeros_like(bias_sums)
    grad_qv_bias = jnp.concatenate(ordered(ctx_place, bias_sums, nothing), axis=1)

    qkv_other = swap(qkv_part, "ctx")
    qkv_first, qkv_second = ordered(ctx_place, qkv_part, qkv_other)
    grad_qkv_first, grad_qkv_second = to_tokens(grad_qkv_part)

    def first_part(start, count):
        return dot(
            lax.dynamic_slice_in_dim(grad_qkv_first, start, count, 0), qkv_first, 1, 1
        ) + dot(lax.dynamic_slice_in_dim(grad_qkv_second, start, count, 0), qkv_second, 1, 1)

    grad_normed_one = sum_tp(first_part, block_len, core_place).astype(jnp.float32)
    grad_inputs_norm, grad_gain_one, grad_shift_one = normalize_back(
        inputs, gain_one, grad_normed_one
    )
    grad_inputs = grad_middle + grad_inputs_norm

    small_grads = jnp.concatenate(
        [
            vector.reshape(owners, drow)
            for vector in (
                grad_out_bias,
                grad_down_bias,
                grad_gain_one,
                grad_shift_one,
                grad_gain_two,
                grad_shift_two,
            )
        ]
        + [
            grad_up_bias.reshape(-1, owners, hrow).transpose(1, 0, 2).reshape(owners, -1),
            grad_qv_bias.reshape(2, heads_local, owners, hrow)
            .transpose(2, 0, 1, 3)
            .reshape(owners, -1),
        ],
        axis=1,
    )
    small_sums = jnp.sum(
        lax.all_to_all(small_grads, ("fsdp", "ctx"), 0, 0, tiled=True), axis=0
    )
    vector_sums = small_sums[: 6 * drow].reshape(6, drow)
    up_bias_sum = small_sums[6 * drow : 6 * drow + up_size].reshape(-1, hrow)
    qv_bias_sum = small_sums[6 * drow + up_size :].reshape(2, heads_local, hrow)

    return (
        finished.astype(jnp.bfloat16)[None],
        grad_inputs[None],
        grad_qkv_out,
        qv_bias_sum,
        grad_out_weight,
        vector_sums[0],
        grad_up,
        up_bias_sum,
        grad_down,
        vector_sums[1],
        vector_sums[2],
        vector_sums[3],
        vector_sums[4],
        vector_sums[5],
    )


def solution(mesh):
    placed = (
        P("fsdp", "ctx", None),
        P("fsdp", None),
        P(("fsdp", "ctx"), None, "tp"),
        P(None, "tp", ("fsdp", "ctx")),
        P("tp", ("fsdp", "ctx")),
        P(("fsdp", "ctx")),
        P(("fsdp", "ctx"), "tp"),
        P("tp", ("fsdp", "ctx")),
        P("tp", ("fsdp", "ctx")),
        P(("fsdp", "ctx")),
        P(("fsdp", "ctx")),
        P(("fsdp", "ctx")),
        P(("fsdp", "ctx")),
        P(("fsdp", "ctx")),
        P("fsdp", "ctx", None),
    )
    return jax.shard_map(
        local,
        mesh=mesh,
        in_specs=placed,
        out_specs=(
            P("fsdp", "ctx", None),
            P("fsdp", "ctx", None),
            P(("fsdp", "ctx"), None, "tp"),
            P(None, "tp", ("fsdp", "ctx")),
            P("tp", ("fsdp", "ctx")),
            P(("fsdp", "ctx")),
            P(("fsdp", "ctx"), "tp"),
            P("tp", ("fsdp", "ctx")),
            P("tp", ("fsdp", "ctx")),
            P(("fsdp", "ctx")),
            P(("fsdp", "ctx")),
            P(("fsdp", "ctx")),
            P(("fsdp", "ctx")),
            P(("fsdp", "ctx")),
        ),
        check_vma=False,
    )
```

```python
import functools

import jax
import jax.numpy as jnp
from jax import lax
from jax.experimental import pallas as pl
from jax.experimental.pallas import tpu as pltpu
from jax.sharding import PartitionSpec as P

HD = 64
LANES = 128
CORE = 1
CHIP = 2
VMEM_LIMIT = 40 * 1024 * 1024

epsilon = 1e-05
negative = -1e30


def swap(array, axis, mask=1):
    devices = lax.axis_size(axis)
    return lax.ppermute(array, axis, [(i, i ^ mask) for i in range(devices)])


def ordered(place, own, other):
    return jnp.where(place == 0, own, other), jnp.where(place == 0, other, own)


def gather_fsdp(block):
    devices = lax.axis_size("fsdp")
    return lax.all_to_all(
        jnp.broadcast_to(block[None], (devices,) + block.shape), "fsdp", 0, 0, tiled=True
    )


def gather_rows(block, ctx_place):
    own = gather_fsdp(block)
    other = swap(own, "ctx")
    first, second = ordered(ctx_place, own, other)
    return jnp.stack([first, second], axis=1).reshape(-1, block.shape[1])


def sum_tp(part_of, rows, core_place, gated=()):
    half = rows // 2
    sent = swap(part_of((1 - core_place) * half, half).astype(jnp.bfloat16), "tp", CORE)
    kept = part_of(core_place * half, half)
    chip_sum = (kept + sent.astype(jnp.float32)).astype(jnp.bfloat16)
    chip_sum, gated = lax.optimization_barrier((chip_sum, gated))
    across = swap(chip_sum, "tp", CHIP)
    total = (chip_sum.astype(jnp.float32) + across.astype(jnp.float32)).astype(jnp.bfloat16)
    summed = jnp.concatenate(ordered(core_place, total, swap(total, "tp", CORE)), axis=0)
    return summed, gated


def scatter_rows(wide, narrow, ctx_place):
    devices = lax.axis_size("fsdp")
    width = wide.shape[1]
    rows = width // (devices * 2)
    product = dot(wide, narrow, 0, 0).astype(jnp.bfloat16).reshape(devices, 2, rows, -1)
    kept, sent = ordered(ctx_place, product[:, 0], product[:, 1])
    pair_sum = kept.astype(jnp.float32) + swap(sent, "ctx").astype(jnp.float32)
    return lax.psum_scatter(
        pair_sum.astype(jnp.bfloat16).reshape(devices * rows, -1),
        "fsdp",
        scatter_dimension=0,
        tiled=True,
    ).astype(jnp.float32)


def normalize(matrix, factor, offset):
    average = jnp.mean(matrix, axis=-1, keepdims=True)
    centered = matrix - average
    spread = jnp.mean(centered * centered, axis=-1, keepdims=True)
    return centered * lax.rsqrt(spread + epsilon) * factor + offset


def normalize_back(matrix, factor, grad):
    average = jnp.mean(matrix, axis=-1, keepdims=True)
    centered = matrix - average
    spread = jnp.mean(centered * centered, axis=-1, keepdims=True)
    inverse = lax.rsqrt(spread + epsilon)
    xhat = centered * inverse
    scaled = grad * factor
    mean_scaled = jnp.mean(scaled, axis=-1, keepdims=True)
    mean_product = jnp.mean(scaled * xhat, axis=-1, keepdims=True)
    grad_in = inverse * (scaled - mean_scaled - xhat * mean_product)
    return grad_in, jnp.sum(grad * xhat, axis=0), jnp.sum(grad, axis=0)


def gelu_tanh(inputs):
    cubed_vals = inputs * inputs * inputs
    return 0.5 * inputs * (1.0 + jnp.tanh(0.7978845608028654 * (inputs + 0.044715 * cubed_vals)))


def dot(left, right, left_dim, right_dim):
    return lax.dot_general(
        left, right, (((left_dim,), (right_dim,)), ((), ())), preferred_element_type=jnp.float32
    )


def head_masks(shape):
    lane = lax.broadcasted_iota(jnp.int32, shape, 1)
    return [(lane // HD) == head for head in range(shape[1] // HD)]


def attend_kernel(
    rows, drow, scale,
    tokens_ref, packs_ref, vectors_ref, bias_ref, seg_row_ref, seg_col_ref,
    normed_ref, qkv_ref, attended_ref, weight_ref,
):
    length = tokens_ref.shape[0]
    part = attended_ref.shape[1]
    for owner in range(packs_ref.shape[0]):
        for kind in range(3):
            weight_ref[owner * drow : (owner + 1) * drow, kind * part : (kind + 1) * part] = (
                packs_ref[owner, kind * drow : (kind + 1) * drow, :]
            )
    masks = head_masks((rows, part))
    for block in range(length // rows):
        here = slice(block * rows, (block + 1) * rows)
        seen = (block + 1) * rows
        inputs = tokens_ref[here, :].astype(jnp.float32)
        centered = inputs - jnp.mean(inputs, axis=-1, keepdims=True)
        spread = jnp.mean(centered * centered, axis=-1, keepdims=True)
        normed = (
            centered * lax.rsqrt(spread + epsilon) * vectors_ref[0:1, :] + vectors_ref[1:2, :]
        ).astype(jnp.bfloat16)
        normed_ref[here, :] = normed
        projected = dot(normed, weight_ref[...], 1, 0) + bias_ref[...]
        qkv_ref[here, :] = projected.astype(jnp.bfloat16)
        queries = qkv_ref[here, :part]
        key_rows = qkv_ref[:seen, part : 2 * part]
        value_rows = qkv_ref[:seen, 2 * part :]
        query_index = block * rows + lax.broadcasted_iota(jnp.int32, (rows, seen), 0)
        key_index = lax.broadcasted_iota(jnp.int32, (rows, seen), 1)
        allowed = (seg_col_ref[here, :] == seg_row_ref[:, :seen]) & (key_index <= query_index)
        result = jnp.zeros((rows, part), jnp.float32)
        for mask in masks:
            scores = dot(jnp.where(mask, queries, 0), key_rows, 1, 1) * scale
            scores = jnp.where(allowed, scores, negative)
            weights = jnp.exp(scores - jnp.max(scores, axis=-1, keepdims=True))
            probs = weights * (1.0 / jnp.sum(weights, axis=-1, keepdims=True))
            result = jnp.where(mask, dot(probs.astype(jnp.bfloat16), value_rows, 1, 0), result)
        attended_ref[here, :] = result.astype(jnp.bfloat16)


def attend_back_kernel(
    rows, scale,
    qkv_ref, grad_ref, seg_row_ref, seg_col_ref,
    out_ref, sums_ref,
    key_sum, value_sum,
):
    length, part = grad_ref.shape
    masks = head_masks((rows, part))
    key_sum[...] = jnp.zeros_like(key_sum)
    value_sum[...] = jnp.zeros_like(value_sum)
    query_total = jnp.zeros((1, part), jnp.float32)
    for block in range(length // rows):
        here = slice(block * rows, (block + 1) * rows)
        seen = (block + 1) * rows
        queries = qkv_ref[here, :part]
        grads = grad_ref[here, :]
        key_rows = qkv_ref[:seen, part : 2 * part]
        value_rows = qkv_ref[:seen, 2 * part :]
        query_index = block * rows + lax.broadcasted_iota(jnp.int32, (seen, rows), 1)
        key_index = lax.broadcasted_iota(jnp.int32, (seen, rows), 0)
        allowed = (seg_col_ref[:seen, :] == seg_row_ref[:, here]) & (key_index <= query_index)
        grad_query = jnp.zeros((rows, part), jnp.float32)
        for mask in masks:
            head_queries = jnp.where(mask, queries, 0)
            head_grads = jnp.where(mask, grads, 0)
            scores = dot(key_rows, head_queries, 1, 1) * scale
            scores = jnp.where(allowed, scores, negative)
            weights = jnp.exp(scores - jnp.max(scores, axis=0, keepdims=True))
            probs = weights * (1.0 / jnp.sum(weights, axis=0, keepdims=True))
            value_sum[:seen, :] += dot(probs.astype(jnp.bfloat16), head_grads, 1, 0)
            grad_probs = dot(value_rows, head_grads, 1, 1)
            inner = jnp.sum(probs * grad_probs, axis=0, keepdims=True)
            grad_scores = (probs * (grad_probs - inner)).astype(jnp.bfloat16)
            key_sum[:seen, :] += dot(grad_scores, head_queries, 1, 0)
            grad_query = jnp.where(mask, dot(grad_scores, key_rows, 0, 0), grad_query)
        grad_query = (grad_query * scale).astype(jnp.bfloat16)
        out_ref[here, :part] = grad_query
        query_total += jnp.sum(grad_query.astype(jnp.float32), axis=0, keepdims=True)
    grad_values = value_sum[...].astype(jnp.bfloat16)
    out_ref[:, part : 2 * part] = (key_sum[...] * scale).astype(jnp.bfloat16)
    out_ref[:, 2 * part :] = grad_values
    sums_ref[0:1, :] = query_total
    sums_ref[1:2, :] = jnp.sum(grad_values.astype(jnp.float32), axis=0, keepdims=True)


def local(
    tokens,
    segments,
    w_qkv,
    b_qv,
    w_out,
    b_out,
    w_up,
    b_up,
    w_down,
    b_down,
    attngain,
    attnshift,
    mlpgain,
    mlpshift,
    cotangent,
):
    fsdp = lax.axis_size("fsdp")
    owners = fsdp * 2
    ctx_place = lax.axis_index("ctx")
    core_place = lax.axis_index("tp") % 2
    block_len, width = tokens.shape[1:]
    length = segments.shape[1]
    local_width = w_qkv.shape[2]
    part_width = local_width // 2
    part_heads = part_width // HD
    heads_local = local_width // HD
    drow = w_qkv.shape[0]
    hrow = b_qv.shape[2]
    score_scale = 1.0 / HD**0.5

    by_kind = jnp.transpose(w_qkv, (1, 0, 2))
    weight_rows = 3 * drow * part_width // LANES
    own_weight = lax.dynamic_slice_in_dim(by_kind, ctx_place * part_width, part_width, 2)
    sent_weight = lax.dynamic_slice_in_dim(by_kind, (1 - ctx_place) * part_width, part_width, 2)
    small_rows = 32
    up_rows = b_up.shape[0]
    qv_rows = b_qv.shape[0] * b_qv.shape[1]

    def padded(array, first):
        array = array.reshape(-1, array.shape[-1])
        rows, lanes = array.shape
        return jnp.pad(array, ((first, small_rows - first - rows), (0, LANES - lanes)))

    small = padded(b_up, 16) + padded(b_qv, 8)
    for place, vector in enumerate((attngain, attnshift, mlpgain, mlpshift, b_out, b_down)):
        small = small + padded(vector, place)
    own_pack = jnp.concatenate([own_weight.reshape(weight_rows, LANES), small])
    other_pack = swap(
        jnp.concatenate([sent_weight.reshape(weight_rows, LANES), small]), "ctx"
    )
    both_packs = jnp.stack(ordered(ctx_place, own_pack, other_pack))
    both_packs, w_out, w_up, w_down = lax.optimization_barrier((both_packs, w_out, w_up, w_down))
    packs = gather_fsdp(both_packs).reshape(owners, weight_rows + small_rows, LANES)
    smalls = packs[:, weight_rows:].astype(jnp.float32)
    vectors = smalls[:, :8, :drow].transpose(1, 0, 2).reshape(8, width)
    gain_one, shift_one, gain_two, shift_two, out_bias, down_bias = (vectors[i] for i in range(6))
    up_bias = smalls[:, 16 : 16 + up_rows, :hrow].transpose(1, 0, 2).reshape(-1)
    qv_bias = (
        smalls[:, 8 : 8 + qv_rows, :hrow].transpose(1, 0, 2).reshape(2, local_width)
    )
    qv_bias_part = lax.dynamic_slice_in_dim(qv_bias, ctx_place * part_width, part_width, 1)
    qkv_bias = jnp.concatenate(
        [qv_bias_part[0], jnp.zeros((part_width,), jnp.float32), qv_bias_part[1]]
    )[None]

    own_tokens = tokens[0]
    half = block_len // 2
    got = swap(lax.dynamic_slice_in_dim(own_tokens, core_place * half, half, 0), "ctx")
    other_tokens = jnp.concatenate(ordered(core_place, got, swap(got, "tp", CORE)))
    all_tokens = jnp.concatenate(ordered(ctx_place, own_tokens, other_tokens))

    out_full = gather_rows(w_out.T, ctx_place)
    up_full = gather_rows(w_up, ctx_place)
    down_full = gather_rows(w_down.T, ctx_place)

    seg_row = segments
    seg_col = segments.reshape(length, 1)
    rows = min(256, length)
    normed_all, qkv_rows, attended_part, qkv_part = pl.pallas_call(
        functools.partial(attend_kernel, rows, drow, score_scale),
        out_shape=(
            jax.ShapeDtypeStruct((length, width), jnp.bfloat16),
            jax.ShapeDtypeStruct((length, 3 * part_width), jnp.bfloat16),
            jax.ShapeDtypeStruct((length, part_width), jnp.bfloat16),
            jax.ShapeDtypeStruct((width, 3 * part_width), jnp.bfloat16),
        ),
        compiler_params=pltpu.CompilerParams(vmem_limit_bytes=VMEM_LIMIT),
        cost_estimate=pl.CostEstimate(
            flops=2 * length * width * 3 * part_width, bytes_accessed=8 * length * width,
            transcendentals=length * length,
        ),
    )(all_tokens, packs, vectors, qkv_bias, seg_row, seg_col)

    def to_tokens(array):
        kept = lax.dynamic_slice_in_dim(array, ctx_place * block_len, block_len, 0)
        sent = swap(
            lax.dynamic_slice_in_dim(array, (1 - ctx_place) * block_len, block_len, 0), "ctx"
        )
        return ordered(ctx_place, kept, sent)

    attended = jnp.concatenate(to_tokens(attended_part), axis=1)
    inputs = own_tokens.astype(jnp.float32)

    def out_part(start, count):
        return dot(lax.dynamic_slice_in_dim(attended, start, count, 0), out_full, 1, 1)

    attn_sum, unused = sum_tp(out_part, block_len, core_place)
    middle = inputs + (attn_sum.astype(jnp.float32) + out_bias)
    normed_two = normalize(middle, gain_two, shift_two).astype(jnp.bfloat16)
    hidden_pre = dot(normed_two, up_full, 1, 0) + up_bias
    activated = gelu_tanh(hidden_pre).astype(jnp.bfloat16)

    grad_out_low = cotangent[0]
    grad_out = grad_out_low.astype(jnp.float32)
    grad_down_bias = jnp.sum(grad_out, axis=0)
    grad_activated = dot(grad_out_low, down_full, 1, 0)
    value, gelu_pull = jax.vjp(gelu_tanh, hidden_pre)
    grad_hidden_low = gelu_pull(grad_activated)[0].astype(jnp.bfloat16)

    def up_part(start, count):
        return dot(lax.dynamic_slice_in_dim(grad_hidden_low, start, count, 0), up_full, 1, 1)

    up_sum, (activated, normed_two, grad_hidden_low) = sum_tp(
        up_part, block_len, core_place, (activated, normed_two, grad_hidden_low)
    )
    grad_up_bias = jnp.sum(grad_hidden_low.astype(jnp.float32), axis=0)
    grad_down = scatter_rows(grad_out_low, activated, ctx_place).T
    grad_up = scatter_rows(normed_two, grad_hidden_low, ctx_place)
    up_sum, activated = lax.optimization_barrier((up_sum, activated))
    grad_normed_two = up_sum.astype(jnp.float32)

    def down_part(start, count):
        return dot(lax.dynamic_slice_in_dim(activated, start, count, 0), down_full, 1, 1)

    mlp_sum, unused = sum_tp(down_part, block_len, core_place)
    finished = middle + (mlp_sum.astype(jnp.float32) + down_bias)
    grad_middle_norm, grad_gain_two, grad_shift_two = normalize_back(
        middle, gain_two, grad_normed_two
    )
    grad_middle = grad_out + grad_middle_norm
    grad_branch_low = grad_middle.astype(jnp.bfloat16)
    grad_out_bias = jnp.sum(grad_branch_low.astype(jnp.float32), axis=0)
    grad_attended_low = dot(grad_branch_low, out_full, 1, 0).astype(jnp.bfloat16)
    grad_out_weight = scatter_rows(grad_branch_low, attended, ctx_place).T

    own_cols = lax.dynamic_slice_in_dim(grad_attended_low, ctx_place * part_width, part_width, 1)
    sent_cols = swap(
        lax.dynamic_slice_in_dim(grad_attended_low, (1 - ctx_place) * part_width, part_width, 1),
        "ctx",
    )
    grad_heads = jnp.concatenate(ordered(ctx_place, own_cols, sent_cols))
    grad_qkv_part, bias_sums = pl.pallas_call(
        functools.partial(attend_back_kernel, rows, score_scale),
        out_shape=(
            jax.ShapeDtypeStruct((length, 3 * part_width), jnp.bfloat16),
            jax.ShapeDtypeStruct((2, part_width), jnp.float32),
        ),
        scratch_shapes=[
            pltpu.VMEM((length, part_width), jnp.float32),
            pltpu.VMEM((length, part_width), jnp.float32),
        ],
        compiler_params=pltpu.CompilerParams(vmem_limit_bytes=VMEM_LIMIT),
        cost_estimate=pl.CostEstimate(
            flops=10 * length * length * part_width, bytes_accessed=2 * length * width,
            transcendentals=length * length,
        ),
    )(qkv_rows, grad_heads, seg_row, seg_col)
    grad_qkv_weight = dot(normed_all, grad_qkv_part, 0, 0).astype(jnp.bfloat16)
    grad_qkv_sum = jnp.sum(
        lax.all_to_all(
            grad_qkv_weight.reshape(fsdp, 2 * drow, 3 * part_width), "fsdp", 0, 0, tiled=True
        ).astype(jnp.float32),
        axis=0,
    )
    own_rows = lax.dynamic_slice_in_dim(grad_qkv_sum, ctx_place * drow, drow, 0)
    sent_rows = swap(
        lax.dynamic_slice_in_dim(grad_qkv_sum, (1 - ctx_place) * drow, drow, 0).astype(
            jnp.bfloat16
        ),
        "ctx",
    ).astype(jnp.float32)
    grad_qkv_out = jnp.concatenate(
        [
            part.reshape(drow, 3, part_width)
            for part in ordered(ctx_place, own_rows, sent_rows)
        ],
        axis=2,
    )
    nothing = jnp.zeros_like(bias_sums)
    grad_qv_bias = jnp.concatenate(ordered(ctx_place, bias_sums, nothing), axis=1)

    qkv_other = swap(qkv_part, "ctx")
    qkv_first, qkv_second = ordered(ctx_place, qkv_part, qkv_other)
    grad_qkv_first, grad_qkv_second = to_tokens(grad_qkv_part)

    def first_part(start, count):
        return dot(
            lax.dynamic_slice_in_dim(grad_qkv_first, start, count, 0), qkv_first, 1, 1
        ) + dot(lax.dynamic_slice_in_dim(grad_qkv_second, start, count, 0), qkv_second, 1, 1)

    first_sum, unused = sum_tp(first_part, block_len, core_place)
    grad_normed_one = first_sum.astype(jnp.float32)
    grad_inputs_norm, grad_gain_one, grad_shift_one = normalize_back(
        inputs, gain_one, grad_normed_one
    )
    grad_inputs = grad_middle + grad_inputs_norm

    small_grads = jnp.concatenate(
        [
            vector.reshape(owners, drow)
            for vector in (
                grad_out_bias,
                grad_down_bias,
                grad_gain_one,
                grad_shift_one,
                grad_gain_two,
                grad_shift_two,
            )
        ]
        + [
            grad_up_bias.reshape(-1, owners, hrow).transpose(1, 0, 2).reshape(owners, -1),
            grad_qv_bias.reshape(2, heads_local, owners, hrow)
            .transpose(2, 0, 1, 3)
            .reshape(owners, -1),
        ],
        axis=1,
    )
    small_sums = jnp.sum(
        lax.all_to_all(small_grads, ("fsdp", "ctx"), 0, 0, tiled=True), axis=0
    )
    vector_sums = small_sums[: 6 * drow].reshape(6, drow)
    up_bias_sum = small_sums[6 * drow : 6 * drow + up_rows * hrow].reshape(-1, hrow)
    qv_bias_sum = small_sums[6 * drow + up_rows * hrow :].reshape(2, heads_local, hrow)

    return (
        finished.astype(jnp.bfloat16)[None],
        grad_inputs[None],
        grad_qkv_out,
        qv_bias_sum,
        grad_out_weight,
        vector_sums[0],
        grad_up,
        up_bias_sum,
        grad_down,
        vector_sums[1],
        vector_sums[2],
        vector_sums[3],
        vector_sums[4],
        vector_sums[5],
    )


def solution(mesh):
    placed = (
        P("fsdp", "ctx", None),
        P("fsdp", None),
        P(("fsdp", "ctx"), None, "tp"),
        P(None, "tp", ("fsdp", "ctx")),
        P("tp", ("fsdp", "ctx")),
        P(("fsdp", "ctx")),
        P(("fsdp", "ctx"), "tp"),
        P("tp", ("fsdp", "ctx")),
        P("tp", ("fsdp", "ctx")),
        P(("fsdp", "ctx")),
        P(("fsdp", "ctx")),
        P(("fsdp", "ctx")),
        P(("fsdp", "ctx")),
        P(("fsdp", "ctx")),
        P("fsdp", "ctx", None),
    )
    return jax.shard_map(
        local,
        mesh=mesh,
        in_specs=placed,
        out_specs=(
            P("fsdp", "ctx", None),
            P("fsdp", "ctx", None),
            P(("fsdp", "ctx"), None, "tp"),
            P(None, "tp", ("fsdp", "ctx")),
            P("tp", ("fsdp", "ctx")),
            P(("fsdp", "ctx")),
            P(("fsdp", "ctx"), "tp"),
            P("tp", ("fsdp", "ctx")),
            P("tp", ("fsdp", "ctx")),
            P(("fsdp", "ctx")),
            P(("fsdp", "ctx")),
            P(("fsdp", "ctx")),
            P(("fsdp", "ctx")),
            P(("fsdp", "ctx")),
        ),
        check_vma=False,
    )
```

```python
import functools

import jax
import jax.numpy as jnp
from jax import lax
from jax.experimental import pallas as pl
from jax.experimental.pallas import tpu as pltpu
from jax.sharding import PartitionSpec as P

HD = 64
LANES = 128
CORE = 1
CHIP = 2
VMEM_LIMIT = 16 * 1024 * 1024

epsilon = 1e-05
negative = -1e30


def swap(array, axis, mask=1):
    devices = lax.axis_size(axis)
    return lax.ppermute(array, axis, [(i, i ^ mask) for i in range(devices)])


def ordered(place, own, other):
    return jnp.where(place == 0, own, other), jnp.where(place == 0, other, own)


def gather_fsdp(block):
    devices = lax.axis_size("fsdp")
    return lax.all_to_all(
        jnp.broadcast_to(block[None], (devices,) + block.shape), "fsdp", 0, 0, tiled=True
    )


def gather_rows(block):
    return lax.all_gather(block, "fsdp", axis=0, tiled=True)


def pair_rows(own, rows, ctx_place):
    own = own.reshape(-1, rows, own.shape[1])
    first, second = ordered(ctx_place, own, swap(own, "ctx"))
    return jnp.stack([first, second], axis=1).reshape(-1, own.shape[2])


def sum_tp(part_of, rows, core_place, work=None, gated=()):
    half = rows // 2
    sent = swap(part_of((1 - core_place) * half, half).astype(jnp.bfloat16), "tp", CORE)
    kept = part_of(core_place * half, half)
    chip_sum = (kept + sent.astype(jnp.float32)).astype(jnp.bfloat16)
    chip_sum, gated = lax.optimization_barrier((chip_sum, gated))
    across = swap(chip_sum, "tp", CHIP)
    done = work(gated, chip_sum) if work else ()
    across, done = lax.optimization_barrier((across, done))
    total = (chip_sum.astype(jnp.float32) + across.astype(jnp.float32)).astype(jnp.bfloat16)
    summed = jnp.concatenate(ordered(core_place, total, swap(total, "tp", CORE)), axis=0)
    return summed, done


def weight_product(wide, narrow, ctx_place):
    devices = lax.axis_size("fsdp")
    rows = wide.shape[1] // (devices * 2)
    product = dot(wide, narrow, 0, 0).astype(jnp.bfloat16).reshape(devices, 2, rows, -1)
    return tuple(
        part.reshape(devices * rows, -1)
        for part in ordered(ctx_place, product[:, 0], product[:, 1])
    )


def pair_sum(kept, sent):
    return (kept.astype(jnp.float32) + sent.astype(jnp.float32)).astype(jnp.bfloat16)


def scatter_rows(array):
    return lax.psum_scatter(array, "fsdp", scatter_dimension=0, tiled=True)


def normalize(matrix, factor, offset):
    average = jnp.mean(matrix, axis=-1, keepdims=True)
    centered = matrix - average
    spread = jnp.mean(centered * centered, axis=-1, keepdims=True)
    return centered * lax.rsqrt(spread + epsilon) * factor + offset


def normalize_back(matrix, factor, grad):
    average = jnp.mean(matrix, axis=-1, keepdims=True)
    centered = matrix - average
    spread = jnp.mean(centered * centered, axis=-1, keepdims=True)
    inverse = lax.rsqrt(spread + epsilon)
    xhat = centered * inverse
    scaled = grad * factor
    mean_scaled = jnp.mean(scaled, axis=-1, keepdims=True)
    mean_product = jnp.mean(scaled * xhat, axis=-1, keepdims=True)
    grad_in = inverse * (scaled - mean_scaled - xhat * mean_product)
    return grad_in, jnp.sum(grad * xhat, axis=0), jnp.sum(grad, axis=0)


def gelu_tanh(inputs):
    cubed_vals = inputs * inputs * inputs
    return 0.5 * inputs * (1.0 + jnp.tanh(0.7978845608028654 * (inputs + 0.044715 * cubed_vals)))


def dot(left, right, left_dim, right_dim):
    return lax.dot_general(
        left, right, (((left_dim,), (right_dim,)), ((), ())), preferred_element_type=jnp.float32
    )


def head_masks(shape):
    lane = lax.broadcasted_iota(jnp.int32, shape, 1)
    return [(lane // HD) == head for head in range(shape[1] // HD)]


def attend_kernel(
    rows, drow, scale,
    tokens_ref, packs_ref, vectors_ref, bias_ref, seg_row_ref, seg_col_ref,
    normed_ref, qkv_ref, attended_ref, weight_ref,
):
    length = tokens_ref.shape[0]
    part = attended_ref.shape[1]
    for owner in range(packs_ref.shape[0]):
        for kind in range(3):
            weight_ref[owner * drow : (owner + 1) * drow, kind * part : (kind + 1) * part] = (
                packs_ref[owner, kind * drow : (kind + 1) * drow, :]
            )
    masks = head_masks((rows, part))
    for block in range(length // rows):
        here = slice(block * rows, (block + 1) * rows)
        seen = (block + 1) * rows
        inputs = tokens_ref[here, :].astype(jnp.float32)
        centered = inputs - jnp.mean(inputs, axis=-1, keepdims=True)
        spread = jnp.mean(centered * centered, axis=-1, keepdims=True)
        normed = (
            centered * lax.rsqrt(spread + epsilon) * vectors_ref[0:1, :] + vectors_ref[1:2, :]
        ).astype(jnp.bfloat16)
        normed_ref[here, :] = normed
        projected = dot(normed, weight_ref[...], 1, 0) + bias_ref[...]
        qkv_ref[here, :] = projected.astype(jnp.bfloat16)
        queries = qkv_ref[here, :part]
        key_rows = qkv_ref[:seen, part : 2 * part]
        value_rows = qkv_ref[:seen, 2 * part :]
        query_index = block * rows + lax.broadcasted_iota(jnp.int32, (rows, seen), 0)
        key_index = lax.broadcasted_iota(jnp.int32, (rows, seen), 1)
        allowed = (seg_col_ref[here, :] == seg_row_ref[:, :seen]) & (key_index <= query_index)
        result = jnp.zeros((rows, part), jnp.float32)
        for mask in masks:
            scores = dot(jnp.where(mask, queries, 0), key_rows, 1, 1) * scale
            scores = jnp.where(allowed, scores, negative)
            weights = jnp.exp(scores - jnp.max(scores, axis=-1, keepdims=True))
            probs = weights * (1.0 / jnp.sum(weights, axis=-1, keepdims=True))
            result = jnp.where(mask, dot(probs.astype(jnp.bfloat16), value_rows, 1, 0), result)
        attended_ref[here, :] = result.astype(jnp.bfloat16)


def attend_back_kernel(
    rows, scale,
    qkv_ref, grad_ref, seg_row_ref, seg_col_ref,
    out_ref, sums_ref,
    key_sum, value_sum,
):
    length, part = grad_ref.shape
    masks = head_masks((rows, part))
    key_sum[...] = jnp.zeros_like(key_sum)
    value_sum[...] = jnp.zeros_like(value_sum)
    query_total = jnp.zeros((1, part), jnp.float32)
    for block in range(length // rows):
        here = slice(block * rows, (block + 1) * rows)
        seen = (block + 1) * rows
        queries = qkv_ref[here, :part]
        grads = grad_ref[here, :]
        key_rows = qkv_ref[:seen, part : 2 * part]
        value_rows = qkv_ref[:seen, 2 * part :]
        query_index = block * rows + lax.broadcasted_iota(jnp.int32, (seen, rows), 1)
        key_index = lax.broadcasted_iota(jnp.int32, (seen, rows), 0)
        allowed = (seg_col_ref[:seen, :] == seg_row_ref[:, here]) & (key_index <= query_index)
        grad_query = jnp.zeros((rows, part), jnp.float32)
        for mask in masks:
            head_queries = jnp.where(mask, queries, 0)
            head_grads = jnp.where(mask, grads, 0)
            scores = dot(key_rows, head_queries, 1, 1) * scale
            scores = jnp.where(allowed, scores, negative)
            weights = jnp.exp(scores - jnp.max(scores, axis=0, keepdims=True))
            probs = weights * (1.0 / jnp.sum(weights, axis=0, keepdims=True))
            value_sum[:seen, :] += dot(probs.astype(jnp.bfloat16), head_grads, 1, 0)
            grad_probs = dot(value_rows, head_grads, 1, 1)
            inner = jnp.sum(probs * grad_probs, axis=0, keepdims=True)
            grad_scores = (probs * (grad_probs - inner)).astype(jnp.bfloat16)
            key_sum[:seen, :] += dot(grad_scores, head_queries, 1, 0)
            grad_query = jnp.where(mask, dot(grad_scores, key_rows, 0, 0), grad_query)
        grad_query = (grad_query * scale).astype(jnp.bfloat16)
        out_ref[here, :part] = grad_query
        query_total += jnp.sum(grad_query.astype(jnp.float32), axis=0, keepdims=True)
    grad_values = value_sum[...].astype(jnp.bfloat16)
    out_ref[:, part : 2 * part] = (key_sum[...] * scale).astype(jnp.bfloat16)
    out_ref[:, 2 * part :] = grad_values
    sums_ref[0:1, :] = query_total
    sums_ref[1:2, :] = jnp.sum(grad_values.astype(jnp.float32), axis=0, keepdims=True)


def local(
    tokens,
    segments,
    w_qkv,
    b_qv,
    w_out,
    b_out,
    w_up,
    b_up,
    w_down,
    b_down,
    attngain,
    attnshift,
    mlpgain,
    mlpshift,
    cotangent,
):
    fsdp = lax.axis_size("fsdp")
    owners = fsdp * 2
    ctx_place = lax.axis_index("ctx")
    core_place = lax.axis_index("tp") % 2
    block_len, width = tokens.shape[1:]
    length = segments.shape[1]
    local_width = w_qkv.shape[2]
    part_width = local_width // 2
    part_heads = part_width // HD
    heads_local = local_width // HD
    drow = w_qkv.shape[0]
    hrow = b_qv.shape[2]
    score_scale = 1.0 / HD**0.5

    by_kind = jnp.transpose(w_qkv, (1, 0, 2))
    weight_rows = 3 * drow * part_width // LANES
    own_weight = lax.dynamic_slice_in_dim(by_kind, ctx_place * part_width, part_width, 2)
    sent_weight = lax.dynamic_slice_in_dim(by_kind, (1 - ctx_place) * part_width, part_width, 2)
    small_rows = 32
    up_rows = b_up.shape[0]
    qv_rows = b_qv.shape[0] * b_qv.shape[1]

    def padded(array, first):
        array = array.reshape(-1, array.shape[-1])
        rows, lanes = array.shape
        return jnp.pad(array, ((first, small_rows - first - rows), (0, LANES - lanes)))

    small = padded(b_up, 16) + padded(b_qv, 8)
    for place, vector in enumerate((attngain, attnshift, mlpgain, mlpshift, b_out, b_down)):
        small = small + padded(vector, place)
    own_pack = jnp.concatenate([own_weight.reshape(weight_rows, LANES), small])
    other_pack = swap(
        jnp.concatenate([sent_weight.reshape(weight_rows, LANES), small]), "ctx"
    )
    both_packs = jnp.stack(ordered(ctx_place, own_pack, other_pack))
    out_rows = gather_rows(w_out.T)
    up_rows_own = gather_rows(w_up)
    down_rows_own = gather_rows(w_down.T)
    packs = gather_fsdp(both_packs).reshape(owners, weight_rows + small_rows, LANES)
    smalls = packs[:, weight_rows:].astype(jnp.float32)
    vectors = smalls[:, :8, :drow].transpose(1, 0, 2).reshape(8, width)
    gain_one, shift_one, gain_two, shift_two, out_bias, down_bias = (vectors[i] for i in range(6))
    up_bias = smalls[:, 16 : 16 + up_rows, :hrow].transpose(1, 0, 2).reshape(-1)
    qv_bias = (
        smalls[:, 8 : 8 + qv_rows, :hrow].transpose(1, 0, 2).reshape(2, local_width)
    )
    qv_bias_part = lax.dynamic_slice_in_dim(qv_bias, ctx_place * part_width, part_width, 1)
    qkv_bias = jnp.concatenate(
        [qv_bias_part[0], jnp.zeros((part_width,), jnp.float32), qv_bias_part[1]]
    )[None]

    own_tokens = tokens[0]
    half = block_len // 2
    got = swap(lax.dynamic_slice_in_dim(own_tokens, core_place * half, half, 0), "ctx")
    other_tokens = jnp.concatenate(ordered(core_place, got, swap(got, "tp", CORE)))
    all_tokens = jnp.concatenate(ordered(ctx_place, own_tokens, other_tokens))

    packs, out_rows = lax.optimization_barrier((packs, out_rows))
    out_full = pair_rows(out_rows, drow, ctx_place)
    up_full = pair_rows(up_rows_own, drow, ctx_place)
    down_full = pair_rows(down_rows_own, drow, ctx_place)

    seg_row = segments
    seg_col = segments.reshape(length, 1)
    rows = min(256, length)
    normed_all, qkv_rows, attended_part, qkv_part = pl.pallas_call(
        functools.partial(attend_kernel, rows, drow, score_scale),
        out_shape=(
            jax.ShapeDtypeStruct((length, width), jnp.bfloat16),
            jax.ShapeDtypeStruct((length, 3 * part_width), jnp.bfloat16),
            jax.ShapeDtypeStruct((length, part_width), jnp.bfloat16),
            jax.ShapeDtypeStruct((width, 3 * part_width), jnp.bfloat16),
        ),
        compiler_params=pltpu.CompilerParams(vmem_limit_bytes=VMEM_LIMIT),
        cost_estimate=pl.CostEstimate(
            flops=2 * length * width * 3 * part_width, bytes_accessed=8 * length * width,
            transcendentals=length * length,
        ),
    )(all_tokens, packs, vectors, qkv_bias, seg_row, seg_col)

    def to_tokens(array):
        kept = lax.dynamic_slice_in_dim(array, ctx_place * block_len, block_len, 0)
        sent = swap(
            lax.dynamic_slice_in_dim(array, (1 - ctx_place) * block_len, block_len, 0), "ctx"
        )
        return ordered(ctx_place, kept, sent)

    attended = jnp.concatenate(to_tokens(attended_part), axis=1)
    inputs = own_tokens.astype(jnp.float32)

    def out_part(start, count):
        return dot(lax.dynamic_slice_in_dim(attended, start, count, 0), out_full, 1, 1)

    attn_sum, unused = sum_tp(out_part, block_len, core_place)
    middle = inputs + (attn_sum.astype(jnp.float32) + out_bias)
    normed_two = normalize(middle, gain_two, shift_two).astype(jnp.bfloat16)
    hidden_pre = dot(normed_two, up_full, 1, 0) + up_bias
    activated = gelu_tanh(hidden_pre).astype(jnp.bfloat16)

    grad_out_low = cotangent[0]
    grad_out = grad_out_low.astype(jnp.float32)
    grad_down_bias = jnp.sum(grad_out, axis=0)
    grad_activated = dot(grad_out_low, down_full, 1, 0)
    value, gelu_pull = jax.vjp(gelu_tanh, hidden_pre)
    grad_hidden_low = gelu_pull(grad_activated)[0].astype(jnp.bfloat16)

    def up_part(start, count):
        return dot(lax.dynamic_slice_in_dim(grad_hidden_low, start, count, 0), up_full, 1, 1)

    def ffn_products(gated, unused):
        activated, normed_two, grad_hidden_low = gated
        kept_down, sent_down = weight_product(grad_out_low, activated, ctx_place)
        kept_up, sent_up = weight_product(normed_two, grad_hidden_low, ctx_place)
        grad_up_bias = jnp.sum(grad_hidden_low.astype(jnp.float32), axis=0)
        return kept_down, sent_down, kept_up, sent_up, grad_up_bias, activated

    up_sum, done = sum_tp(
        up_part, block_len, core_place, ffn_products, (activated, normed_two, grad_hidden_low)
    )
    kept_down, sent_down, kept_up, sent_up, grad_up_bias, activated = done
    got_down = swap(sent_down, "ctx")
    got_up = swap(sent_up, "ctx")
    grad_normed_two = up_sum.astype(jnp.float32)
    grad_middle_norm, grad_gain_two, grad_shift_two = normalize_back(
        middle, gain_two, grad_normed_two
    )
    grad_middle = grad_out + grad_middle_norm
    grad_branch_low = grad_middle.astype(jnp.bfloat16)
    grad_out_bias = jnp.sum(grad_branch_low.astype(jnp.float32), axis=0)
    grad_attended_low = dot(grad_branch_low, out_full, 1, 0).astype(jnp.bfloat16)
    own_cols = lax.dynamic_slice_in_dim(grad_attended_low, ctx_place * part_width, part_width, 1)
    sent_cols = lax.dynamic_slice_in_dim(
        grad_attended_low, (1 - ctx_place) * part_width, part_width, 1
    )
    sent_cols, late_branch, activated = lax.optimization_barrier(
        (sent_cols, grad_branch_low, activated)
    )
    got_cols = swap(sent_cols, "ctx")
    kept_out, sent_out = weight_product(late_branch, attended, ctx_place)
    got_cols, sent_out = lax.optimization_barrier((got_cols, sent_out))
    got_out = swap(sent_out, "ctx")
    grad_heads = jnp.concatenate(ordered(ctx_place, own_cols, got_cols))
    grad_qkv_part, bias_sums = pl.pallas_call(
        functools.partial(attend_back_kernel, rows, score_scale),
        out_shape=(
            jax.ShapeDtypeStruct((length, 3 * part_width), jnp.bfloat16),
            jax.ShapeDtypeStruct((2, part_width), jnp.float32),
        ),
        scratch_shapes=[
            pltpu.VMEM((length, part_width), jnp.float32),
            pltpu.VMEM((length, part_width), jnp.float32),
        ],
        compiler_params=pltpu.CompilerParams(vmem_limit_bytes=VMEM_LIMIT),
        cost_estimate=pl.CostEstimate(
            flops=10 * length * length * part_width, bytes_accessed=2 * length * width,
            transcendentals=length * length,
        ),
    )(qkv_rows, grad_heads, seg_row, seg_col)
    def down_part(start, count):
        return dot(lax.dynamic_slice_in_dim(activated, start, count, 0), down_full, 1, 1)

    grad_qkv_kept = lax.dynamic_slice_in_dim(grad_qkv_part, ctx_place * block_len, block_len, 0)
    grad_qkv_sent = lax.dynamic_slice_in_dim(
        grad_qkv_part, (1 - ctx_place) * block_len, block_len, 0
    )
    grad_qkv_sent, late_part, activated, got_down, kept_down = lax.optimization_barrier(
        (grad_qkv_sent, grad_qkv_part, activated, got_down, kept_down)
    )
    grad_qkv_got = swap(grad_qkv_sent, "ctx")
    grad_qkv_weight = dot(normed_all, late_part, 0, 0).astype(jnp.bfloat16)
    down_pairs = pair_sum(kept_down, got_down)
    mlp_sum, unused = sum_tp(down_part, block_len, core_place)
    finished = middle + (mlp_sum.astype(jnp.float32) + down_bias)
    grad_qkv_got, grad_qkv_weight, down_pairs = lax.optimization_barrier(
        (grad_qkv_got, grad_qkv_weight, down_pairs)
    )
    grad_down = scatter_rows(down_pairs).T.astype(jnp.float32)
    grad_qkv_first, grad_qkv_second = ordered(ctx_place, grad_qkv_kept, grad_qkv_got)
    grad_qkv_sum = jnp.sum(
        lax.all_to_all(
            grad_qkv_weight.reshape(fsdp, 2 * drow, 3 * part_width), "fsdp", 0, 0, tiled=True
        ).astype(jnp.float32),
        axis=0,
    )
    own_rows = lax.dynamic_slice_in_dim(grad_qkv_sum, ctx_place * drow, drow, 0)
    sent_rows = swap(
        lax.dynamic_slice_in_dim(grad_qkv_sum, (1 - ctx_place) * drow, drow, 0).astype(
            jnp.bfloat16
        ),
        "ctx",
    ).astype(jnp.float32)
    grad_qkv_out = jnp.concatenate(
        [
            part.reshape(drow, 3, part_width)
            for part in ordered(ctx_place, own_rows, sent_rows)
        ],
        axis=2,
    )
    nothing = jnp.zeros_like(bias_sums)
    grad_qv_bias = jnp.concatenate(ordered(ctx_place, bias_sums, nothing), axis=1)

    qkv_other = swap(qkv_part, "ctx")
    qkv_first, qkv_second = ordered(ctx_place, qkv_part, qkv_other)

    def first_part(start, count):
        return dot(
            lax.dynamic_slice_in_dim(grad_qkv_first, start, count, 0), qkv_first, 1, 1
        ) + dot(lax.dynamic_slice_in_dim(grad_qkv_second, start, count, 0), qkv_second, 1, 1)

    def by_owner(vector):
        return vector.reshape(owners, 1, drow)

    def row_block(array, first):
        rows, lanes = array.shape[1:]
        return jnp.pad(
            array, ((0, 0), (first, small_rows - first - rows), (0, LANES - lanes))
        )

    def small_work(gated, chip_sum):
        kept_up, got_up, kept_out, got_out = gated
        half_inputs = lax.dynamic_slice_in_dim(inputs, core_place * half, half, 0)
        half_grad = chip_sum.astype(jnp.float32)
        unused, gain_share, shift_share = normalize_back(half_inputs, gain_one, half_grad)
        small_grads = row_block(
            grad_up_bias.reshape(up_rows, owners, hrow).transpose(1, 0, 2), 16
        ) + row_block(grad_qv_bias.reshape(qv_rows, owners, hrow).transpose(1, 0, 2), 8)
        for place, vector in enumerate(
            (
                gain_share,
                shift_share,
                grad_gain_two,
                grad_shift_two,
                grad_out_bias,
                grad_down_bias,
            )
        ):
            small_grads = small_grads + row_block(by_owner(vector), place)
        return small_grads, pair_sum(kept_up, got_up), pair_sum(kept_out, got_out)

    first_sum, (small_grads, up_pairs, out_pairs) = sum_tp(
        first_part, block_len, core_place, small_work, (kept_up, got_up, kept_out, got_out)
    )
    grad_up = scatter_rows(up_pairs).astype(jnp.float32)
    grad_out_weight = scatter_rows(out_pairs).T.astype(jnp.float32)
    grad_inputs_norm, unused, unused = normalize_back(
        inputs, gain_one, first_sum.astype(jnp.float32)
    )
    grad_inputs = grad_middle + grad_inputs_norm
    small_sums = jnp.sum(
        lax.all_to_all(small_grads, ("fsdp", "ctx"), 0, 0, tiled=True), axis=0
    )
    share = small_sums[:2]
    share = share + swap(share, "tp", CORE)
    share = share + swap(share, "tp", CHIP)
    gain_one_sum, shift_one_sum = share[0, :drow], share[1, :drow]
    vector_sums = small_sums[:8, :drow]
    up_bias_sum = small_sums[16 : 16 + up_rows, :hrow]
    qv_bias_sum = small_sums[8 : 8 + qv_rows, :hrow].reshape(2, heads_local, hrow)

    return (
        finished.astype(jnp.bfloat16)[None],
        grad_inputs[None],
        grad_qkv_out,
        qv_bias_sum,
        grad_out_weight,
        vector_sums[4],
        grad_up,
        up_bias_sum,
        grad_down,
        vector_sums[5],
        gain_one_sum,
        shift_one_sum,
        vector_sums[2],
        vector_sums[3],
    )


def solution(mesh):
    placed = (
        P("fsdp", "ctx", None),
        P("fsdp", None),
        P(("fsdp", "ctx"), None, "tp"),
        P(None, "tp", ("fsdp", "ctx")),
        P("tp", ("fsdp", "ctx")),
        P(("fsdp", "ctx")),
        P(("fsdp", "ctx"), "tp"),
        P("tp", ("fsdp", "ctx")),
        P("tp", ("fsdp", "ctx")),
        P(("fsdp", "ctx")),
        P(("fsdp", "ctx")),
        P(("fsdp", "ctx")),
        P(("fsdp", "ctx")),
        P(("fsdp", "ctx")),
        P("fsdp", "ctx", None),
    )
    return jax.shard_map(
        local,
        mesh=mesh,
        in_specs=placed,
        out_specs=(
            P("fsdp", "ctx", None),
            P("fsdp", "ctx", None),
            P(("fsdp", "ctx"), None, "tp"),
            P(None, "tp", ("fsdp", "ctx")),
            P("tp", ("fsdp", "ctx")),
            P(("fsdp", "ctx")),
            P(("fsdp", "ctx"), "tp"),
            P("tp", ("fsdp", "ctx")),
            P("tp", ("fsdp", "ctx")),
            P(("fsdp", "ctx")),
            P(("fsdp", "ctx")),
            P(("fsdp", "ctx")),
            P(("fsdp", "ctx")),
            P(("fsdp", "ctx")),
        ),
        check_vma=False,
    )
```

```python
import functools

import jax
import jax.numpy as jnp
from jax import lax
from jax.experimental import pallas as pl
from jax.experimental.layout import Layout, with_layout_constraint
from jax.experimental.pallas import tpu as pltpu
from jax.sharding import PartitionSpec as P

HD = 64
LANES = 128
CORE = 1
CHIP = 2
VMEM_LIMIT = 16 * 1024 * 1024

epsilon = 1e-05
negative = -1e30


def swap(array, axis, mask=1):
    devices = lax.axis_size(axis)
    return lax.ppermute(array, axis, [(i, i ^ mask) for i in range(devices)])


def ordered(place, own, other):
    return jnp.where(place == 0, own, other), jnp.where(place == 0, other, own)


def gather_fsdp(block):
    devices = lax.axis_size("fsdp")
    return lax.all_to_all(
        jnp.broadcast_to(block[None], (devices,) + block.shape), "fsdp", 0, 0, tiled=True
    )


def gather_rows(block):
    return lax.all_gather(block, "fsdp", axis=0, tiled=True)


def gather_cyclic(block):
    devices = lax.axis_size("fsdp")
    if devices > 4:
        return gather_fsdp(block)
    parts = [block] + [
        lax.ppermute(block, "fsdp", [(i, (i - step) % devices) for i in range(devices)])
        for step in range(1, devices)
    ]
    return lax.dynamic_slice_in_dim(
        jnp.stack(parts + parts), devices - lax.axis_index("fsdp"), devices, 0
    )


def row_major(array):
    return with_layout_constraint(array, Layout(tuple(range(array.ndim))))


def pair_rows(own, rows, ctx_place):
    own = own.reshape(-1, rows, own.shape[1])
    first, second = ordered(ctx_place, own, swap(own, "ctx"))
    return jnp.stack([first, second], axis=1).reshape(-1, own.shape[2])


def sum_tp(part_of, rows, core_place, work=None, gated=()):
    half = rows // 2
    sent = swap(part_of((1 - core_place) * half, half).astype(jnp.bfloat16), "tp", CORE)
    kept = part_of(core_place * half, half)
    chip_sum = (kept + sent.astype(jnp.float32)).astype(jnp.bfloat16)
    chip_sum, gated = lax.optimization_barrier((chip_sum, gated))
    across = swap(chip_sum, "tp", CHIP)
    done, free = work(gated, chip_sum) if work else ((), ())
    across, done = lax.optimization_barrier((across, done))
    total = (chip_sum.astype(jnp.float32) + across.astype(jnp.float32)).astype(jnp.bfloat16)
    summed = jnp.concatenate(ordered(core_place, total, swap(total, "tp", CORE)), axis=0)
    return summed, done, free


def weight_product(wide, narrow, ctx_place):
    devices = lax.axis_size("fsdp")
    rows = wide.shape[1] // (devices * 2)
    product = dot(wide, narrow, 0, 0).astype(jnp.bfloat16).reshape(devices, 2, rows, -1)
    return tuple(
        part.reshape(devices * rows, -1)
        for part in ordered(ctx_place, product[:, 0], product[:, 1])
    )


def pair_sum(kept, sent):
    return (kept.astype(jnp.float32) + sent.astype(jnp.float32)).astype(jnp.bfloat16)


def scatter_rows(array):
    return lax.psum_scatter(array, "fsdp", scatter_dimension=0, tiled=True)


def normalize(matrix, factor, offset):
    average = jnp.mean(matrix, axis=-1, keepdims=True)
    centered = matrix - average
    spread = jnp.mean(centered * centered, axis=-1, keepdims=True)
    return centered * lax.rsqrt(spread + epsilon) * factor + offset


def normalize_back(matrix, factor, grad):
    average = jnp.mean(matrix, axis=-1, keepdims=True)
    centered = matrix - average
    spread = jnp.mean(centered * centered, axis=-1, keepdims=True)
    inverse = lax.rsqrt(spread + epsilon)
    xhat = centered * inverse
    scaled = grad * factor
    mean_scaled = jnp.mean(scaled, axis=-1, keepdims=True)
    mean_product = jnp.mean(scaled * xhat, axis=-1, keepdims=True)
    grad_in = inverse * (scaled - mean_scaled - xhat * mean_product)
    return grad_in, jnp.sum(grad * xhat, axis=0), jnp.sum(grad, axis=0)


def gelu_tanh(inputs):
    cubed_vals = inputs * inputs * inputs
    return 0.5 * inputs * (1.0 + jnp.tanh(0.7978845608028654 * (inputs + 0.044715 * cubed_vals)))


def dot(left, right, left_dim, right_dim):
    return lax.dot_general(
        left, right, (((left_dim,), (right_dim,)), ((), ())), preferred_element_type=jnp.float32
    )


def head_masks(shape):
    lane = lax.broadcasted_iota(jnp.int32, shape, 1)
    return [(lane // HD) == head for head in range(shape[1] // HD)]


def attend_kernel(
    rows, drow, scale,
    tokens_ref, packs_ref, vectors_ref, bias_ref, seg_row_ref, seg_col_ref,
    normed_ref, qkv_ref, attended_ref, weight_ref,
):
    length = tokens_ref.shape[0]
    part = attended_ref.shape[1]
    for owner in range(packs_ref.shape[0]):
        for kind in range(3):
            weight_ref[owner * drow : (owner + 1) * drow, kind * part : (kind + 1) * part] = (
                packs_ref[owner, kind * drow : (kind + 1) * drow, :]
            )
    masks = head_masks((rows, part))
    for block in range(length // rows):
        here = slice(block * rows, (block + 1) * rows)
        seen = (block + 1) * rows
        inputs = tokens_ref[here, :].astype(jnp.float32)
        centered = inputs - jnp.mean(inputs, axis=-1, keepdims=True)
        spread = jnp.mean(centered * centered, axis=-1, keepdims=True)
        normed = (
            centered * lax.rsqrt(spread + epsilon) * vectors_ref[0:1, :] + vectors_ref[1:2, :]
        ).astype(jnp.bfloat16)
        normed_ref[here, :] = normed
        projected = dot(normed, weight_ref[...], 1, 0) + bias_ref[...]
        qkv_ref[here, :] = projected.astype(jnp.bfloat16)
        queries = qkv_ref[here, :part]
        key_rows = qkv_ref[:seen, part : 2 * part]
        value_rows = qkv_ref[:seen, 2 * part :]
        query_index = block * rows + lax.broadcasted_iota(jnp.int32, (rows, seen), 0)
        key_index = lax.broadcasted_iota(jnp.int32, (rows, seen), 1)
        allowed = (seg_col_ref[here, :] == seg_row_ref[:, :seen]) & (key_index <= query_index)
        result = jnp.zeros((rows, part), jnp.float32)
        for mask in masks:
            scores = dot(jnp.where(mask, queries, 0), key_rows, 1, 1) * scale
            scores = jnp.where(allowed, scores, negative)
            weights = jnp.exp(scores - jnp.max(scores, axis=-1, keepdims=True))
            probs = weights * (1.0 / jnp.sum(weights, axis=-1, keepdims=True))
            result = jnp.where(mask, dot(probs.astype(jnp.bfloat16), value_rows, 1, 0), result)
        attended_ref[here, :] = result.astype(jnp.bfloat16)


def attend_back_kernel(
    rows, scale,
    qkv_ref, grad_ref, seg_row_ref, seg_col_ref,
    out_ref, sums_ref,
    key_sum, value_sum,
):
    length, part = grad_ref.shape
    masks = head_masks((rows, part))
    key_sum[...] = jnp.zeros_like(key_sum)
    value_sum[...] = jnp.zeros_like(value_sum)
    query_total = jnp.zeros((1, part), jnp.float32)
    for block in range(length // rows):
        here = slice(block * rows, (block + 1) * rows)
        seen = (block + 1) * rows
        queries = qkv_ref[here, :part]
        grads = grad_ref[here, :]
        key_rows = qkv_ref[:seen, part : 2 * part]
        value_rows = qkv_ref[:seen, 2 * part :]
        query_index = block * rows + lax.broadcasted_iota(jnp.int32, (seen, rows), 1)
        key_index = lax.broadcasted_iota(jnp.int32, (seen, rows), 0)
        allowed = (seg_col_ref[:seen, :] == seg_row_ref[:, here]) & (key_index <= query_index)
        grad_query = jnp.zeros((rows, part), jnp.float32)
        for mask in masks:
            head_queries = jnp.where(mask, queries, 0)
            head_grads = jnp.where(mask, grads, 0)
            scores = dot(key_rows, head_queries, 1, 1) * scale
            scores = jnp.where(allowed, scores, negative)
            weights = jnp.exp(scores - jnp.max(scores, axis=0, keepdims=True))
            probs = weights * (1.0 / jnp.sum(weights, axis=0, keepdims=True))
            value_sum[:seen, :] += dot(probs.astype(jnp.bfloat16), head_grads, 1, 0)
            grad_probs = dot(value_rows, head_grads, 1, 1)
            inner = jnp.sum(probs * grad_probs, axis=0, keepdims=True)
            grad_scores = (probs * (grad_probs - inner)).astype(jnp.bfloat16)
            key_sum[:seen, :] += dot(grad_scores, head_queries, 1, 0)
            grad_query = jnp.where(mask, dot(grad_scores, key_rows, 0, 0), grad_query)
        grad_query = (grad_query * scale).astype(jnp.bfloat16)
        out_ref[here, :part] = grad_query
        query_total += jnp.sum(grad_query.astype(jnp.float32), axis=0, keepdims=True)
    grad_values = value_sum[...].astype(jnp.bfloat16)
    out_ref[:, part : 2 * part] = (key_sum[...] * scale).astype(jnp.bfloat16)
    out_ref[:, 2 * part :] = grad_values
    sums_ref[0:1, :] = query_total
    sums_ref[1:2, :] = jnp.sum(grad_values.astype(jnp.float32), axis=0, keepdims=True)


def local(
    tokens,
    segments,
    w_qkv,
    b_qv,
    w_out,
    b_out,
    w_up,
    b_up,
    w_down,
    b_down,
    attngain,
    attnshift,
    mlpgain,
    mlpshift,
    cotangent,
):
    fsdp = lax.axis_size("fsdp")
    owners = fsdp * 2
    ctx_place = lax.axis_index("ctx")
    core_place = lax.axis_index("tp") % 2
    block_len, width = tokens.shape[1:]
    length = segments.shape[1]
    local_width = w_qkv.shape[2]
    part_width = local_width // 2
    part_heads = part_width // HD
    heads_local = local_width // HD
    drow = w_qkv.shape[0]
    hrow = b_qv.shape[2]
    score_scale = 1.0 / HD**0.5

    by_kind = jnp.transpose(w_qkv, (1, 0, 2))
    weight_rows = 3 * drow * part_width // LANES
    own_weight = lax.dynamic_slice_in_dim(by_kind, ctx_place * part_width, part_width, 2)
    sent_weight = lax.dynamic_slice_in_dim(by_kind, (1 - ctx_place) * part_width, part_width, 2)
    small_rows = 32
    up_rows = b_up.shape[0]
    qv_rows = b_qv.shape[0] * b_qv.shape[1]

    def padded(array, first):
        array = array.reshape(-1, array.shape[-1])
        rows, lanes = array.shape
        return jnp.pad(array, ((first, small_rows - first - rows), (0, LANES - lanes)))

    small = padded(b_up, 16) + padded(b_qv, 8)
    for place, vector in enumerate((attngain, attnshift, mlpgain, mlpshift, b_out, b_down)):
        small = small + padded(vector, place)
    own_pack = jnp.concatenate([own_weight.reshape(weight_rows, LANES), small])
    other_pack = swap(
        jnp.concatenate([sent_weight.reshape(weight_rows, LANES), small]), "ctx"
    )
    own_tokens, other_pack = lax.optimization_barrier((tokens[0], other_pack))
    half = block_len // 2
    got = swap(lax.dynamic_slice_in_dim(own_tokens, core_place * half, half, 0), "ctx")
    other_tokens = jnp.concatenate(ordered(core_place, got, swap(got, "tp", CORE)))
    all_tokens = jnp.concatenate(ordered(ctx_place, own_tokens, other_tokens))

    both_packs = jnp.stack(ordered(ctx_place, own_pack, other_pack))
    up_rows_own = gather_rows(w_up)
    down_rows_own = gather_rows(row_major(w_down.T))
    both_packs, w_out_rows = lax.optimization_barrier((both_packs, row_major(w_out.T)))
    packs = gather_fsdp(both_packs).reshape(owners, weight_rows + small_rows, LANES)
    smalls = packs[:, weight_rows:].astype(jnp.float32)
    vectors = smalls[:, :8, :drow].transpose(1, 0, 2).reshape(8, width)
    gain_one, shift_one, gain_two, shift_two, out_bias, down_bias = (vectors[i] for i in range(6))
    up_bias = smalls[:, 16 : 16 + up_rows, :hrow].transpose(1, 0, 2).reshape(-1)
    qv_bias = (
        smalls[:, 8 : 8 + qv_rows, :hrow].transpose(1, 0, 2).reshape(2, local_width)
    )
    qv_bias_part = lax.dynamic_slice_in_dim(qv_bias, ctx_place * part_width, part_width, 1)
    qkv_bias = jnp.concatenate(
        [qv_bias_part[0], jnp.zeros((part_width,), jnp.float32), qv_bias_part[1]]
    )[None]

    out_full = pair_rows(
        gather_cyclic(w_out_rows).reshape(fsdp * drow, local_width), drow, ctx_place
    )
    up_full = pair_rows(up_rows_own, drow, ctx_place)
    down_full = pair_rows(down_rows_own, drow, ctx_place)

    seg_row = segments
    seg_col = segments.reshape(length, 1)
    rows = min(256, length)
    normed_all, qkv_rows, attended_part, qkv_part = pl.pallas_call(
        functools.partial(attend_kernel, rows, drow, score_scale),
        out_shape=(
            jax.ShapeDtypeStruct((length, width), jnp.bfloat16),
            jax.ShapeDtypeStruct((length, 3 * part_width), jnp.bfloat16),
            jax.ShapeDtypeStruct((length, part_width), jnp.bfloat16),
            jax.ShapeDtypeStruct((width, 3 * part_width), jnp.bfloat16),
        ),
        compiler_params=pltpu.CompilerParams(vmem_limit_bytes=VMEM_LIMIT),
        cost_estimate=pl.CostEstimate(
            flops=2 * length * width * 3 * part_width, bytes_accessed=8 * length * width,
            transcendentals=length * length,
        ),
    )(all_tokens, packs, vectors, qkv_bias, seg_row, seg_col)

    def to_tokens(array):
        kept = lax.dynamic_slice_in_dim(array, ctx_place * block_len, block_len, 0)
        sent = swap(
            lax.dynamic_slice_in_dim(array, (1 - ctx_place) * block_len, block_len, 0), "ctx"
        )
        return ordered(ctx_place, kept, sent)

    attended = jnp.concatenate(to_tokens(attended_part), axis=1)
    inputs = own_tokens.astype(jnp.float32)

    def out_part(start, count):
        return dot(lax.dynamic_slice_in_dim(attended, start, count, 0), out_full, 1, 1)

    attn_sum, unused, unused = sum_tp(out_part, block_len, core_place)
    middle = inputs + (attn_sum.astype(jnp.float32) + out_bias)
    normed_two = normalize(middle, gain_two, shift_two).astype(jnp.bfloat16)
    hidden_pre = dot(normed_two, up_full, 1, 0) + up_bias
    activated = gelu_tanh(hidden_pre).astype(jnp.bfloat16)

    grad_out_low = cotangent[0]
    grad_out = grad_out_low.astype(jnp.float32)
    kept_down, sent_down = weight_product(grad_out_low, activated, ctx_place)
    sent_down, hidden_pre = lax.optimization_barrier((sent_down, hidden_pre))
    got_down = swap(sent_down, "ctx")
    grad_activated = dot(grad_out_low, down_full, 1, 0)
    value, gelu_pull = jax.vjp(gelu_tanh, hidden_pre)
    grad_hidden_low = gelu_pull(grad_activated)[0].astype(jnp.bfloat16)

    def up_part(start, count):
        return dot(lax.dynamic_slice_in_dim(grad_hidden_low, start, count, 0), up_full, 1, 1)

    def ffn_products(gated, unused):
        activated, normed_two, grad_hidden_low, grad_out = gated
        kept_up, sent_up = weight_product(normed_two, grad_hidden_low, ctx_place)
        got_first = swap(sent_up[:, : sent_up.shape[1] // 2], "ctx")
        grad_up_bias = jnp.sum(grad_hidden_low.astype(jnp.float32), axis=0)
        grad_down_bias = jnp.sum(grad_out, axis=0)
        return (kept_up, sent_up, grad_up_bias, grad_down_bias, activated), got_first

    up_sum, done, got_up_first = sum_tp(
        up_part,
        block_len,
        core_place,
        ffn_products,
        (activated, normed_two, grad_hidden_low, grad_out),
    )
    kept_up, sent_up, grad_up_bias, grad_down_bias, activated = done
    sent_up = sent_up[:, sent_up.shape[1] // 2 :]
    grad_normed_two = up_sum.astype(jnp.float32)
    grad_middle_norm, grad_gain_two, grad_shift_two = normalize_back(
        middle, gain_two, grad_normed_two
    )
    grad_middle = grad_out + grad_middle_norm
    grad_branch_low = grad_middle.astype(jnp.bfloat16)
    grad_out_bias = jnp.sum(grad_branch_low.astype(jnp.float32), axis=0)
    grad_branch_low, got_down, kept_down = lax.optimization_barrier(
        (grad_branch_low, got_down, kept_down)
    )
    down_pairs = pair_sum(kept_down, got_down)
    grad_branch_low, down_pairs = lax.optimization_barrier((grad_branch_low, down_pairs))
    grad_down = row_major(scatter_rows(down_pairs))
    grad_attended_low = dot(grad_branch_low, out_full, 1, 0).astype(jnp.bfloat16)
    own_cols = lax.dynamic_slice_in_dim(grad_attended_low, ctx_place * part_width, part_width, 1)
    sent_cols = lax.dynamic_slice_in_dim(
        grad_attended_low, (1 - ctx_place) * part_width, part_width, 1
    )
    sent_cols, late_branch, sent_up, activated = lax.optimization_barrier(
        (sent_cols, grad_branch_low, sent_up, activated)
    )
    got_cols = swap(sent_cols, "ctx")
    kept_out, sent_out = weight_product(late_branch, attended, ctx_place)
    sent_out, sent_up = lax.optimization_barrier((sent_out, sent_up))
    got_up_second = swap(sent_up, "ctx")
    got_cols, sent_out = lax.optimization_barrier((got_cols, sent_out))
    grad_heads = jnp.concatenate(ordered(ctx_place, own_cols, got_cols))
    grad_qkv_part, bias_sums = pl.pallas_call(
        functools.partial(attend_back_kernel, rows, score_scale),
        out_shape=(
            jax.ShapeDtypeStruct((length, 3 * part_width), jnp.bfloat16),
            jax.ShapeDtypeStruct((2, part_width), jnp.float32),
        ),
        scratch_shapes=[
            pltpu.VMEM((length, part_width), jnp.float32),
            pltpu.VMEM((length, part_width), jnp.float32),
        ],
        compiler_params=pltpu.CompilerParams(vmem_limit_bytes=VMEM_LIMIT),
        cost_estimate=pl.CostEstimate(
            flops=10 * length * length * part_width, bytes_accessed=2 * length * width,
            transcendentals=length * length,
        ),
    )(qkv_rows, grad_heads, seg_row, seg_col)
    def down_part(start, count):
        return dot(lax.dynamic_slice_in_dim(activated, start, count, 0), down_full, 1, 1)

    grad_qkv_kept = lax.dynamic_slice_in_dim(grad_qkv_part, ctx_place * block_len, block_len, 0)
    grad_qkv_sent = lax.dynamic_slice_in_dim(
        grad_qkv_part, (1 - ctx_place) * block_len, block_len, 0
    )
    grad_qkv_sent, late_part, activated, sent_out, got_up_first, got_up_second = (
        lax.optimization_barrier(
            (grad_qkv_sent, grad_qkv_part, activated, sent_out, got_up_first, got_up_second)
        )
    )
    grad_qkv_got = swap(grad_qkv_sent, "ctx")
    up_pairs = pair_sum(kept_up, jnp.concatenate([got_up_first, got_up_second], axis=1))
    grad_qkv_weight = dot(normed_all, late_part, 0, 0).astype(jnp.bfloat16)
    grad_qkv_weight, sent_out = lax.optimization_barrier((grad_qkv_weight, sent_out))
    got_out = swap(sent_out, "ctx")
    mlp_sum, unused, unused = sum_tp(down_part, block_len, core_place)
    finished = middle + (mlp_sum.astype(jnp.float32) + down_bias)
    grad_qkv_got, grad_qkv_weight, up_pairs = lax.optimization_barrier(
        (grad_qkv_got, grad_qkv_weight, up_pairs)
    )
    grad_up = scatter_rows(up_pairs)
    grad_qkv_first, grad_qkv_second = ordered(ctx_place, grad_qkv_kept, grad_qkv_got)
    grad_qkv_sum = jnp.sum(
        lax.all_to_all(
            grad_qkv_weight.reshape(fsdp, 2 * drow, 3 * part_width), "fsdp", 0, 0, tiled=True
        ).astype(jnp.float32),
        axis=0,
    )
    own_rows = lax.dynamic_slice_in_dim(grad_qkv_sum, ctx_place * drow, drow, 0)
    sent_rows = swap(
        lax.dynamic_slice_in_dim(grad_qkv_sum, (1 - ctx_place) * drow, drow, 0).astype(
            jnp.bfloat16
        ),
        "ctx",
    ).astype(jnp.float32)
    grad_qkv_out = jnp.concatenate(
        [
            part.reshape(drow, 3, part_width)
            for part in ordered(ctx_place, own_rows, sent_rows)
        ],
        axis=2,
    )
    nothing = jnp.zeros_like(bias_sums)
    grad_qv_bias = jnp.concatenate(ordered(ctx_place, bias_sums, nothing), axis=1)

    qkv_other = swap(qkv_part, "ctx")
    qkv_first, qkv_second = ordered(ctx_place, qkv_part, qkv_other)

    def first_part(start, count):
        return dot(
            lax.dynamic_slice_in_dim(grad_qkv_first, start, count, 0), qkv_first, 1, 1
        ) + dot(lax.dynamic_slice_in_dim(grad_qkv_second, start, count, 0), qkv_second, 1, 1)

    def by_owner(vector):
        return vector.reshape(owners, 1, drow)

    def row_block(array, first):
        rows, lanes = array.shape[1:]
        return jnp.pad(
            array, ((0, 0), (first, small_rows - first - rows), (0, LANES - lanes))
        )

    def small_work(gated, chip_sum):
        kept_out, got_out = gated
        half_inputs = lax.dynamic_slice_in_dim(inputs, core_place * half, half, 0)
        half_grad = chip_sum.astype(jnp.float32)
        unused, gain_share, shift_share = normalize_back(half_inputs, gain_one, half_grad)
        small_grads = row_block(
            grad_up_bias.reshape(up_rows, owners, hrow).transpose(1, 0, 2), 16
        ) + row_block(grad_qv_bias.reshape(qv_rows, owners, hrow).transpose(1, 0, 2), 8)
        for place, vector in enumerate(
            (
                gain_share,
                shift_share,
                grad_gain_two,
                grad_shift_two,
                grad_out_bias,
                grad_down_bias,
            )
        ):
            small_grads = small_grads + row_block(by_owner(vector), place)
        return (small_grads, pair_sum(kept_out, got_out)), ()

    first_sum, (small_grads, out_pairs), unused = sum_tp(
        first_part, block_len, core_place, small_work, (kept_out, got_out)
    )
    grad_out_weight = row_major(scatter_rows(out_pairs))
    grad_inputs_norm, unused, unused = normalize_back(
        inputs, gain_one, first_sum.astype(jnp.float32)
    )
    grad_inputs = grad_middle + grad_inputs_norm
    small_sums = jnp.sum(
        lax.all_to_all(small_grads, ("fsdp", "ctx"), 0, 0, tiled=True), axis=0
    )
    share = small_sums[:2]
    share = share + swap(share, "tp", CORE)
    share = share + swap(share, "tp", CHIP)
    gain_one_sum, shift_one_sum = share[0, :drow], share[1, :drow]
    vector_sums = small_sums[:8, :drow]
    up_bias_sum = small_sums[16 : 16 + up_rows, :hrow]
    qv_bias_sum = small_sums[8 : 8 + qv_rows, :hrow].reshape(2, heads_local, hrow)

    return (
        finished.astype(jnp.bfloat16)[None],
        grad_inputs[None],
        grad_qkv_out,
        qv_bias_sum,
        grad_out_weight.T.astype(jnp.float32),
        vector_sums[4],
        grad_up.astype(jnp.float32),
        up_bias_sum,
        grad_down.T.astype(jnp.float32),
        vector_sums[5],
        gain_one_sum,
        shift_one_sum,
        vector_sums[2],
        vector_sums[3],
    )


def solution(mesh):
    placed = (
        P("fsdp", "ctx", None),
        P("fsdp", None),
        P(("fsdp", "ctx"), None, "tp"),
        P(None, "tp", ("fsdp", "ctx")),
        P("tp", ("fsdp", "ctx")),
        P(("fsdp", "ctx")),
        P(("fsdp", "ctx"), "tp"),
        P("tp", ("fsdp", "ctx")),
        P("tp", ("fsdp", "ctx")),
        P(("fsdp", "ctx")),
        P(("fsdp", "ctx")),
        P(("fsdp", "ctx")),
        P(("fsdp", "ctx")),
        P(("fsdp", "ctx")),
        P("fsdp", "ctx", None),
    )
    return jax.shard_map(
        local,
        mesh=mesh,
        in_specs=placed,
        out_specs=(
            P("fsdp", "ctx", None),
            P("fsdp", "ctx", None),
            P(("fsdp", "ctx"), None, "tp"),
            P(None, "tp", ("fsdp", "ctx")),
            P("tp", ("fsdp", "ctx")),
            P(("fsdp", "ctx")),
            P(("fsdp", "ctx"), "tp"),
            P("tp", ("fsdp", "ctx")),
            P("tp", ("fsdp", "ctx")),
            P(("fsdp", "ctx")),
            P(("fsdp", "ctx")),
            P(("fsdp", "ctx")),
            P(("fsdp", "ctx")),
            P(("fsdp", "ctx")),
        ),
        check_vma=False,
    )
```

```python
import functools

import jax
import jax.numpy as jnp
from jax import lax
from jax.experimental import pallas as pl
from jax.experimental.layout import Layout, with_layout_constraint
from jax.experimental.pallas import tpu as pltpu
from jax.sharding import PartitionSpec as P

HD = 64
LANES = 128
CORE = 1
CHIP = 2
VMEM_LIMIT = 16 * 1024 * 1024

epsilon = 1e-05
negative = -1e30


def swap(array, axis, mask=1):
    devices = lax.axis_size(axis)
    return lax.ppermute(array, axis, [(i, i ^ mask) for i in range(devices)])


def ordered(place, own, other):
    return jnp.where(place == 0, own, other), jnp.where(place == 0, other, own)


def gather_fsdp(block):
    devices = lax.axis_size("fsdp")
    return lax.all_to_all(
        jnp.broadcast_to(block[None], (devices,) + block.shape), "fsdp", 0, 0, tiled=True
    )


def gather_rows(block):
    return lax.all_gather(block, "fsdp", axis=0, tiled=True)


def row_major(array):
    return with_layout_constraint(array, Layout(tuple(range(array.ndim))))


def sum_tp(part_of, rows, core_place, work=None, gated=()):
    half = rows // 2
    sent = swap(part_of((1 - core_place) * half, half).astype(jnp.bfloat16), "tp", CORE)
    kept = part_of(core_place * half, half)
    chip_sum = (kept + sent.astype(jnp.float32)).astype(jnp.bfloat16)
    chip_sum, gated = lax.optimization_barrier((chip_sum, gated))
    across = swap(chip_sum, "tp", CHIP)
    done, free = work(gated, chip_sum) if work else ((), ())
    across, done = lax.optimization_barrier((across, done))
    total = (chip_sum.astype(jnp.float32) + across.astype(jnp.float32)).astype(jnp.bfloat16)
    summed = jnp.concatenate(ordered(core_place, total, swap(total, "tp", CORE)), axis=0)
    return summed, done, free


def both_tokens(rows, ctx_place, core_place):
    half = rows.shape[0] // 2
    got = swap(lax.dynamic_slice_in_dim(rows, core_place * half, half, 0), "ctx")
    other = jnp.concatenate(ordered(core_place, got, swap(got, "tp", CORE)))
    return jnp.concatenate(ordered(ctx_place, rows, other))


def chip_part(left, right, core_place):
    length = left.shape[0]
    split = left.reshape(2, 2, length // 4, -1)

    def product(core):
        rows = lax.dynamic_index_in_dim(split, core, 1, False).reshape(length // 2, -1)
        return dot(rows, right, 1, 1)

    sent = swap(product(1 - core_place).astype(jnp.bfloat16), "tp", CORE)
    total = (product(core_place) + sent.astype(jnp.float32)).astype(jnp.bfloat16)
    return total.reshape(2, length // 4, -1)


def weight_product(wide, narrow, ctx_place):
    devices = lax.axis_size("fsdp")
    rows = wide.shape[1] // (devices * 2)
    product = dot(wide, narrow, 0, 0).astype(jnp.bfloat16).reshape(devices, 2, rows, -1)
    return tuple(
        part.reshape(devices * rows, -1)
        for part in ordered(ctx_place, product[:, 0], product[:, 1])
    )


def pair_sum(kept, sent):
    return (kept.astype(jnp.float32) + sent.astype(jnp.float32)).astype(jnp.bfloat16)


def scatter_rows(array):
    return lax.psum_scatter(array, "fsdp", scatter_dimension=0, tiled=True)


def normalize(matrix, factor, offset):
    average = jnp.mean(matrix, axis=-1, keepdims=True)
    centered = matrix - average
    spread = jnp.mean(centered * centered, axis=-1, keepdims=True)
    return centered * lax.rsqrt(spread + epsilon) * factor + offset


def normalize_back(matrix, factor, grad):
    average = jnp.mean(matrix, axis=-1, keepdims=True)
    centered = matrix - average
    spread = jnp.mean(centered * centered, axis=-1, keepdims=True)
    inverse = lax.rsqrt(spread + epsilon)
    xhat = centered * inverse
    scaled = grad * factor
    mean_scaled = jnp.mean(scaled, axis=-1, keepdims=True)
    mean_product = jnp.mean(scaled * xhat, axis=-1, keepdims=True)
    grad_in = inverse * (scaled - mean_scaled - xhat * mean_product)
    return grad_in, jnp.sum(grad * xhat, axis=0), jnp.sum(grad, axis=0)


def gelu_tanh(inputs):
    cubed_vals = inputs * inputs * inputs
    return 0.5 * inputs * (1.0 + jnp.tanh(0.7978845608028654 * (inputs + 0.044715 * cubed_vals)))


def dot(left, right, left_dim, right_dim):
    return lax.dot_general(
        left, right, (((left_dim,), (right_dim,)), ((), ())), preferred_element_type=jnp.float32
    )


def head_masks(shape):
    lane = lax.broadcasted_iota(jnp.int32, shape, 1)
    return [(lane // HD) == head for head in range(shape[1] // HD)]


def attend_kernel(
    rows, drow, scale,
    tokens_ref, packs_ref, vectors_ref, bias_ref, seg_row_ref, seg_col_ref,
    normed_ref, qkv_ref, attended_ref, weight_ref, out_ref,
):
    length = tokens_ref.shape[0]
    part = attended_ref.shape[1]
    for owner in range(packs_ref.shape[0]):
        for kind in range(3):
            weight_ref[owner * drow : (owner + 1) * drow, kind * part : (kind + 1) * part] = (
                packs_ref[owner, kind * drow : (kind + 1) * drow, :]
            )
        for side in range(2):
            first = packs_ref.shape[1] - (2 - side) * drow
            out_ref[owner * drow : (owner + 1) * drow, side * part : (side + 1) * part] = (
                packs_ref[owner, first : first + drow, :]
            )
    masks = head_masks((rows, part))
    for block in range(length // rows):
        here = slice(block * rows, (block + 1) * rows)
        seen = (block + 1) * rows
        inputs = tokens_ref[here, :].astype(jnp.float32)
        centered = inputs - jnp.mean(inputs, axis=-1, keepdims=True)
        spread = jnp.mean(centered * centered, axis=-1, keepdims=True)
        normed = (
            centered * lax.rsqrt(spread + epsilon) * vectors_ref[0:1, :] + vectors_ref[1:2, :]
        ).astype(jnp.bfloat16)
        normed_ref[here, :] = normed
        projected = dot(normed, weight_ref[...], 1, 0) + bias_ref[...]
        qkv_ref[here, :] = projected.astype(jnp.bfloat16)
        queries = qkv_ref[here, :part]
        key_rows = qkv_ref[:seen, part : 2 * part]
        value_rows = qkv_ref[:seen, 2 * part :]
        query_index = block * rows + lax.broadcasted_iota(jnp.int32, (rows, seen), 0)
        key_index = lax.broadcasted_iota(jnp.int32, (rows, seen), 1)
        allowed = (seg_col_ref[here, :] == seg_row_ref[:, :seen]) & (key_index <= query_index)
        result = jnp.zeros((rows, part), jnp.float32)
        for mask in masks:
            scores = dot(jnp.where(mask, queries, 0), key_rows, 1, 1) * scale
            scores = jnp.where(allowed, scores, negative)
            weights = jnp.exp(scores - jnp.max(scores, axis=-1, keepdims=True))
            probs = weights * (1.0 / jnp.sum(weights, axis=-1, keepdims=True))
            result = jnp.where(mask, dot(probs.astype(jnp.bfloat16), value_rows, 1, 0), result)
        attended_ref[here, :] = result.astype(jnp.bfloat16)


def attend_back_kernel(
    rows, scale,
    qkv_ref, grad_ref, seg_row_ref, seg_col_ref,
    out_ref, sums_ref,
    key_sum, value_sum,
):
    length, part = grad_ref.shape
    masks = head_masks((rows, part))
    key_sum[...] = jnp.zeros_like(key_sum)
    value_sum[...] = jnp.zeros_like(value_sum)
    query_total = jnp.zeros((1, part), jnp.float32)
    for block in range(length // rows):
        here = slice(block * rows, (block + 1) * rows)
        seen = (block + 1) * rows
        queries = qkv_ref[here, :part]
        grads = grad_ref[here, :]
        key_rows = qkv_ref[:seen, part : 2 * part]
        value_rows = qkv_ref[:seen, 2 * part :]
        query_index = block * rows + lax.broadcasted_iota(jnp.int32, (seen, rows), 1)
        key_index = lax.broadcasted_iota(jnp.int32, (seen, rows), 0)
        allowed = (seg_col_ref[:seen, :] == seg_row_ref[:, here]) & (key_index <= query_index)
        grad_query = jnp.zeros((rows, part), jnp.float32)
        for mask in masks:
            head_queries = jnp.where(mask, queries, 0)
            head_grads = jnp.where(mask, grads, 0)
            scores = dot(key_rows, head_queries, 1, 1) * scale
            scores = jnp.where(allowed, scores, negative)
            weights = jnp.exp(scores - jnp.max(scores, axis=0, keepdims=True))
            probs = weights * (1.0 / jnp.sum(weights, axis=0, keepdims=True))
            value_sum[:seen, :] += dot(probs.astype(jnp.bfloat16), head_grads, 1, 0)
            grad_probs = dot(value_rows, head_grads, 1, 1)
            inner = jnp.sum(probs * grad_probs, axis=0, keepdims=True)
            grad_scores = (probs * (grad_probs - inner)).astype(jnp.bfloat16)
            key_sum[:seen, :] += dot(grad_scores, head_queries, 1, 0)
            grad_query = jnp.where(mask, dot(grad_scores, key_rows, 0, 0), grad_query)
        grad_query = (grad_query * scale).astype(jnp.bfloat16)
        out_ref[here, :part] = grad_query
        query_total += jnp.sum(grad_query.astype(jnp.float32), axis=0, keepdims=True)
    grad_values = value_sum[...].astype(jnp.bfloat16)
    out_ref[:, part : 2 * part] = (key_sum[...] * scale).astype(jnp.bfloat16)
    out_ref[:, 2 * part :] = grad_values
    sums_ref[0:1, :] = query_total
    sums_ref[1:2, :] = jnp.sum(grad_values.astype(jnp.float32), axis=0, keepdims=True)


def local(
    tokens,
    segments,
    w_qkv,
    b_qv,
    w_out,
    b_out,
    w_up,
    b_up,
    w_down,
    b_down,
    attngain,
    attnshift,
    mlpgain,
    mlpshift,
    cotangent,
):
    fsdp = lax.axis_size("fsdp")
    owners = fsdp * 2
    ctx_place = lax.axis_index("ctx")
    core_place = lax.axis_index("tp") % 2
    block_len, width = tokens.shape[1:]
    length = segments.shape[1]
    local_width = w_qkv.shape[2]
    part_width = local_width // 2
    part_heads = part_width // HD
    heads_local = local_width // HD
    drow = w_qkv.shape[0]
    hrow = b_qv.shape[2]
    score_scale = 1.0 / HD**0.5

    by_kind = jnp.transpose(w_qkv, (1, 0, 2))
    weight_rows = 3 * drow * part_width // LANES
    own_weight = lax.dynamic_slice_in_dim(by_kind, ctx_place * part_width, part_width, 2)
    sent_weight = lax.dynamic_slice_in_dim(by_kind, (1 - ctx_place) * part_width, part_width, 2)
    small_rows = 32
    up_rows = b_up.shape[0]
    qv_rows = b_qv.shape[0] * b_qv.shape[1]

    def padded(array, first):
        array = array.reshape(-1, array.shape[-1])
        rows, lanes = array.shape
        return jnp.pad(array, ((first, small_rows - first - rows), (0, LANES - lanes)))

    small = padded(b_up, 16) + padded(b_qv, 8)
    for place, vector in enumerate((attngain, attnshift, mlpgain, mlpshift, b_out, b_down)):
        small = small + padded(vector, place)
    out_turned = w_out.T
    small = jnp.concatenate([small, out_turned[:, :part_width], out_turned[:, part_width:]])
    own_pack = jnp.concatenate([own_weight.reshape(weight_rows, LANES), small])
    other_pack = swap(
        jnp.concatenate([sent_weight.reshape(weight_rows, LANES), small]), "ctx"
    )
    own_tokens, w_up, w_down, other_pack = lax.optimization_barrier(
        (tokens[0], w_up, w_down, other_pack)
    )
    half = block_len // 2
    all_tokens = both_tokens(own_tokens, ctx_place, core_place)

    part_hidden = w_up.shape[1] // 2
    own_ffn = jnp.concatenate([w_up, row_major(w_down.T)])
    sent_ffn = lax.dynamic_slice_in_dim(own_ffn, (1 - ctx_place) * part_hidden, part_hidden, 1)
    own_ffn = lax.dynamic_slice_in_dim(own_ffn, ctx_place * part_hidden, part_hidden, 1)
    ffn_pair = jnp.stack(ordered(ctx_place, own_ffn, swap(sent_ffn, "ctx")))
    ffn_pair, own_grad = lax.optimization_barrier((ffn_pair, cotangent[0]))
    all_grad = both_tokens(own_grad, ctx_place, core_place)

    both_packs = jnp.stack(ordered(ctx_place, own_pack, other_pack))
    packs = gather_fsdp(both_packs)
    packs, ffn_pair = lax.optimization_barrier((packs, ffn_pair))
    ffn_rows = gather_rows(ffn_pair.reshape(-1, part_hidden)).reshape(
        owners, 2, drow, part_hidden
    )
    up_full = ffn_rows[:, 0].reshape(width, part_hidden)
    down_full = ffn_rows[:, 1].reshape(width, part_hidden)
    packs = packs.reshape(owners, -1, LANES)
    smalls = packs[:, weight_rows : weight_rows + small_rows].astype(jnp.float32)
    vectors = smalls[:, :8, :drow].transpose(1, 0, 2).reshape(8, width)
    gain_one, shift_one, gain_two, shift_two, out_bias, down_bias = (vectors[i] for i in range(6))
    up_bias = smalls[:, 16 : 16 + up_rows, :hrow].transpose(1, 0, 2).reshape(-1)
    qv_bias = (
        smalls[:, 8 : 8 + qv_rows, :hrow].transpose(1, 0, 2).reshape(2, local_width)
    )
    qv_bias_part = lax.dynamic_slice_in_dim(qv_bias, ctx_place * part_width, part_width, 1)
    qkv_bias = jnp.concatenate(
        [qv_bias_part[0], jnp.zeros((part_width,), jnp.float32), qv_bias_part[1]]
    )[None]

    seg_row = segments
    seg_col = segments.reshape(length, 1)
    rows = min(256, length)
    normed_all, qkv_rows, attended_part, qkv_part, out_full = pl.pallas_call(
        functools.partial(attend_kernel, rows, drow, score_scale),
        out_shape=(
            jax.ShapeDtypeStruct((length, width), jnp.bfloat16),
            jax.ShapeDtypeStruct((length, 3 * part_width), jnp.bfloat16),
            jax.ShapeDtypeStruct((length, part_width), jnp.bfloat16),
            jax.ShapeDtypeStruct((width, 3 * part_width), jnp.bfloat16),
            jax.ShapeDtypeStruct((width, local_width), jnp.bfloat16),
        ),
        compiler_params=pltpu.CompilerParams(vmem_limit_bytes=VMEM_LIMIT),
        cost_estimate=pl.CostEstimate(
            flops=2 * length * width * 3 * part_width, bytes_accessed=8 * length * width,
            transcendentals=length * length,
        ),
    )(all_tokens, packs, vectors, qkv_bias, seg_row, seg_col)

    def to_tokens(array):
        kept = lax.dynamic_slice_in_dim(array, ctx_place * block_len, block_len, 0)
        sent = swap(
            lax.dynamic_slice_in_dim(array, (1 - ctx_place) * block_len, block_len, 0), "ctx"
        )
        return ordered(ctx_place, kept, sent)

    attended = jnp.concatenate(to_tokens(attended_part), axis=1)
    inputs = own_tokens.astype(jnp.float32)

    def out_part(start, count):
        return dot(lax.dynamic_slice_in_dim(attended, start, count, 0), out_full, 1, 1)

    attn_sum, unused, unused = sum_tp(out_part, block_len, core_place)
    middle = inputs + (attn_sum.astype(jnp.float32) + out_bias)
    normed_two = normalize(middle, gain_two, shift_two).astype(jnp.bfloat16)
    normed_pair = both_tokens(normed_two, ctx_place, core_place)
    up_bias_part = lax.dynamic_slice_in_dim(up_bias, ctx_place * part_hidden, part_hidden, 0)
    hidden_pre = dot(normed_pair, up_full, 1, 0) + up_bias_part
    activated = gelu_tanh(hidden_pre).astype(jnp.bfloat16)
    grad_activated = dot(all_grad, down_full, 1, 0)
    value, gelu_pull = jax.vjp(gelu_tanh, hidden_pre)
    grad_hidden_low = gelu_pull(grad_activated)[0].astype(jnp.bfloat16)

    up_kept, up_sent = ordered(ctx_place, *chip_part(grad_hidden_low, up_full, core_place))
    up_sent, late_grad, late_normed, late_hidden, late_activated = lax.optimization_barrier(
        (up_sent, all_grad, normed_pair, grad_hidden_low, activated)
    )
    up_got = swap(up_sent, "ctx")
    down_product = dot(late_grad, late_activated, 0, 0).astype(jnp.bfloat16)
    up_product = dot(late_normed, late_hidden, 0, 0).astype(jnp.bfloat16)
    up_got, down_product, up_product, late_hidden, late_activated = lax.optimization_barrier(
        (up_got, down_product, up_product, late_hidden, late_activated)
    )
    down_rows = row_major(scatter_rows(down_product))
    up_rows_sum = row_major(scatter_rows(up_product))
    up_pair = pair_sum(up_kept, up_got)
    up_pair, late_hidden, late_activated = lax.optimization_barrier(
        (up_pair, late_hidden, late_activated)
    )
    up_across = swap(up_pair, "tp", CHIP)
    mlp_kept, mlp_sent = ordered(ctx_place, *chip_part(late_activated, down_full, core_place))
    mlp_got = swap(mlp_sent, "ctx")
    grad_up_bias = jnp.sum(late_hidden.astype(jnp.float32), axis=0)
    up_across, mlp_kept, mlp_sent, grad_up_bias = lax.optimization_barrier(
        (up_across, mlp_kept, mlp_sent, grad_up_bias)
    )
    up_total = pair_sum(up_pair, up_across)
    grad_normed_two = jnp.concatenate(
        ordered(core_place, up_total, swap(up_total, "tp", CORE))
    ).astype(jnp.float32)
    grad_out = own_grad.astype(jnp.float32)
    grad_down_bias = jnp.sum(grad_out, axis=0)
    grad_middle_norm, grad_gain_two, grad_shift_two = normalize_back(
        middle, gain_two, grad_normed_two
    )
    grad_middle = grad_out + grad_middle_norm
    grad_branch_low = grad_middle.astype(jnp.bfloat16)
    grad_out_bias = jnp.sum(grad_branch_low.astype(jnp.float32), axis=0)
    grad_attended_low = dot(grad_branch_low, out_full, 1, 0).astype(jnp.bfloat16)
    own_cols = lax.dynamic_slice_in_dim(grad_attended_low, ctx_place * part_width, part_width, 1)
    sent_cols = lax.dynamic_slice_in_dim(
        grad_attended_low, (1 - ctx_place) * part_width, part_width, 1
    )
    sent_cols, late_branch, mlp_got, mlp_kept = lax.optimization_barrier(
        (sent_cols, grad_branch_low, mlp_got, mlp_kept)
    )
    got_cols = swap(sent_cols, "ctx")
    mlp_pair = pair_sum(mlp_kept, mlp_got)
    mlp_across = swap(mlp_pair, "tp", CHIP)
    kept_out, sent_out = weight_product(late_branch, attended, ctx_place)
    got_cols, sent_out, mlp_pair = lax.optimization_barrier((got_cols, sent_out, mlp_pair))
    grad_heads = jnp.concatenate(ordered(ctx_place, own_cols, got_cols))
    grad_qkv_part, bias_sums = pl.pallas_call(
        functools.partial(attend_back_kernel, rows, score_scale),
        out_shape=(
            jax.ShapeDtypeStruct((length, 3 * part_width), jnp.bfloat16),
            jax.ShapeDtypeStruct((2, part_width), jnp.float32),
        ),
        scratch_shapes=[
            pltpu.VMEM((length, part_width), jnp.float32),
            pltpu.VMEM((length, part_width), jnp.float32),
        ],
        compiler_params=pltpu.CompilerParams(vmem_limit_bytes=VMEM_LIMIT),
        cost_estimate=pl.CostEstimate(
            flops=10 * length * length * part_width, bytes_accessed=2 * length * width,
            transcendentals=length * length,
        ),
    )(qkv_rows, grad_heads, seg_row, seg_col)
    grad_qkv_kept = lax.dynamic_slice_in_dim(grad_qkv_part, ctx_place * block_len, block_len, 0)
    grad_qkv_sent = lax.dynamic_slice_in_dim(
        grad_qkv_part, (1 - ctx_place) * block_len, block_len, 0
    )
    grad_qkv_sent, late_part, sent_out, mlp_across, mlp_pair = lax.optimization_barrier(
        (grad_qkv_sent, grad_qkv_part, sent_out, mlp_across, mlp_pair)
    )
    grad_qkv_got = swap(grad_qkv_sent, "ctx")
    grad_qkv_weight = dot(normed_all, late_part, 0, 0).astype(jnp.bfloat16)
    mlp_total = pair_sum(mlp_pair, mlp_across)
    mlp_sum = jnp.concatenate(ordered(core_place, mlp_total, swap(mlp_total, "tp", CORE)))
    finished = middle + (mlp_sum.astype(jnp.float32) + down_bias)
    grad_qkv_weight, sent_out = lax.optimization_barrier((grad_qkv_weight, sent_out))
    got_out = swap(sent_out, "ctx")
    grad_qkv_got, grad_qkv_weight, finished = lax.optimization_barrier(
        (grad_qkv_got, grad_qkv_weight, finished)
    )
    grad_qkv_first, grad_qkv_second = ordered(ctx_place, grad_qkv_kept, grad_qkv_got)
    grad_qkv_sum = jnp.sum(
        lax.all_to_all(
            grad_qkv_weight.reshape(fsdp, 2 * drow, 3 * part_width), "fsdp", 0, 0, tiled=True
        ).astype(jnp.float32),
        axis=0,
    )
    own_rows = lax.dynamic_slice_in_dim(grad_qkv_sum, ctx_place * drow, drow, 0)
    sent_rows = swap(
        lax.dynamic_slice_in_dim(grad_qkv_sum, (1 - ctx_place) * drow, drow, 0).astype(
            jnp.bfloat16
        ),
        "ctx",
    ).astype(jnp.float32)
    grad_qkv_out = jnp.concatenate(
        [
            part.reshape(drow, 3, part_width)
            for part in ordered(ctx_place, own_rows, sent_rows)
        ],
        axis=2,
    )
    nothing = jnp.zeros_like(bias_sums)
    grad_qv_bias = jnp.concatenate(ordered(ctx_place, bias_sums, nothing), axis=1)

    qkv_other = swap(qkv_part, "ctx")
    qkv_first, qkv_second = ordered(ctx_place, qkv_part, qkv_other)

    def first_part(start, count):
        return dot(
            lax.dynamic_slice_in_dim(grad_qkv_first, start, count, 0), qkv_first, 1, 1
        ) + dot(lax.dynamic_slice_in_dim(grad_qkv_second, start, count, 0), qkv_second, 1, 1)

    def by_owner(vector):
        return vector.reshape(owners, 1, drow)

    def row_block(array, first):
        rows, lanes = array.shape[1:]
        return jnp.pad(
            array, ((0, 0), (first, small_rows - first - rows), (0, LANES - lanes))
        )

    def small_work(gated, chip_sum):
        kept_out, got_out, up_rows_sum, down_rows = gated
        ffn_rows = jnp.stack([up_rows_sum, down_rows]).reshape(2, 2, drow, part_hidden)
        ffn_kept, ffn_sent = ordered(ctx_place, ffn_rows[:, 0], ffn_rows[:, 1])
        ffn_got = swap(ffn_sent, "ctx")
        half_inputs = lax.dynamic_slice_in_dim(inputs, core_place * half, half, 0)
        half_grad = chip_sum.astype(jnp.float32)
        unused, gain_share, shift_share = normalize_back(half_inputs, gain_one, half_grad)
        up_bias_rows = grad_up_bias.reshape(up_rows // 2, HD)
        up_bias_rows = jnp.concatenate(
            ordered(ctx_place, up_bias_rows, jnp.zeros_like(up_bias_rows))
        )
        small_grads = row_block(
            up_bias_rows.reshape(up_rows, owners, hrow).transpose(1, 0, 2), 16
        ) + row_block(grad_qv_bias.reshape(qv_rows, owners, hrow).transpose(1, 0, 2), 8)
        for place, vector in enumerate(
            (
                gain_share,
                shift_share,
                grad_gain_two,
                grad_shift_two,
                grad_out_bias,
                grad_down_bias,
            )
        ):
            small_grads = small_grads + row_block(by_owner(vector), place)
        return (small_grads, pair_sum(kept_out, got_out), ffn_kept), ffn_got

    first_sum, (small_grads, out_pairs, ffn_kept), ffn_got = sum_tp(
        first_part,
        block_len,
        core_place,
        small_work,
        (kept_out, got_out, up_rows_sum, down_rows),
    )
    grad_up, grad_down = jnp.concatenate(ordered(ctx_place, ffn_kept, ffn_got), axis=2)
    grad_out_weight = row_major(scatter_rows(out_pairs))
    grad_inputs_norm, unused, unused = normalize_back(
        inputs, gain_one, first_sum.astype(jnp.float32)
    )
    grad_inputs = grad_middle + grad_inputs_norm
    small_sums = jnp.sum(
        lax.all_to_all(small_grads, ("fsdp", "ctx"), 0, 0, tiled=True), axis=0
    )
    share = small_sums[:2]
    share = share + swap(share, "tp", CORE)
    share = share + swap(share, "tp", CHIP)
    gain_one_sum, shift_one_sum = share[0, :drow], share[1, :drow]
    vector_sums = small_sums[:8, :drow]
    up_bias_sum = small_sums[16 : 16 + up_rows, :hrow]
    qv_bias_sum = small_sums[8 : 8 + qv_rows, :hrow].reshape(2, heads_local, hrow)

    return (
        finished.astype(jnp.bfloat16)[None],
        grad_inputs[None],
        grad_qkv_out,
        qv_bias_sum,
        grad_out_weight.T.astype(jnp.float32),
        vector_sums[4],
        grad_up.astype(jnp.float32),
        up_bias_sum,
        grad_down.T.astype(jnp.float32),
        vector_sums[5],
        gain_one_sum,
        shift_one_sum,
        vector_sums[2],
        vector_sums[3],
    )


def solution(mesh):
    placed = (
        P("fsdp", "ctx", None),
        P("fsdp", None),
        P(("fsdp", "ctx"), None, "tp"),
        P(None, "tp", ("fsdp", "ctx")),
        P("tp", ("fsdp", "ctx")),
        P(("fsdp", "ctx")),
        P(("fsdp", "ctx"), "tp"),
        P("tp", ("fsdp", "ctx")),
        P("tp", ("fsdp", "ctx")),
        P(("fsdp", "ctx")),
        P(("fsdp", "ctx")),
        P(("fsdp", "ctx")),
        P(("fsdp", "ctx")),
        P(("fsdp", "ctx")),
        P("fsdp", "ctx", None),
    )
    return jax.shard_map(
        local,
        mesh=mesh,
        in_specs=placed,
        out_specs=(
            P("fsdp", "ctx", None),
            P("fsdp", "ctx", None),
            P(("fsdp", "ctx"), None, "tp"),
            P(None, "tp", ("fsdp", "ctx")),
            P("tp", ("fsdp", "ctx")),
            P(("fsdp", "ctx")),
            P(("fsdp", "ctx"), "tp"),
            P("tp", ("fsdp", "ctx")),
            P("tp", ("fsdp", "ctx")),
            P(("fsdp", "ctx")),
            P(("fsdp", "ctx")),
            P(("fsdp", "ctx")),
            P(("fsdp", "ctx")),
            P(("fsdp", "ctx")),
        ),
        check_vma=False,
    )
```

```python
import functools

import jax
import jax.numpy as jnp
from jax import lax
from jax.experimental import pallas as pl
from jax.experimental.layout import Layout, with_layout_constraint
from jax.experimental.pallas import tpu as pltpu
from jax.sharding import PartitionSpec as P

HD = 64
LANES = 128
CORE = 1
CHIP = 2
VMEM_LIMIT = 16 * 1024 * 1024

epsilon = 1e-05
negative = -1e30


def swap(array, axis, mask=1):
    devices = lax.axis_size(axis)
    return lax.ppermute(array, axis, [(i, i ^ mask) for i in range(devices)])


def ordered(place, own, other):
    return jnp.where(place == 0, own, other), jnp.where(place == 0, other, own)


def gather_fsdp(block):
    devices = lax.axis_size("fsdp")
    return lax.all_to_all(
        jnp.broadcast_to(block[None], (devices,) + block.shape), "fsdp", 0, 0, tiled=True
    )


def gather_rows(block):
    return lax.all_gather(block, "fsdp", axis=0, tiled=True)


def row_major(array):
    return with_layout_constraint(array, Layout(tuple(range(array.ndim))))


def sum_tp(part_of, rows, core_place, work=None, gated=()):
    half = rows // 2
    sent = swap(part_of((1 - core_place) * half, half).astype(jnp.bfloat16), "tp", CORE)
    kept = part_of(core_place * half, half)
    chip_sum = (kept + sent.astype(jnp.float32)).astype(jnp.bfloat16)
    chip_sum, gated = lax.optimization_barrier((chip_sum, gated))
    across = swap(chip_sum, "tp", CHIP)
    done, free = work(gated, chip_sum) if work else ((), ())
    across, done = lax.optimization_barrier((across, done))
    total = (chip_sum.astype(jnp.float32) + across.astype(jnp.float32)).astype(jnp.bfloat16)
    summed = jnp.concatenate(ordered(core_place, total, swap(total, "tp", CORE)), axis=0)
    return summed, done, free


def other_tokens(rows, core_place):
    half = rows.shape[0] // 2
    got = swap(lax.dynamic_slice_in_dim(rows, core_place * half, half, 0), "ctx")
    return got, swap(got, "tp", CORE)


def chip_parts(own, other, right, core_place):
    half = own.shape[0] // 2

    def summed(sent, kept):
        sent = swap(dot(sent, right, 1, 1).astype(jnp.bfloat16), "tp", CORE)
        return (dot(kept, right, 1, 1) + sent.astype(jnp.float32)).astype(jnp.bfloat16)

    return (
        summed(
            lax.dynamic_slice_in_dim(own, (1 - core_place) * half, half, 0),
            lax.dynamic_slice_in_dim(own, core_place * half, half, 0),
        ),
        summed(other[half:], other[:half]),
    )


def weight_product(wide, narrow, ctx_place):
    devices = lax.axis_size("fsdp")
    rows = wide.shape[1] // (devices * 2)
    product = dot(wide, narrow, 0, 0).astype(jnp.bfloat16).reshape(devices, 2, rows, -1)
    return tuple(
        part.reshape(devices * rows, -1)
        for part in ordered(ctx_place, product[:, 0], product[:, 1])
    )


def pair_sum(kept, sent):
    return (kept.astype(jnp.float32) + sent.astype(jnp.float32)).astype(jnp.bfloat16)


def scatter_rows(array):
    return lax.psum_scatter(array, "fsdp", scatter_dimension=0, tiled=True)


def normalize(matrix, factor, offset):
    average = jnp.mean(matrix, axis=-1, keepdims=True)
    centered = matrix - average
    spread = jnp.mean(centered * centered, axis=-1, keepdims=True)
    return centered * lax.rsqrt(spread + epsilon) * factor + offset


def normalize_back(matrix, factor, grad):
    average = jnp.mean(matrix, axis=-1, keepdims=True)
    centered = matrix - average
    spread = jnp.mean(centered * centered, axis=-1, keepdims=True)
    inverse = lax.rsqrt(spread + epsilon)
    xhat = centered * inverse
    scaled = grad * factor
    mean_scaled = jnp.mean(scaled, axis=-1, keepdims=True)
    mean_product = jnp.mean(scaled * xhat, axis=-1, keepdims=True)
    grad_in = inverse * (scaled - mean_scaled - xhat * mean_product)
    return grad_in, jnp.sum(grad * xhat, axis=0), jnp.sum(grad, axis=0)


def gelu_tanh(inputs):
    cubed_vals = inputs * inputs * inputs
    return 0.5 * inputs * (1.0 + jnp.tanh(0.7978845608028654 * (inputs + 0.044715 * cubed_vals)))


def dot(left, right, left_dim, right_dim):
    return lax.dot_general(
        left, right, (((left_dim,), (right_dim,)), ((), ())), preferred_element_type=jnp.float32
    )


def head_masks(shape):
    lane = lax.broadcasted_iota(jnp.int32, shape, 1)
    return [(lane // HD) == head for head in range(shape[1] // HD)]


def attend_kernel(
    rows, drow, scale,
    tokens_ref, packs_ref, vectors_ref, bias_ref, seg_row_ref, seg_col_ref,
    normed_ref, qkv_ref, attended_ref, weight_ref, out_ref,
):
    length = tokens_ref.shape[0]
    part = attended_ref.shape[1]
    for owner in range(packs_ref.shape[0]):
        for kind in range(3):
            weight_ref[owner * drow : (owner + 1) * drow, kind * part : (kind + 1) * part] = (
                packs_ref[owner, kind * drow : (kind + 1) * drow, :]
            )
        for side in range(2):
            first = packs_ref.shape[1] - (2 - side) * drow
            out_ref[owner * drow : (owner + 1) * drow, side * part : (side + 1) * part] = (
                packs_ref[owner, first : first + drow, :]
            )
    masks = head_masks((rows, part))
    for block in range(length // rows):
        here = slice(block * rows, (block + 1) * rows)
        seen = (block + 1) * rows
        inputs = tokens_ref[here, :].astype(jnp.float32)
        centered = inputs - jnp.mean(inputs, axis=-1, keepdims=True)
        spread = jnp.mean(centered * centered, axis=-1, keepdims=True)
        normed = (
            centered * lax.rsqrt(spread + epsilon) * vectors_ref[0:1, :] + vectors_ref[1:2, :]
        ).astype(jnp.bfloat16)
        normed_ref[here, :] = normed
        projected = dot(normed, weight_ref[...], 1, 0) + bias_ref[...]
        qkv_ref[here, :] = projected.astype(jnp.bfloat16)
        queries = qkv_ref[here, :part]
        key_rows = qkv_ref[:seen, part : 2 * part]
        value_rows = qkv_ref[:seen, 2 * part :]
        query_index = block * rows + lax.broadcasted_iota(jnp.int32, (rows, seen), 0)
        key_index = lax.broadcasted_iota(jnp.int32, (rows, seen), 1)
        allowed = (seg_col_ref[here, :] == seg_row_ref[:, :seen]) & (key_index <= query_index)
        result = jnp.zeros((rows, part), jnp.float32)
        for mask in masks:
            scores = dot(jnp.where(mask, queries, 0), key_rows, 1, 1) * scale
            scores = jnp.where(allowed, scores, negative)
            weights = jnp.exp(scores - jnp.max(scores, axis=-1, keepdims=True))
            probs = weights * (1.0 / jnp.sum(weights, axis=-1, keepdims=True))
            result = jnp.where(mask, dot(probs.astype(jnp.bfloat16), value_rows, 1, 0), result)
        attended_ref[here, :] = result.astype(jnp.bfloat16)


def attend_back_kernel(
    rows, scale,
    qkv_ref, grad_ref, seg_row_ref, seg_col_ref,
    out_ref, sums_ref,
    key_sum, value_sum,
):
    length, part = grad_ref.shape
    masks = head_masks((rows, part))
    key_sum[...] = jnp.zeros_like(key_sum)
    value_sum[...] = jnp.zeros_like(value_sum)
    query_total = jnp.zeros((1, part), jnp.float32)
    for block in range(length // rows):
        here = slice(block * rows, (block + 1) * rows)
        seen = (block + 1) * rows
        queries = qkv_ref[here, :part]
        grads = grad_ref[here, :]
        key_rows = qkv_ref[:seen, part : 2 * part]
        value_rows = qkv_ref[:seen, 2 * part :]
        query_index = block * rows + lax.broadcasted_iota(jnp.int32, (seen, rows), 1)
        key_index = lax.broadcasted_iota(jnp.int32, (seen, rows), 0)
        allowed = (seg_col_ref[:seen, :] == seg_row_ref[:, here]) & (key_index <= query_index)
        grad_query = jnp.zeros((rows, part), jnp.float32)
        for mask in masks:
            head_queries = jnp.where(mask, queries, 0)
            head_grads = jnp.where(mask, grads, 0)
            scores = dot(key_rows, head_queries, 1, 1) * scale
            scores = jnp.where(allowed, scores, negative)
            weights = jnp.exp(scores - jnp.max(scores, axis=0, keepdims=True))
            probs = weights * (1.0 / jnp.sum(weights, axis=0, keepdims=True))
            value_sum[:seen, :] += dot(probs.astype(jnp.bfloat16), head_grads, 1, 0)
            grad_probs = dot(value_rows, head_grads, 1, 1)
            inner = jnp.sum(probs * grad_probs, axis=0, keepdims=True)
            grad_scores = (probs * (grad_probs - inner)).astype(jnp.bfloat16)
            key_sum[:seen, :] += dot(grad_scores, head_queries, 1, 0)
            grad_query = jnp.where(mask, dot(grad_scores, key_rows, 0, 0), grad_query)
        grad_query = (grad_query * scale).astype(jnp.bfloat16)
        out_ref[here, :part] = grad_query
        query_total += jnp.sum(grad_query.astype(jnp.float32), axis=0, keepdims=True)
    grad_values = value_sum[...].astype(jnp.bfloat16)
    out_ref[:, part : 2 * part] = (key_sum[...] * scale).astype(jnp.bfloat16)
    out_ref[:, 2 * part :] = grad_values
    sums_ref[0:1, :] = query_total
    sums_ref[1:2, :] = jnp.sum(grad_values.astype(jnp.float32), axis=0, keepdims=True)


def local(
    tokens,
    segments,
    w_qkv,
    b_qv,
    w_out,
    b_out,
    w_up,
    b_up,
    w_down,
    b_down,
    attngain,
    attnshift,
    mlpgain,
    mlpshift,
    cotangent,
):
    fsdp = lax.axis_size("fsdp")
    owners = fsdp * 2
    ctx_place = lax.axis_index("ctx")
    core_place = lax.axis_index("tp") % 2
    block_len, width = tokens.shape[1:]
    length = segments.shape[1]
    local_width = w_qkv.shape[2]
    part_width = local_width // 2
    part_heads = part_width // HD
    heads_local = local_width // HD
    drow = w_qkv.shape[0]
    hrow = b_qv.shape[2]
    score_scale = 1.0 / HD**0.5

    by_kind = jnp.transpose(w_qkv, (1, 0, 2))
    weight_rows = 3 * drow * part_width // LANES
    own_weight = lax.dynamic_slice_in_dim(by_kind, ctx_place * part_width, part_width, 2)
    sent_weight = lax.dynamic_slice_in_dim(by_kind, (1 - ctx_place) * part_width, part_width, 2)
    small_rows = 32
    up_rows = b_up.shape[0]
    qv_rows = b_qv.shape[0] * b_qv.shape[1]

    def padded(array, first):
        array = array.reshape(-1, array.shape[-1])
        rows, lanes = array.shape
        return jnp.pad(array, ((first, small_rows - first - rows), (0, LANES - lanes)))

    small = padded(b_up, 16) + padded(b_qv, 8)
    for place, vector in enumerate((attngain, attnshift, mlpgain, mlpshift, b_out, b_down)):
        small = small + padded(vector, place)
    out_turned = w_out.T
    small = jnp.concatenate([small, out_turned[:, :part_width], out_turned[:, part_width:]])
    own_pack = jnp.concatenate([own_weight.reshape(weight_rows, LANES), small])
    other_pack = swap(
        jnp.concatenate([sent_weight.reshape(weight_rows, LANES), small]), "ctx"
    )
    own_tokens, w_up, w_down, other_pack = lax.optimization_barrier(
        (tokens[0], w_up, w_down, other_pack)
    )
    half = block_len // 2
    other_block = jnp.concatenate(ordered(core_place, *other_tokens(own_tokens, core_place)))
    all_tokens = jnp.concatenate(ordered(ctx_place, own_tokens, other_block))

    part_hidden = w_up.shape[1] // 2
    own_ffn = jnp.concatenate([w_up, row_major(w_down.T)])
    sent_ffn = lax.dynamic_slice_in_dim(own_ffn, (1 - ctx_place) * part_hidden, part_hidden, 1)
    own_ffn = lax.dynamic_slice_in_dim(own_ffn, ctx_place * part_hidden, part_hidden, 1)
    ffn_pair = jnp.stack(ordered(ctx_place, own_ffn, swap(sent_ffn, "ctx")))
    ffn_pair, own_grad = lax.optimization_barrier((ffn_pair, cotangent[0]))
    other_grad = jnp.concatenate(other_tokens(own_grad, core_place))

    both_packs = jnp.stack(ordered(ctx_place, own_pack, other_pack))
    packs = gather_fsdp(both_packs)
    packs, ffn_pair = lax.optimization_barrier((packs, ffn_pair))
    up_full = gather_rows(ffn_pair[:, :drow].reshape(-1, part_hidden))
    down_full = gather_rows(ffn_pair[:, drow:].reshape(-1, part_hidden))
    packs = packs.reshape(owners, -1, LANES)
    smalls = packs[:, weight_rows : weight_rows + small_rows].astype(jnp.float32)
    first_vectors = smalls[:, :8, :drow].transpose(1, 0, 2).reshape(8, width)
    qv_bias = (
        smalls[:, 8 : 8 + qv_rows, :hrow].transpose(1, 0, 2).reshape(2, local_width)
    )
    qv_bias_part = lax.dynamic_slice_in_dim(qv_bias, ctx_place * part_width, part_width, 1)
    qkv_bias = jnp.concatenate(
        [qv_bias_part[0], jnp.zeros((part_width,), jnp.float32), qv_bias_part[1]]
    )[None]

    seg_row = segments
    seg_col = segments.reshape(length, 1)
    rows = min(256, length)
    normed_all, qkv_rows, attended_part, qkv_part, out_full = pl.pallas_call(
        functools.partial(attend_kernel, rows, drow, score_scale),
        out_shape=(
            jax.ShapeDtypeStruct((length, width), jnp.bfloat16),
            jax.ShapeDtypeStruct((length, 3 * part_width), jnp.bfloat16),
            jax.ShapeDtypeStruct((length, part_width), jnp.bfloat16),
            jax.ShapeDtypeStruct((width, 3 * part_width), jnp.bfloat16),
            jax.ShapeDtypeStruct((width, local_width), jnp.bfloat16),
        ),
        compiler_params=pltpu.CompilerParams(vmem_limit_bytes=VMEM_LIMIT),
        cost_estimate=pl.CostEstimate(
            flops=2 * length * width * 3 * part_width, bytes_accessed=8 * length * width,
            transcendentals=length * length,
        ),
    )(all_tokens, packs, first_vectors, qkv_bias, seg_row, seg_col)

    def to_tokens(array):
        kept = lax.dynamic_slice_in_dim(array, ctx_place * block_len, block_len, 0)
        sent = swap(
            lax.dynamic_slice_in_dim(array, (1 - ctx_place) * block_len, block_len, 0), "ctx"
        )
        return ordered(ctx_place, kept, sent)

    attended = jnp.concatenate(to_tokens(attended_part), axis=1)
    inputs = own_tokens.astype(jnp.float32)

    def out_part(start, count):
        return dot(lax.dynamic_slice_in_dim(attended, start, count, 0), out_full, 1, 1)

    def small_vectors(gated, unused):
        vectors = gated[:, :8, :drow].transpose(1, 0, 2).reshape(8, width)
        up_bias = lax.dynamic_slice_in_dim(
            gated[:, 16 : 16 + up_rows, :hrow], ctx_place * (up_rows // 2), up_rows // 2, 1
        )
        return (vectors, up_bias.transpose(1, 0, 2).reshape(1, -1)), ()

    attn_sum, (vectors, up_bias_part), unused = sum_tp(
        out_part, block_len, core_place, small_vectors, smalls
    )
    gain_one, shift_one, gain_two, shift_two, out_bias, down_bias = (vectors[i] for i in range(6))
    middle = inputs + (attn_sum.astype(jnp.float32) + out_bias)
    normed_two = normalize(middle, gain_two, shift_two).astype(jnp.bfloat16)
    def hidden(rows):
        return dot(rows, up_full, 1, 0) + up_bias_part

    def hidden_grad(pre, grads):
        grad_activated = dot(grads, down_full, 1, 0)
        value, gelu_pull = jax.vjp(gelu_tanh, pre)
        return gelu_pull(grad_activated)[0].astype(jnp.bfloat16)

    half_rows = lax.dynamic_slice_in_dim(normed_two, core_place * half, half, 0)
    half_rows, late_normed = lax.optimization_barrier((half_rows, normed_two))
    got = swap(half_rows, "ctx")
    own_pre = hidden(late_normed)
    own_active = gelu_tanh(own_pre).astype(jnp.bfloat16)
    got, own_pre, own_active, qkv_part = lax.optimization_barrier(
        (got, own_pre, own_active, qkv_part)
    )
    qkv_other = swap(qkv_part, "ctx")
    other_normed = jnp.concatenate([got, swap(got, "tp", CORE)])
    own_hidden = hidden_grad(own_pre, own_grad)
    other_pre = hidden(other_normed)
    other_active = gelu_tanh(other_pre).astype(jnp.bfloat16)
    other_hidden = hidden_grad(other_pre, other_grad)

    up_kept, up_sent = chip_parts(own_hidden, other_hidden, up_full, core_place)
    up_sent, qkv_other, own_active, other_active, own_hidden, other_hidden = (
        lax.optimization_barrier(
            (up_sent, qkv_other, own_active, other_active, own_hidden, other_hidden)
        )
    )
    up_got = swap(up_sent, "ctx")
    down_product = (
        dot(own_grad, own_active, 0, 0) + dot(other_grad, other_active, 0, 0)
    ).astype(jnp.bfloat16)
    up_product = (
        dot(normed_two, own_hidden, 0, 0) + dot(other_normed, other_hidden, 0, 0)
    ).astype(jnp.bfloat16)
    mlp_kept, mlp_sent = chip_parts(own_active, other_active, down_full, core_place)
    up_got, down_product, up_product, mlp_kept, mlp_sent = lax.optimization_barrier(
        (up_got, down_product, up_product, mlp_kept, mlp_sent)
    )
    down_rows = row_major(scatter_rows(down_product))
    up_rows_sum = row_major(scatter_rows(up_product))
    up_pair = pair_sum(up_kept, up_got)
    up_pair, mlp_sent, own_hidden, other_hidden, own_grad = lax.optimization_barrier(
        (up_pair, mlp_sent, own_hidden, other_hidden, own_grad)
    )
    up_across = swap(up_pair, "tp", CHIP)
    mlp_got = swap(mlp_sent, "ctx")
    grad_up_bias = jnp.sum(own_hidden.astype(jnp.float32), axis=0) + jnp.sum(
        other_hidden.astype(jnp.float32), axis=0
    )
    grad_down_bias = jnp.sum(own_grad.astype(jnp.float32), axis=0)
    up_across, mlp_got, grad_up_bias, grad_down_bias = lax.optimization_barrier(
        (up_across, mlp_got, grad_up_bias, grad_down_bias)
    )
    up_total = pair_sum(up_pair, up_across)
    grad_normed_two = jnp.concatenate(
        ordered(core_place, up_total, swap(up_total, "tp", CORE))
    ).astype(jnp.float32)
    grad_out = own_grad.astype(jnp.float32)
    grad_middle_norm, grad_gain_two, grad_shift_two = normalize_back(
        middle, gain_two, grad_normed_two
    )
    grad_middle = grad_out + grad_middle_norm
    grad_branch_low = grad_middle.astype(jnp.bfloat16)
    grad_out_bias = jnp.sum(grad_branch_low.astype(jnp.float32), axis=0)
    grad_attended_low = dot(grad_branch_low, out_full, 1, 0).astype(jnp.bfloat16)
    own_cols = lax.dynamic_slice_in_dim(grad_attended_low, ctx_place * part_width, part_width, 1)
    sent_cols = lax.dynamic_slice_in_dim(
        grad_attended_low, (1 - ctx_place) * part_width, part_width, 1
    )
    sent_cols, late_branch, mlp_got, mlp_kept = lax.optimization_barrier(
        (sent_cols, grad_branch_low, mlp_got, mlp_kept)
    )
    got_cols = swap(sent_cols, "ctx")
    mlp_pair = pair_sum(mlp_kept, mlp_got)
    mlp_across = swap(mlp_pair, "tp", CHIP)
    kept_out, sent_out = weight_product(late_branch, attended, ctx_place)
    got_cols, sent_out, mlp_pair = lax.optimization_barrier((got_cols, sent_out, mlp_pair))
    grad_heads = jnp.concatenate(ordered(ctx_place, own_cols, got_cols))
    grad_qkv_part, bias_sums = pl.pallas_call(
        functools.partial(attend_back_kernel, rows, score_scale),
        out_shape=(
            jax.ShapeDtypeStruct((length, 3 * part_width), jnp.bfloat16),
            jax.ShapeDtypeStruct((2, part_width), jnp.float32),
        ),
        scratch_shapes=[
            pltpu.VMEM((length, part_width), jnp.float32),
            pltpu.VMEM((length, part_width), jnp.float32),
        ],
        compiler_params=pltpu.CompilerParams(vmem_limit_bytes=VMEM_LIMIT),
        cost_estimate=pl.CostEstimate(
            flops=10 * length * length * part_width, bytes_accessed=2 * length * width,
            transcendentals=length * length,
        ),
    )(qkv_rows, grad_heads, seg_row, seg_col)
    grad_qkv_kept = lax.dynamic_slice_in_dim(grad_qkv_part, ctx_place * block_len, block_len, 0)
    grad_qkv_sent = lax.dynamic_slice_in_dim(
        grad_qkv_part, (1 - ctx_place) * block_len, block_len, 0
    )
    grad_qkv_sent, late_part, sent_out = lax.optimization_barrier(
        (grad_qkv_sent, grad_qkv_part, sent_out)
    )
    grad_qkv_got = swap(grad_qkv_sent, "ctx")
    grad_qkv_weight = dot(normed_all, late_part, 0, 0).astype(jnp.bfloat16)
    mlp_total = pair_sum(mlp_pair, mlp_across)
    mlp_sum = jnp.concatenate(ordered(core_place, mlp_total, swap(mlp_total, "tp", CORE)))
    finished = middle + (mlp_sum.astype(jnp.float32) + down_bias)
    grad_qkv_weight, sent_out = lax.optimization_barrier((grad_qkv_weight, sent_out))
    got_out = swap(sent_out, "ctx")
    grad_qkv_got, grad_qkv_weight, finished = lax.optimization_barrier(
        (grad_qkv_got, grad_qkv_weight, finished)
    )
    grad_qkv_first, grad_qkv_second = ordered(ctx_place, grad_qkv_kept, grad_qkv_got)
    grad_qkv_sum = row_major(scatter_rows(grad_qkv_weight)).astype(jnp.float32)
    own_rows = lax.dynamic_slice_in_dim(grad_qkv_sum, ctx_place * drow, drow, 0)
    sent_rows = swap(
        lax.dynamic_slice_in_dim(grad_qkv_sum, (1 - ctx_place) * drow, drow, 0).astype(
            jnp.bfloat16
        ),
        "ctx",
    ).astype(jnp.float32)
    grad_qkv_out = jnp.concatenate(
        [
            part.reshape(drow, 3, part_width)
            for part in ordered(ctx_place, own_rows, sent_rows)
        ],
        axis=2,
    )
    nothing = jnp.zeros_like(bias_sums)
    grad_qv_bias = jnp.concatenate(ordered(ctx_place, bias_sums, nothing), axis=1)

    qkv_first, qkv_second = ordered(ctx_place, qkv_part, qkv_other)

    def first_part(start, count):
        return dot(
            lax.dynamic_slice_in_dim(grad_qkv_first, start, count, 0), qkv_first, 1, 1
        ) + dot(lax.dynamic_slice_in_dim(grad_qkv_second, start, count, 0), qkv_second, 1, 1)

    def by_owner(vector):
        return vector.reshape(owners, 1, drow)

    def row_block(array, first):
        rows, lanes = array.shape[1:]
        return jnp.pad(
            array, ((0, 0), (first, small_rows - first - rows), (0, LANES - lanes))
        )

    def small_work(gated, chip_sum):
        kept_out, got_out, up_rows_sum, down_rows, grad_up_bias = gated
        ffn_rows = jnp.stack([up_rows_sum, down_rows]).reshape(2, 2, drow, part_hidden)
        ffn_kept, ffn_sent = ordered(ctx_place, ffn_rows[:, 0], ffn_rows[:, 1])
        ffn_got = swap(ffn_sent, "ctx")
        half_inputs = lax.dynamic_slice_in_dim(inputs, core_place * half, half, 0)
        half_grad = chip_sum.astype(jnp.float32)
        unused, gain_share, shift_share = normalize_back(half_inputs, gain_one, half_grad)
        up_bias_rows = grad_up_bias.reshape(up_rows // 2, HD)
        up_bias_rows = jnp.concatenate(
            ordered(ctx_place, up_bias_rows, jnp.zeros_like(up_bias_rows))
        )
        small_grads = row_block(
            up_bias_rows.reshape(up_rows, owners, hrow).transpose(1, 0, 2), 16
        ) + row_block(grad_qv_bias.reshape(qv_rows, owners, hrow).transpose(1, 0, 2), 8)
        for place, vector in enumerate(
            (
                gain_share,
                shift_share,
                grad_gain_two,
                grad_shift_two,
                grad_out_bias,
                grad_down_bias,
            )
        ):
            small_grads = small_grads + row_block(by_owner(vector), place)
        return (small_grads, pair_sum(kept_out, got_out), ffn_kept), ffn_got

    first_sum, (small_grads, out_pairs, ffn_kept), ffn_got = sum_tp(
        first_part,
        block_len,
        core_place,
        small_work,
        (kept_out, got_out, up_rows_sum, down_rows, grad_up_bias),
    )
    grad_up, grad_down = jnp.concatenate(ordered(ctx_place, ffn_kept, ffn_got), axis=2)
    grad_out_weight = row_major(scatter_rows(out_pairs))
    grad_inputs_norm, unused, unused = normalize_back(
        inputs, gain_one, first_sum.astype(jnp.float32)
    )
    grad_inputs = grad_middle + grad_inputs_norm
    small_sums = jnp.sum(
        lax.all_to_all(small_grads, ("fsdp", "ctx"), 0, 0, tiled=True), axis=0
    )
    share = small_sums[:2]
    share = share + swap(share, "tp", CORE)
    share = share + swap(share, "tp", CHIP)
    gain_one_sum, shift_one_sum = share[0, :drow], share[1, :drow]
    vector_sums = small_sums[:8, :drow]
    up_bias_sum = small_sums[16 : 16 + up_rows, :hrow]
    qv_bias_sum = small_sums[8 : 8 + qv_rows, :hrow].reshape(2, heads_local, hrow)

    return (
        finished.astype(jnp.bfloat16)[None],
        grad_inputs[None],
        grad_qkv_out,
        qv_bias_sum,
        grad_out_weight.T.astype(jnp.float32),
        vector_sums[4],
        grad_up.astype(jnp.float32),
        up_bias_sum,
        grad_down.T.astype(jnp.float32),
        vector_sums[5],
        gain_one_sum,
        shift_one_sum,
        vector_sums[2],
        vector_sums[3],
    )


def solution(mesh):
    placed = (
        P("fsdp", "ctx", None),
        P("fsdp", None),
        P(("fsdp", "ctx"), None, "tp"),
        P(None, "tp", ("fsdp", "ctx")),
        P("tp", ("fsdp", "ctx")),
        P(("fsdp", "ctx")),
        P(("fsdp", "ctx"), "tp"),
        P("tp", ("fsdp", "ctx")),
        P("tp", ("fsdp", "ctx")),
        P(("fsdp", "ctx")),
        P(("fsdp", "ctx")),
        P(("fsdp", "ctx")),
        P(("fsdp", "ctx")),
        P(("fsdp", "ctx")),
        P("fsdp", "ctx", None),
    )
    return jax.shard_map(
        local,
        mesh=mesh,
        in_specs=placed,
        out_specs=(
            P("fsdp", "ctx", None),
            P("fsdp", "ctx", None),
            P(("fsdp", "ctx"), None, "tp"),
            P(None, "tp", ("fsdp", "ctx")),
            P("tp", ("fsdp", "ctx")),
            P(("fsdp", "ctx")),
            P(("fsdp", "ctx"), "tp"),
            P("tp", ("fsdp", "ctx")),
            P("tp", ("fsdp", "ctx")),
            P(("fsdp", "ctx")),
            P(("fsdp", "ctx")),
            P(("fsdp", "ctx")),
            P(("fsdp", "ctx")),
            P(("fsdp", "ctx")),
        ),
        check_vma=False,
    )
```

```python
import functools

import jax
import jax.numpy as jnp
from jax import lax
from jax.experimental import pallas as pl
from jax.experimental.layout import Layout, with_layout_constraint
from jax.experimental.pallas import tpu as pltpu
from jax.sharding import PartitionSpec as P

HD = 64
LANES = 128
CORE = 1
CHIP = 2
VMEM_LIMIT = 16 * 1024 * 1024

epsilon = 1e-05
negative = -1e30


def swap(array, axis, mask=1):
    devices = lax.axis_size(axis)
    return lax.ppermute(array, axis, [(i, i ^ mask) for i in range(devices)])


def ordered(place, own, other):
    return jnp.where(place == 0, own, other), jnp.where(place == 0, other, own)


def gather_fsdp(block):
    devices = lax.axis_size("fsdp")
    return lax.all_to_all(
        jnp.broadcast_to(block[None], (devices,) + block.shape), "fsdp", 0, 0, tiled=True
    )


def gather_rows(block):
    return lax.all_gather(block, "fsdp", axis=0, tiled=True)


def row_major(array):
    return with_layout_constraint(array, Layout(tuple(range(array.ndim))))


def sum_tp(part_of, rows, core_place, work=None, gated=()):
    half = rows // 2
    sent = swap(part_of((1 - core_place) * half, half).astype(jnp.bfloat16), "tp", CORE)
    kept = part_of(core_place * half, half)
    chip_sum = (kept + sent.astype(jnp.float32)).astype(jnp.bfloat16)
    chip_sum, gated = lax.optimization_barrier((chip_sum, gated))
    across = swap(chip_sum, "tp", CHIP)
    done, free = work(gated, chip_sum) if work else ((), ())
    across, done = lax.optimization_barrier((across, done))
    total = (chip_sum.astype(jnp.float32) + across.astype(jnp.float32)).astype(jnp.bfloat16)
    summed = jnp.concatenate(ordered(core_place, total, swap(total, "tp", CORE)), axis=0)
    return summed, done, free


def other_tokens(rows, core_place):
    half = rows.shape[0] // 2
    got = swap(lax.dynamic_slice_in_dim(rows, core_place * half, half, 0), "ctx")
    return got, swap(got, "tp", CORE)


def chip_parts(own, other, right, core_place):
    half = own.shape[0] // 2

    def summed(sent, kept):
        sent = swap(dot(sent, right, 1, 1).astype(jnp.bfloat16), "tp", CORE)
        return (dot(kept, right, 1, 1) + sent.astype(jnp.float32)).astype(jnp.bfloat16)

    return (
        summed(
            lax.dynamic_slice_in_dim(own, (1 - core_place) * half, half, 0),
            lax.dynamic_slice_in_dim(own, core_place * half, half, 0),
        ),
        summed(other[half:], other[:half]),
    )


def weight_product(wide, narrow, ctx_place):
    devices = lax.axis_size("fsdp")
    rows = wide.shape[1] // (devices * 2)
    product = dot(wide, narrow, 0, 0).astype(jnp.bfloat16).reshape(devices, 2, rows, -1)
    return tuple(
        part.reshape(devices * rows, -1)
        for part in ordered(ctx_place, product[:, 0], product[:, 1])
    )


def pair_sum(kept, sent):
    return (kept.astype(jnp.float32) + sent.astype(jnp.float32)).astype(jnp.bfloat16)


def scatter_rows(array):
    return lax.psum_scatter(array, "fsdp", scatter_dimension=0, tiled=True)


def normalize(matrix, factor, offset):
    average = jnp.mean(matrix, axis=-1, keepdims=True)
    centered = matrix - average
    spread = jnp.mean(centered * centered, axis=-1, keepdims=True)
    return centered * lax.rsqrt(spread + epsilon) * factor + offset


def normalize_back(matrix, factor, grad):
    average = jnp.mean(matrix, axis=-1, keepdims=True)
    centered = matrix - average
    spread = jnp.mean(centered * centered, axis=-1, keepdims=True)
    inverse = lax.rsqrt(spread + epsilon)
    xhat = centered * inverse
    scaled = grad * factor
    mean_scaled = jnp.mean(scaled, axis=-1, keepdims=True)
    mean_product = jnp.mean(scaled * xhat, axis=-1, keepdims=True)
    grad_in = inverse * (scaled - mean_scaled - xhat * mean_product)
    return grad_in, jnp.sum(grad * xhat, axis=0), jnp.sum(grad, axis=0)


def gelu_tanh(inputs):
    cubed_vals = inputs * inputs * inputs
    return 0.5 * inputs * (1.0 + jnp.tanh(0.7978845608028654 * (inputs + 0.044715 * cubed_vals)))


def dot(left, right, left_dim, right_dim):
    return lax.dot_general(
        left, right, (((left_dim,), (right_dim,)), ((), ())), preferred_element_type=jnp.float32
    )


def head_masks(shape):
    lane = lax.broadcasted_iota(jnp.int32, shape, 1)
    return [(lane // HD) == head for head in range(shape[1] // HD)]


def attend_kernel(
    rows, drow, scale,
    tokens_ref, packs_ref, vectors_ref, bias_ref, seg_row_ref, seg_col_ref,
    normed_ref, qkv_ref, attended_ref, weight_ref, out_ref,
):
    length = tokens_ref.shape[0]
    part = attended_ref.shape[1]
    for owner in range(packs_ref.shape[0]):
        for kind in range(3):
            weight_ref[owner * drow : (owner + 1) * drow, kind * part : (kind + 1) * part] = (
                packs_ref[owner, kind * drow : (kind + 1) * drow, :]
            )
        for side in range(2):
            first = packs_ref.shape[1] - (2 - side) * drow
            out_ref[owner * drow : (owner + 1) * drow, side * part : (side + 1) * part] = (
                packs_ref[owner, first : first + drow, :]
            )
    masks = head_masks((rows, part))
    for block in range(length // rows):
        here = slice(block * rows, (block + 1) * rows)
        seen = (block + 1) * rows
        inputs = tokens_ref[here, :].astype(jnp.float32)
        centered = inputs - jnp.mean(inputs, axis=-1, keepdims=True)
        spread = jnp.mean(centered * centered, axis=-1, keepdims=True)
        normed = (
            centered * lax.rsqrt(spread + epsilon) * vectors_ref[0:1, :] + vectors_ref[1:2, :]
        ).astype(jnp.bfloat16)
        normed_ref[here, :] = normed
        projected = dot(normed, weight_ref[...], 1, 0) + bias_ref[...]
        qkv_ref[here, :] = projected.astype(jnp.bfloat16)
        queries = qkv_ref[here, :part]
        key_rows = qkv_ref[:seen, part : 2 * part]
        value_rows = qkv_ref[:seen, 2 * part :]
        query_index = block * rows + lax.broadcasted_iota(jnp.int32, (rows, seen), 0)
        key_index = lax.broadcasted_iota(jnp.int32, (rows, seen), 1)
        allowed = (seg_col_ref[here, :] == seg_row_ref[:, :seen]) & (key_index <= query_index)
        result = jnp.zeros((rows, part), jnp.float32)
        for mask in masks:
            scores = dot(jnp.where(mask, queries, 0), key_rows, 1, 1) * scale
            scores = jnp.where(allowed, scores, negative)
            weights = jnp.exp(scores - jnp.max(scores, axis=-1, keepdims=True))
            probs = weights * (1.0 / jnp.sum(weights, axis=-1, keepdims=True))
            result = jnp.where(mask, dot(probs.astype(jnp.bfloat16), value_rows, 1, 0), result)
        attended_ref[here, :] = result.astype(jnp.bfloat16)


def attend_back_kernel(
    rows, scale,
    qkv_ref, grad_ref, seg_row_ref, seg_col_ref,
    out_ref, sums_ref,
    key_sum, value_sum,
):
    length, part = grad_ref.shape
    masks = head_masks((rows, part))
    key_sum[...] = jnp.zeros_like(key_sum)
    value_sum[...] = jnp.zeros_like(value_sum)
    query_total = jnp.zeros((1, part), jnp.float32)
    for block in range(length // rows):
        here = slice(block * rows, (block + 1) * rows)
        seen = (block + 1) * rows
        queries = qkv_ref[here, :part]
        grads = grad_ref[here, :]
        key_rows = qkv_ref[:seen, part : 2 * part]
        value_rows = qkv_ref[:seen, 2 * part :]
        query_index = block * rows + lax.broadcasted_iota(jnp.int32, (seen, rows), 1)
        key_index = lax.broadcasted_iota(jnp.int32, (seen, rows), 0)
        allowed = (seg_col_ref[:seen, :] == seg_row_ref[:, here]) & (key_index <= query_index)
        grad_query = jnp.zeros((rows, part), jnp.float32)
        for mask in masks:
            head_queries = jnp.where(mask, queries, 0)
            head_grads = jnp.where(mask, grads, 0)
            scores = dot(key_rows, head_queries, 1, 1) * scale
            scores = jnp.where(allowed, scores, negative)
            weights = jnp.exp(scores - jnp.max(scores, axis=0, keepdims=True))
            probs = weights * (1.0 / jnp.sum(weights, axis=0, keepdims=True))
            value_sum[:seen, :] += dot(probs.astype(jnp.bfloat16), head_grads, 1, 0)
            grad_probs = dot(value_rows, head_grads, 1, 1)
            inner = jnp.sum(probs * grad_probs, axis=0, keepdims=True)
            grad_scores = (probs * (grad_probs - inner)).astype(jnp.bfloat16)
            key_sum[:seen, :] += dot(grad_scores, head_queries, 1, 0)
            grad_query = jnp.where(mask, dot(grad_scores, key_rows, 0, 0), grad_query)
        grad_query = (grad_query * scale).astype(jnp.bfloat16)
        out_ref[here, :part] = grad_query
        query_total += jnp.sum(grad_query.astype(jnp.float32), axis=0, keepdims=True)
    grad_values = value_sum[...].astype(jnp.bfloat16)
    out_ref[:, part : 2 * part] = (key_sum[...] * scale).astype(jnp.bfloat16)
    out_ref[:, 2 * part :] = grad_values
    sums_ref[0:1, :] = query_total
    sums_ref[1:2, :] = jnp.sum(grad_values.astype(jnp.float32), axis=0, keepdims=True)


def local(
    tokens,
    segments,
    w_qkv,
    b_qv,
    w_out,
    b_out,
    w_up,
    b_up,
    w_down,
    b_down,
    attngain,
    attnshift,
    mlpgain,
    mlpshift,
    cotangent,
):
    fsdp = lax.axis_size("fsdp")
    owners = fsdp * 2
    ctx_place = lax.axis_index("ctx")
    core_place = lax.axis_index("tp") % 2
    block_len, width = tokens.shape[1:]
    length = segments.shape[1]
    local_width = w_qkv.shape[2]
    part_width = local_width // 2
    part_heads = part_width // HD
    heads_local = local_width // HD
    drow = w_qkv.shape[0]
    hrow = b_qv.shape[2]
    score_scale = 1.0 / HD**0.5

    by_kind = jnp.transpose(w_qkv, (1, 0, 2))
    weight_rows = 3 * drow * part_width // LANES
    own_weight = lax.dynamic_slice_in_dim(by_kind, ctx_place * part_width, part_width, 2)
    sent_weight = lax.dynamic_slice_in_dim(by_kind, (1 - ctx_place) * part_width, part_width, 2)
    small_rows = 32
    up_rows = b_up.shape[0]
    qv_rows = b_qv.shape[0] * b_qv.shape[1]

    def padded(array, first):
        array = array.reshape(-1, array.shape[-1])
        rows, lanes = array.shape
        return jnp.pad(array, ((first, small_rows - first - rows), (0, LANES - lanes)))

    small = padded(b_up, 16) + padded(b_qv, 8)
    for place, vector in enumerate((attngain, attnshift, mlpgain, mlpshift, b_out, b_down)):
        small = small + padded(vector, place)
    out_turned = w_out.T
    small = jnp.concatenate([small, out_turned[:, :part_width], out_turned[:, part_width:]])
    own_pack = jnp.concatenate([own_weight.reshape(weight_rows, LANES), small])
    other_pack = swap(
        jnp.concatenate([sent_weight.reshape(weight_rows, LANES), small]), "ctx"
    )
    own_tokens, w_up, w_down, other_pack = lax.optimization_barrier(
        (tokens[0], w_up, w_down, other_pack)
    )
    half = block_len // 2
    other_block = jnp.concatenate(ordered(core_place, *other_tokens(own_tokens, core_place)))
    all_tokens = jnp.concatenate(ordered(ctx_place, own_tokens, other_block))

    part_hidden = w_up.shape[1] // 2
    own_ffn = jnp.concatenate([w_up, row_major(w_down.T)])
    sent_ffn = lax.dynamic_slice_in_dim(own_ffn, (1 - ctx_place) * part_hidden, part_hidden, 1)
    own_ffn = lax.dynamic_slice_in_dim(own_ffn, ctx_place * part_hidden, part_hidden, 1)
    ffn_pair = jnp.stack(ordered(ctx_place, own_ffn, swap(sent_ffn, "ctx")))
    ffn_pair, own_grad = lax.optimization_barrier((ffn_pair, cotangent[0]))
    other_grad = jnp.concatenate(other_tokens(own_grad, core_place))

    both_packs = jnp.stack(ordered(ctx_place, own_pack, other_pack))
    packs = gather_fsdp(both_packs)
    packs, ffn_pair, other_grad = lax.optimization_barrier((packs, ffn_pair, other_grad))
    up_full = gather_rows(ffn_pair[:, :drow].reshape(-1, part_hidden))
    down_full = gather_rows(ffn_pair[:, drow:].reshape(-1, part_hidden))
    packs = packs.reshape(owners, -1, LANES)
    smalls = packs[:, weight_rows : weight_rows + small_rows].astype(jnp.float32)
    first_vectors = smalls[:, :8, :drow].transpose(1, 0, 2).reshape(8, width)
    qv_bias = (
        smalls[:, 8 : 8 + qv_rows, :hrow].transpose(1, 0, 2).reshape(2, local_width)
    )
    qv_bias_part = lax.dynamic_slice_in_dim(qv_bias, ctx_place * part_width, part_width, 1)
    qkv_bias = jnp.concatenate(
        [qv_bias_part[0], jnp.zeros((part_width,), jnp.float32), qv_bias_part[1]]
    )[None]

    seg_row = segments
    seg_col = segments.reshape(length, 1)
    rows = min(256, length)
    normed_all, qkv_rows, attended_part, qkv_part, out_full = pl.pallas_call(
        functools.partial(attend_kernel, rows, drow, score_scale),
        out_shape=(
            jax.ShapeDtypeStruct((length, width), jnp.bfloat16),
            jax.ShapeDtypeStruct((length, 3 * part_width), jnp.bfloat16),
            jax.ShapeDtypeStruct((length, part_width), jnp.bfloat16),
            jax.ShapeDtypeStruct((width, 3 * part_width), jnp.bfloat16),
            jax.ShapeDtypeStruct((width, local_width), jnp.bfloat16),
        ),
        compiler_params=pltpu.CompilerParams(vmem_limit_bytes=VMEM_LIMIT),
        cost_estimate=pl.CostEstimate(
            flops=2 * length * width * 3 * part_width, bytes_accessed=8 * length * width,
            transcendentals=length * length,
        ),
    )(all_tokens, packs, first_vectors, qkv_bias, seg_row, seg_col)

    def to_tokens(array):
        kept = lax.dynamic_slice_in_dim(array, ctx_place * block_len, block_len, 0)
        sent = swap(
            lax.dynamic_slice_in_dim(array, (1 - ctx_place) * block_len, block_len, 0), "ctx"
        )
        return ordered(ctx_place, kept, sent)

    attended = jnp.concatenate(to_tokens(attended_part), axis=1)
    inputs = own_tokens.astype(jnp.float32)

    def out_part(start, count):
        return dot(lax.dynamic_slice_in_dim(attended, start, count, 0), out_full, 1, 1)

    def small_vectors(gated, unused):
        smalls = gated
        vectors = smalls[:, :8, :drow].transpose(1, 0, 2).reshape(8, width)
        up_bias = lax.dynamic_slice_in_dim(
            smalls[:, 16 : 16 + up_rows, :hrow], ctx_place * (up_rows // 2), up_rows // 2, 1
        )
        up_bias = up_bias.transpose(1, 0, 2).reshape(1, -1)
        return (vectors, up_bias), ()

    attended, late_weight = lax.optimization_barrier((attended, qkv_part))
    attn_sum, (vectors, up_bias_part), unused = sum_tp(
        out_part, block_len, core_place, small_vectors, smalls
    )
    qkv_other = swap(late_weight, "ctx")
    attn_sum, up_full, qkv_other = lax.optimization_barrier((attn_sum, up_full, qkv_other))
    gain_one, shift_one, gain_two, shift_two, out_bias, down_bias = (vectors[i] for i in range(6))
    middle = inputs + (attn_sum.astype(jnp.float32) + out_bias)
    normed_two = normalize(middle, gain_two, shift_two).astype(jnp.bfloat16)
    def hidden(rows):
        return dot(rows, up_full, 1, 0) + up_bias_part

    def hidden_grad(pre, grads):
        grad_activated = dot(grads, down_full, 1, 0)
        value, gelu_pull = jax.vjp(gelu_tanh, pre)
        return gelu_pull(grad_activated)[0].astype(jnp.bfloat16)

    half_rows = lax.dynamic_slice_in_dim(normed_two, core_place * half, half, 0)
    half_rows, late_normed = lax.optimization_barrier((half_rows, normed_two))
    got = swap(half_rows, "ctx")
    own_pre = hidden(late_normed)
    own_active = gelu_tanh(own_pre).astype(jnp.bfloat16)
    got, own_pre, own_active, down_full = lax.optimization_barrier(
        (got, own_pre, own_active, down_full)
    )
    other_normed = jnp.concatenate([got, swap(got, "tp", CORE)])
    own_hidden = hidden_grad(own_pre, own_grad)
    other_pre = hidden(other_normed)
    other_active = gelu_tanh(other_pre).astype(jnp.bfloat16)
    other_hidden = hidden_grad(other_pre, other_grad)

    up_kept, up_sent = chip_parts(own_hidden, other_hidden, up_full, core_place)
    up_sent, own_active, other_active, own_hidden, other_hidden = lax.optimization_barrier(
        (up_sent, own_active, other_active, own_hidden, other_hidden)
    )
    up_got = swap(up_sent, "ctx")
    down_product = (
        dot(own_grad, own_active, 0, 0) + dot(other_grad, other_active, 0, 0)
    ).astype(jnp.bfloat16)
    up_product = (
        dot(normed_two, own_hidden, 0, 0) + dot(other_normed, other_hidden, 0, 0)
    ).astype(jnp.bfloat16)
    up_got, down_product, up_product = lax.optimization_barrier(
        (up_got, down_product, up_product)
    )
    down_rows = row_major(scatter_rows(down_product))
    up_rows_sum = row_major(scatter_rows(up_product))
    up_pair = pair_sum(up_kept, up_got)
    up_pair, own_active, other_active, own_hidden, other_hidden, own_grad = (
        lax.optimization_barrier(
            (up_pair, own_active, other_active, own_hidden, other_hidden, own_grad)
        )
    )
    up_across = swap(up_pair, "tp", CHIP)
    mlp_kept, mlp_sent = chip_parts(own_active, other_active, down_full, core_place)
    mlp_got = swap(mlp_sent, "ctx")
    grad_up_bias = jnp.sum(own_hidden.astype(jnp.float32), axis=0) + jnp.sum(
        other_hidden.astype(jnp.float32), axis=0
    )
    grad_down_bias = jnp.sum(own_grad.astype(jnp.float32), axis=0)
    up_across, mlp_kept, mlp_sent, grad_up_bias, grad_down_bias = lax.optimization_barrier(
        (up_across, mlp_kept, mlp_sent, grad_up_bias, grad_down_bias)
    )
    up_total = pair_sum(up_pair, up_across)
    grad_normed_two = jnp.concatenate(
        ordered(core_place, up_total, swap(up_total, "tp", CORE))
    ).astype(jnp.float32)
    grad_out = own_grad.astype(jnp.float32)
    grad_middle_norm, grad_gain_two, grad_shift_two = normalize_back(
        middle, gain_two, grad_normed_two
    )
    grad_middle = grad_out + grad_middle_norm
    grad_branch_low = grad_middle.astype(jnp.bfloat16)
    grad_out_bias = jnp.sum(grad_branch_low.astype(jnp.float32), axis=0)
    grad_attended_low = dot(grad_branch_low, out_full, 1, 0).astype(jnp.bfloat16)
    own_cols = lax.dynamic_slice_in_dim(grad_attended_low, ctx_place * part_width, part_width, 1)
    sent_cols = lax.dynamic_slice_in_dim(
        grad_attended_low, (1 - ctx_place) * part_width, part_width, 1
    )
    sent_cols, late_branch, mlp_got, mlp_kept = lax.optimization_barrier(
        (sent_cols, grad_branch_low, mlp_got, mlp_kept)
    )
    got_cols = swap(sent_cols, "ctx")
    mlp_pair = pair_sum(mlp_kept, mlp_got)
    mlp_across = swap(mlp_pair, "tp", CHIP)
    kept_out, sent_out = weight_product(late_branch, attended, ctx_place)
    got_cols, kept_out, sent_out = lax.optimization_barrier((got_cols, kept_out, sent_out))
    got_out = swap(sent_out, "ctx")
    grad_heads = jnp.concatenate(ordered(ctx_place, own_cols, got_cols))
    grad_qkv_part, bias_sums = pl.pallas_call(
        functools.partial(attend_back_kernel, rows, score_scale),
        out_shape=(
            jax.ShapeDtypeStruct((length, 3 * part_width), jnp.bfloat16),
            jax.ShapeDtypeStruct((2, part_width), jnp.float32),
        ),
        scratch_shapes=[
            pltpu.VMEM((length, part_width), jnp.float32),
            pltpu.VMEM((length, part_width), jnp.float32),
        ],
        compiler_params=pltpu.CompilerParams(vmem_limit_bytes=VMEM_LIMIT),
        cost_estimate=pl.CostEstimate(
            flops=10 * length * length * part_width, bytes_accessed=2 * length * width,
            transcendentals=length * length,
        ),
    )(qkv_rows, grad_heads, seg_row, seg_col)
    grad_qkv_kept = lax.dynamic_slice_in_dim(grad_qkv_part, ctx_place * block_len, block_len, 0)
    grad_qkv_sent = lax.dynamic_slice_in_dim(
        grad_qkv_part, (1 - ctx_place) * block_len, block_len, 0
    )
    grad_qkv_sent, late_part, kept_out, got_out = lax.optimization_barrier(
        (grad_qkv_sent, grad_qkv_part, kept_out, got_out)
    )
    grad_qkv_got = swap(grad_qkv_sent, "ctx")
    grad_qkv_weight = dot(normed_all, late_part, 0, 0).astype(jnp.bfloat16)
    out_pairs = pair_sum(kept_out, got_out)
    grad_qkv_got, grad_qkv_weight, out_pairs, mlp_across, mlp_pair = lax.optimization_barrier(
        (grad_qkv_got, grad_qkv_weight, out_pairs, mlp_across, mlp_pair)
    )
    grad_out_weight = row_major(scatter_rows(out_pairs))
    grad_qkv_first, grad_qkv_second = ordered(ctx_place, grad_qkv_kept, grad_qkv_got)
    grad_qkv_sum = row_major(scatter_rows(grad_qkv_weight)).astype(jnp.float32)
    own_rows = lax.dynamic_slice_in_dim(grad_qkv_sum, ctx_place * drow, drow, 0)
    sent_rows = swap(
        lax.dynamic_slice_in_dim(grad_qkv_sum, (1 - ctx_place) * drow, drow, 0).astype(
            jnp.bfloat16
        ),
        "ctx",
    ).astype(jnp.float32)
    grad_qkv_out = jnp.concatenate(
        [
            part.reshape(drow, 3, part_width)
            for part in ordered(ctx_place, own_rows, sent_rows)
        ],
        axis=2,
    )
    nothing = jnp.zeros_like(bias_sums)
    grad_qv_bias = jnp.concatenate(ordered(ctx_place, bias_sums, nothing), axis=1)

    qkv_first, qkv_second = ordered(ctx_place, qkv_part, qkv_other)

    def first_part(start, count):
        return dot(
            lax.dynamic_slice_in_dim(grad_qkv_first, start, count, 0), qkv_first, 1, 1
        ) + dot(lax.dynamic_slice_in_dim(grad_qkv_second, start, count, 0), qkv_second, 1, 1)

    def by_owner(vector):
        return vector.reshape(owners, 1, drow)

    def row_block(array, first):
        rows, lanes = array.shape[1:]
        return jnp.pad(
            array, ((0, 0), (first, small_rows - first - rows), (0, LANES - lanes))
        )

    def small_work(gated, chip_sum):
        up_rows_sum, down_rows, grad_up_bias, mlp_pair, mlp_across = gated
        ffn_rows = jnp.stack([up_rows_sum, down_rows]).reshape(2, 2, drow, part_hidden)
        ffn_kept, ffn_sent = ordered(ctx_place, ffn_rows[:, 0], ffn_rows[:, 1])
        ffn_got = swap(ffn_sent, "ctx")
        half_inputs = lax.dynamic_slice_in_dim(inputs, core_place * half, half, 0)
        half_grad = chip_sum.astype(jnp.float32)
        unused, gain_share, shift_share = normalize_back(half_inputs, gain_one, half_grad)
        up_bias_rows = grad_up_bias.reshape(up_rows // 2, HD)
        up_bias_rows = jnp.concatenate(
            ordered(ctx_place, up_bias_rows, jnp.zeros_like(up_bias_rows))
        )
        small_grads = row_block(
            up_bias_rows.reshape(up_rows, owners, hrow).transpose(1, 0, 2), 16
        ) + row_block(grad_qv_bias.reshape(qv_rows, owners, hrow).transpose(1, 0, 2), 8)
        for place, vector in enumerate(
            (
                gain_share,
                shift_share,
                grad_gain_two,
                grad_shift_two,
                grad_out_bias,
                grad_down_bias,
            )
        ):
            small_grads = small_grads + row_block(by_owner(vector), place)
        small_sums = jnp.sum(
            lax.all_to_all(small_grads, ("fsdp", "ctx"), 0, 0, tiled=True), axis=0
        )
        mlp_total = pair_sum(mlp_pair, mlp_across)
        return (small_sums, ffn_kept, mlp_total), ffn_got

    first_sum, (small_sums, ffn_kept, mlp_total), ffn_got = sum_tp(
        first_part,
        block_len,
        core_place,
        small_work,
        (up_rows_sum, down_rows, grad_up_bias, mlp_pair, mlp_across),
    )
    grad_up, grad_down = jnp.concatenate(ordered(ctx_place, ffn_kept, ffn_got), axis=2)
    mlp_sum = jnp.concatenate(ordered(core_place, mlp_total, swap(mlp_total, "tp", CORE)))
    finished = middle + (mlp_sum.astype(jnp.float32) + down_bias)
    grad_inputs_norm, unused, unused = normalize_back(
        inputs, gain_one, first_sum.astype(jnp.float32)
    )
    grad_inputs = grad_middle + grad_inputs_norm
    share = small_sums[:2]
    share = share + swap(share, "tp", CORE)
    share = share + swap(share, "tp", CHIP)
    gain_one_sum, shift_one_sum = share[0, :drow], share[1, :drow]
    vector_sums = small_sums[:8, :drow]
    up_bias_sum = small_sums[16 : 16 + up_rows, :hrow]
    qv_bias_sum = small_sums[8 : 8 + qv_rows, :hrow].reshape(2, heads_local, hrow)

    return (
        finished.astype(jnp.bfloat16)[None],
        grad_inputs[None],
        grad_qkv_out,
        qv_bias_sum,
        grad_out_weight.T.astype(jnp.float32),
        vector_sums[4],
        grad_up.astype(jnp.float32),
        up_bias_sum,
        grad_down.T.astype(jnp.float32),
        vector_sums[5],
        gain_one_sum,
        shift_one_sum,
        vector_sums[2],
        vector_sums[3],
    )


def solution(mesh):
    placed = (
        P("fsdp", "ctx", None),
        P("fsdp", None),
        P(("fsdp", "ctx"), None, "tp"),
        P(None, "tp", ("fsdp", "ctx")),
        P("tp", ("fsdp", "ctx")),
        P(("fsdp", "ctx")),
        P(("fsdp", "ctx"), "tp"),
        P("tp", ("fsdp", "ctx")),
        P("tp", ("fsdp", "ctx")),
        P(("fsdp", "ctx")),
        P(("fsdp", "ctx")),
        P(("fsdp", "ctx")),
        P(("fsdp", "ctx")),
        P(("fsdp", "ctx")),
        P("fsdp", "ctx", None),
    )
    return jax.shard_map(
        local,
        mesh=mesh,
        in_specs=placed,
        out_specs=(
            P("fsdp", "ctx", None),
            P("fsdp", "ctx", None),
            P(("fsdp", "ctx"), None, "tp"),
            P(None, "tp", ("fsdp", "ctx")),
            P("tp", ("fsdp", "ctx")),
            P(("fsdp", "ctx")),
            P(("fsdp", "ctx"), "tp"),
            P("tp", ("fsdp", "ctx")),
            P("tp", ("fsdp", "ctx")),
            P(("fsdp", "ctx")),
            P(("fsdp", "ctx")),
            P(("fsdp", "ctx")),
            P(("fsdp", "ctx")),
            P(("fsdp", "ctx")),
        ),
        check_vma=False,
    )
```

```python
import functools

import jax
import jax.numpy as jnp
from jax import lax
from jax.experimental import pallas as pl
from jax.experimental.layout import Layout, with_layout_constraint
from jax.experimental.pallas import tpu as pltpu
from jax.sharding import PartitionSpec as P

HD = 64
LANES = 128
CORE = 1
CHIP = 2
VMEM_LIMIT = 16 * 1024 * 1024

epsilon = 1e-05
negative = -1e30


def swap(array, axis, mask=1):
    devices = lax.axis_size(axis)
    return lax.ppermute(array, axis, [(i, i ^ mask) for i in range(devices)])


def ordered(place, own, other):
    return jnp.where(place == 0, own, other), jnp.where(place == 0, other, own)


def gather_fsdp(block):
    devices = lax.axis_size("fsdp")
    return lax.all_to_all(
        jnp.broadcast_to(block[None], (devices,) + block.shape), "fsdp", 0, 0, tiled=True
    )


def gather_rows(block):
    return lax.all_gather(block, "fsdp", axis=0, tiled=True)


def row_major(array):
    return with_layout_constraint(array, Layout(tuple(range(array.ndim))))


def sum_tp(part_of, rows, core_place, work=None, gated=()):
    half = rows // 2
    sent = swap(part_of((1 - core_place) * half, half).astype(jnp.bfloat16), "tp", CORE)
    kept = part_of(core_place * half, half)
    chip_sum = (kept + sent.astype(jnp.float32)).astype(jnp.bfloat16)
    chip_sum, gated = lax.optimization_barrier((chip_sum, gated))
    across = swap(chip_sum, "tp", CHIP)
    done, free = work(gated, chip_sum) if work else ((), ())
    across, done = lax.optimization_barrier((across, done))
    total = (chip_sum.astype(jnp.float32) + across.astype(jnp.float32)).astype(jnp.bfloat16)
    summed = jnp.concatenate(ordered(core_place, total, swap(total, "tp", CORE)), axis=0)
    return summed, done, free


def other_tokens(rows, core_place):
    half = rows.shape[0] // 2
    got = swap(lax.dynamic_slice_in_dim(rows, core_place * half, half, 0), "ctx")
    return got, swap(got, "tp", CORE)


def chip_sum_rows(sent, kept, right):
    sent = swap(dot(sent, right, 1, 1).astype(jnp.bfloat16), "tp", CORE)
    return (dot(kept, right, 1, 1) + sent.astype(jnp.float32)).astype(jnp.bfloat16)


def chip_parts(own, other, right, core_place):
    half = own.shape[0] // 2
    return (
        chip_sum_rows(
            lax.dynamic_slice_in_dim(own, (1 - core_place) * half, half, 0),
            lax.dynamic_slice_in_dim(own, core_place * half, half, 0),
            right,
        ),
        chip_sum_rows(other[half:], other[:half], right),
    )


def weight_product(wide, narrow, ctx_place):
    devices = lax.axis_size("fsdp")
    rows = wide.shape[1] // (devices * 2)
    product = dot(wide, narrow, 0, 0).astype(jnp.bfloat16).reshape(devices, 2, rows, -1)
    return tuple(
        part.reshape(devices * rows, -1)
        for part in ordered(ctx_place, product[:, 0], product[:, 1])
    )


def pair_sum(kept, sent):
    return (kept.astype(jnp.float32) + sent.astype(jnp.float32)).astype(jnp.bfloat16)


def scatter_rows(array):
    return lax.psum_scatter(array, "fsdp", scatter_dimension=0, tiled=True)


def normalize(matrix, factor, offset):
    average = jnp.mean(matrix, axis=-1, keepdims=True)
    centered = matrix - average
    spread = jnp.mean(centered * centered, axis=-1, keepdims=True)
    return centered * lax.rsqrt(spread + epsilon) * factor + offset


def normalize_back(matrix, factor, grad):
    average = jnp.mean(matrix, axis=-1, keepdims=True)
    centered = matrix - average
    spread = jnp.mean(centered * centered, axis=-1, keepdims=True)
    inverse = lax.rsqrt(spread + epsilon)
    xhat = centered * inverse
    scaled = grad * factor
    mean_scaled = jnp.mean(scaled, axis=-1, keepdims=True)
    mean_product = jnp.mean(scaled * xhat, axis=-1, keepdims=True)
    grad_in = inverse * (scaled - mean_scaled - xhat * mean_product)
    return grad_in, jnp.sum(grad * xhat, axis=0), jnp.sum(grad, axis=0)


def gelu_tanh(inputs):
    cubed_vals = inputs * inputs * inputs
    return 0.5 * inputs * (1.0 + jnp.tanh(0.7978845608028654 * (inputs + 0.044715 * cubed_vals)))


def dot(left, right, left_dim, right_dim):
    return lax.dot_general(
        left, right, (((left_dim,), (right_dim,)), ((), ())), preferred_element_type=jnp.float32
    )


def head_masks(shape):
    lane = lax.broadcasted_iota(jnp.int32, shape, 1)
    return [(lane // HD) == head for head in range(shape[1] // HD)]


def attend_kernel(
    rows, drow, scale,
    tokens_ref, packs_ref, vectors_ref, bias_ref, seg_row_ref, seg_col_ref,
    normed_ref, qkv_ref, attended_ref, weight_ref, out_ref,
):
    length = tokens_ref.shape[0]
    part = attended_ref.shape[1]
    for owner in range(packs_ref.shape[0]):
        for kind in range(3):
            weight_ref[owner * drow : (owner + 1) * drow, kind * part : (kind + 1) * part] = (
                packs_ref[owner, kind * drow : (kind + 1) * drow, :]
            )
        for side in range(2):
            first = packs_ref.shape[1] - (2 - side) * drow
            out_ref[owner * drow : (owner + 1) * drow, side * part : (side + 1) * part] = (
                packs_ref[owner, first : first + drow, :]
            )
    masks = head_masks((rows, part))
    for block in range(length // rows):
        here = slice(block * rows, (block + 1) * rows)
        seen = (block + 1) * rows
        inputs = tokens_ref[here, :].astype(jnp.float32)
        centered = inputs - jnp.mean(inputs, axis=-1, keepdims=True)
        spread = jnp.mean(centered * centered, axis=-1, keepdims=True)
        normed = (
            centered * lax.rsqrt(spread + epsilon) * vectors_ref[0:1, :] + vectors_ref[1:2, :]
        ).astype(jnp.bfloat16)
        normed_ref[here, :] = normed
        projected = dot(normed, weight_ref[...], 1, 0) + bias_ref[...]
        qkv_ref[here, :] = projected.astype(jnp.bfloat16)
        queries = qkv_ref[here, :part]
        key_rows = qkv_ref[:seen, part : 2 * part]
        value_rows = qkv_ref[:seen, 2 * part :]
        query_index = block * rows + lax.broadcasted_iota(jnp.int32, (rows, seen), 0)
        key_index = lax.broadcasted_iota(jnp.int32, (rows, seen), 1)
        allowed = (seg_col_ref[here, :] == seg_row_ref[:, :seen]) & (key_index <= query_index)
        result = jnp.zeros((rows, part), jnp.float32)
        for mask in masks:
            scores = dot(jnp.where(mask, queries, 0), key_rows, 1, 1) * scale
            scores = jnp.where(allowed, scores, negative)
            weights = jnp.exp(scores - jnp.max(scores, axis=-1, keepdims=True))
            probs = weights * (1.0 / jnp.sum(weights, axis=-1, keepdims=True))
            result = jnp.where(mask, dot(probs.astype(jnp.bfloat16), value_rows, 1, 0), result)
        attended_ref[here, :] = result.astype(jnp.bfloat16)


def attend_back_kernel(
    rows, scale,
    qkv_ref, grad_ref, seg_row_ref, seg_col_ref,
    out_ref, sums_ref,
    key_sum, value_sum,
):
    length, part = grad_ref.shape
    masks = head_masks((rows, part))
    key_sum[...] = jnp.zeros_like(key_sum)
    value_sum[...] = jnp.zeros_like(value_sum)
    query_total = jnp.zeros((1, part), jnp.float32)
    for block in range(length // rows):
        here = slice(block * rows, (block + 1) * rows)
        seen = (block + 1) * rows
        queries = qkv_ref[here, :part]
        grads = grad_ref[here, :]
        key_rows = qkv_ref[:seen, part : 2 * part]
        value_rows = qkv_ref[:seen, 2 * part :]
        query_index = block * rows + lax.broadcasted_iota(jnp.int32, (seen, rows), 1)
        key_index = lax.broadcasted_iota(jnp.int32, (seen, rows), 0)
        allowed = (seg_col_ref[:seen, :] == seg_row_ref[:, here]) & (key_index <= query_index)
        grad_query = jnp.zeros((rows, part), jnp.float32)
        for mask in masks:
            head_queries = jnp.where(mask, queries, 0)
            head_grads = jnp.where(mask, grads, 0)
            scores = dot(key_rows, head_queries, 1, 1) * scale
            scores = jnp.where(allowed, scores, negative)
            weights = jnp.exp(scores - jnp.max(scores, axis=0, keepdims=True))
            probs = weights * (1.0 / jnp.sum(weights, axis=0, keepdims=True))
            value_sum[:seen, :] += dot(probs.astype(jnp.bfloat16), head_grads, 1, 0)
            grad_probs = dot(value_rows, head_grads, 1, 1)
            inner = jnp.sum(probs * grad_probs, axis=0, keepdims=True)
            grad_scores = (probs * (grad_probs - inner)).astype(jnp.bfloat16)
            key_sum[:seen, :] += dot(grad_scores, head_queries, 1, 0)
            grad_query = jnp.where(mask, dot(grad_scores, key_rows, 0, 0), grad_query)
        grad_query = (grad_query * scale).astype(jnp.bfloat16)
        out_ref[here, :part] = grad_query
        query_total += jnp.sum(grad_query.astype(jnp.float32), axis=0, keepdims=True)
    grad_values = value_sum[...].astype(jnp.bfloat16)
    out_ref[:, part : 2 * part] = (key_sum[...] * scale).astype(jnp.bfloat16)
    out_ref[:, 2 * part :] = grad_values
    sums_ref[0:1, :] = query_total
    sums_ref[1:2, :] = jnp.sum(grad_values.astype(jnp.float32), axis=0, keepdims=True)


def local(
    tokens,
    segments,
    w_qkv,
    b_qv,
    w_out,
    b_out,
    w_up,
    b_up,
    w_down,
    b_down,
    attngain,
    attnshift,
    mlpgain,
    mlpshift,
    cotangent,
):
    fsdp = lax.axis_size("fsdp")
    owners = fsdp * 2
    ctx_place = lax.axis_index("ctx")
    core_place = lax.axis_index("tp") % 2
    block_len, width = tokens.shape[1:]
    length = segments.shape[1]
    local_width = w_qkv.shape[2]
    part_width = local_width // 2
    part_heads = part_width // HD
    heads_local = local_width // HD
    drow = w_qkv.shape[0]
    hrow = b_qv.shape[2]
    score_scale = 1.0 / HD**0.5

    by_kind = jnp.transpose(w_qkv, (1, 0, 2))
    weight_rows = 3 * drow * part_width // LANES
    own_weight = lax.dynamic_slice_in_dim(by_kind, ctx_place * part_width, part_width, 2)
    sent_weight = lax.dynamic_slice_in_dim(by_kind, (1 - ctx_place) * part_width, part_width, 2)
    small_rows = 32
    up_rows = b_up.shape[0]
    qv_rows = b_qv.shape[0] * b_qv.shape[1]

    def padded(array, first):
        array = array.reshape(-1, array.shape[-1])
        rows, lanes = array.shape
        return jnp.pad(array, ((first, small_rows - first - rows), (0, LANES - lanes)))

    small = padded(b_up, 16) + padded(b_qv, 8)
    for place, vector in enumerate((attngain, attnshift, mlpgain, mlpshift, b_out, b_down)):
        small = small + padded(vector, place)
    out_turned = w_out.T
    small = jnp.concatenate([small, out_turned[:, :part_width], out_turned[:, part_width:]])
    own_pack = jnp.concatenate([own_weight.reshape(weight_rows, LANES), small])
    other_pack = swap(
        jnp.concatenate([sent_weight.reshape(weight_rows, LANES), small]), "ctx"
    )
    own_tokens, w_up, w_down, other_pack = lax.optimization_barrier(
        (tokens[0], w_up, w_down, other_pack)
    )
    half = block_len // 2
    other_block = jnp.concatenate(ordered(core_place, *other_tokens(own_tokens, core_place)))
    all_tokens = jnp.concatenate(ordered(ctx_place, own_tokens, other_block))

    part_hidden = w_up.shape[1] // 2
    own_ffn = jnp.concatenate([w_up, row_major(w_down.T)])
    sent_ffn = lax.dynamic_slice_in_dim(own_ffn, (1 - ctx_place) * part_hidden, part_hidden, 1)
    own_ffn = lax.dynamic_slice_in_dim(own_ffn, ctx_place * part_hidden, part_hidden, 1)
    ffn_pair = jnp.stack(ordered(ctx_place, own_ffn, swap(sent_ffn, "ctx")))
    all_tokens, own_grad = lax.optimization_barrier((all_tokens, cotangent[0]))
    grad_got, grad_turned = other_tokens(own_grad, core_place)

    both_packs = jnp.stack(ordered(ctx_place, own_pack, other_pack))
    packs = gather_fsdp(both_packs)
    packs, ffn_pair = lax.optimization_barrier((packs, ffn_pair))
    up_full = gather_rows(ffn_pair[:, :drow].reshape(-1, part_hidden))
    down_full = gather_rows(ffn_pair[:, drow:].reshape(-1, part_hidden))
    packs = packs.reshape(owners, -1, LANES)
    smalls = packs[:, weight_rows : weight_rows + small_rows].astype(jnp.float32)
    first_vectors = smalls[:, :8, :drow].transpose(1, 0, 2).reshape(8, width)
    qv_bias = (
        smalls[:, 8 : 8 + qv_rows, :hrow].transpose(1, 0, 2).reshape(2, local_width)
    )
    qv_bias_part = lax.dynamic_slice_in_dim(qv_bias, ctx_place * part_width, part_width, 1)
    qkv_bias = jnp.concatenate(
        [qv_bias_part[0], jnp.zeros((part_width,), jnp.float32), qv_bias_part[1]]
    )[None]

    seg_row = segments
    seg_col = segments.reshape(length, 1)
    rows = min(256, length)
    normed_all, qkv_rows, attended_part, qkv_part, out_full = pl.pallas_call(
        functools.partial(attend_kernel, rows, drow, score_scale),
        out_shape=(
            jax.ShapeDtypeStruct((length, width), jnp.bfloat16),
            jax.ShapeDtypeStruct((length, 3 * part_width), jnp.bfloat16),
            jax.ShapeDtypeStruct((length, part_width), jnp.bfloat16),
            jax.ShapeDtypeStruct((width, 3 * part_width), jnp.bfloat16),
            jax.ShapeDtypeStruct((width, local_width), jnp.bfloat16),
        ),
        compiler_params=pltpu.CompilerParams(vmem_limit_bytes=VMEM_LIMIT),
        cost_estimate=pl.CostEstimate(
            flops=2 * length * width * 3 * part_width, bytes_accessed=8 * length * width,
            transcendentals=length * length,
        ),
    )(all_tokens, packs, first_vectors, qkv_bias, seg_row, seg_col)

    def to_tokens(array):
        kept = lax.dynamic_slice_in_dim(array, ctx_place * block_len, block_len, 0)
        sent = swap(
            lax.dynamic_slice_in_dim(array, (1 - ctx_place) * block_len, block_len, 0), "ctx"
        )
        return ordered(ctx_place, kept, sent)

    attended = to_tokens(attended_part)
    attended, up_full, grad_got, grad_turned = lax.optimization_barrier(
        (attended, up_full, grad_got, grad_turned)
    )
    attended = jnp.concatenate(attended, axis=1)
    inputs = own_tokens.astype(jnp.float32)

    def out_part(start, count):
        return dot(lax.dynamic_slice_in_dim(attended, start, count, 0), out_full, 1, 1)

    def small_vectors(gated, unused):
        smalls = gated
        vectors = smalls[:, :8, :drow].transpose(1, 0, 2).reshape(8, width)
        up_bias = lax.dynamic_slice_in_dim(
            smalls[:, 16 : 16 + up_rows, :hrow], ctx_place * (up_rows // 2), up_rows // 2, 1
        )
        up_bias = up_bias.transpose(1, 0, 2).reshape(1, -1)
        return (vectors, up_bias), ()

    attn_sum, (vectors, up_bias_part), unused = sum_tp(
        out_part, block_len, core_place, small_vectors, smalls
    )
    gain_one, shift_one, gain_two, shift_two, out_bias, down_bias = (vectors[i] for i in range(6))
    middle = inputs + (attn_sum.astype(jnp.float32) + out_bias)
    normed_two = normalize(middle, gain_two, shift_two).astype(jnp.bfloat16)
    def hidden(rows):
        return dot(rows, up_full, 1, 0) + up_bias_part

    def hidden_grad(pre, grads):
        grad_activated = dot(grads, down_full, 1, 0)
        value, gelu_pull = jax.vjp(gelu_tanh, pre)
        return gelu_pull(grad_activated)[0].astype(jnp.bfloat16)

    half_rows = lax.dynamic_slice_in_dim(normed_two, core_place * half, half, 0)
    half_rows, late_normed, down_full = lax.optimization_barrier(
        (half_rows, normed_two, down_full)
    )
    got = swap(half_rows, "ctx")
    own_pre = hidden(late_normed)
    own_active = gelu_tanh(own_pre).astype(jnp.bfloat16)
    own_hidden = hidden_grad(own_pre, own_grad)
    other_grad = jnp.concatenate([grad_got, grad_turned])
    got, own_hidden, own_active, other_grad = lax.optimization_barrier(
        (got, own_hidden, own_active, other_grad)
    )
    other_normed = jnp.concatenate([got, swap(got, "tp", CORE)])
    other_pre = hidden(other_normed)
    other_active = gelu_tanh(other_pre).astype(jnp.bfloat16)
    other_hidden = hidden_grad(other_pre, other_grad)

    up_kept, up_sent = chip_parts(own_hidden, other_hidden, up_full, core_place)
    up_sent, own_active, other_active, own_hidden, other_hidden = lax.optimization_barrier(
        (up_sent, own_active, other_active, own_hidden, other_hidden)
    )
    up_got = swap(up_sent, "ctx")
    up_product = (
        dot(normed_two, own_hidden, 0, 0) + dot(other_normed, other_hidden, 0, 0)
    ).astype(jnp.bfloat16)
    mlp_kept, mlp_sent = chip_parts(own_active, other_active, down_full, core_place)
    up_got, up_product, mlp_kept, mlp_sent = lax.optimization_barrier(
        (up_got, up_product, mlp_kept, mlp_sent)
    )
    up_rows_sum = row_major(scatter_rows(up_product))
    up_pair = pair_sum(up_kept, up_got)
    up_pair, own_active, other_active, own_hidden, other_hidden, own_grad, mlp_sent = (
        lax.optimization_barrier(
            (up_pair, own_active, other_active, own_hidden, other_hidden, own_grad, mlp_sent)
        )
    )
    up_across = swap(up_pair, "tp", CHIP)
    mlp_got = swap(mlp_sent, "ctx")
    down_product = (
        dot(own_grad, own_active, 0, 0) + dot(other_grad, other_active, 0, 0)
    ).astype(jnp.bfloat16)
    grad_up_bias = jnp.sum(own_hidden.astype(jnp.float32), axis=0) + jnp.sum(
        other_hidden.astype(jnp.float32), axis=0
    )
    grad_down_bias = jnp.sum(own_grad.astype(jnp.float32), axis=0)
    up_across, mlp_got, down_product, grad_up_bias, grad_down_bias = lax.optimization_barrier(
        (up_across, mlp_got, down_product, grad_up_bias, grad_down_bias)
    )
    down_rows = row_major(scatter_rows(down_product))
    up_total = pair_sum(up_pair, up_across)
    grad_normed_two = jnp.concatenate(
        ordered(core_place, up_total, swap(up_total, "tp", CORE))
    ).astype(jnp.float32)
    grad_out = own_grad.astype(jnp.float32)
    grad_middle_norm, grad_gain_two, grad_shift_two = normalize_back(
        middle, gain_two, grad_normed_two
    )
    grad_middle = grad_out + grad_middle_norm
    grad_branch_low = grad_middle.astype(jnp.bfloat16)
    grad_out_bias = jnp.sum(grad_branch_low.astype(jnp.float32), axis=0)
    grad_attended_low = dot(grad_branch_low, out_full, 1, 0).astype(jnp.bfloat16)
    own_cols = lax.dynamic_slice_in_dim(grad_attended_low, ctx_place * part_width, part_width, 1)
    sent_cols = lax.dynamic_slice_in_dim(
        grad_attended_low, (1 - ctx_place) * part_width, part_width, 1
    )
    sent_cols, late_branch, mlp_got, mlp_kept = lax.optimization_barrier(
        (sent_cols, grad_branch_low, mlp_got, mlp_kept)
    )
    got_cols = swap(sent_cols, "ctx")
    mlp_pair = pair_sum(mlp_kept, mlp_got)
    mlp_across = swap(mlp_pair, "tp", CHIP)
    kept_out, sent_out = weight_product(late_branch, attended, ctx_place)
    got_cols, kept_out, sent_out = lax.optimization_barrier((got_cols, kept_out, sent_out))
    got_out = swap(sent_out, "ctx")
    grad_heads = jnp.concatenate(ordered(ctx_place, own_cols, got_cols))
    grad_qkv_part, bias_sums = pl.pallas_call(
        functools.partial(attend_back_kernel, rows, score_scale),
        out_shape=(
            jax.ShapeDtypeStruct((length, 3 * part_width), jnp.bfloat16),
            jax.ShapeDtypeStruct((2, part_width), jnp.float32),
        ),
        scratch_shapes=[
            pltpu.VMEM((length, part_width), jnp.float32),
            pltpu.VMEM((length, part_width), jnp.float32),
        ],
        compiler_params=pltpu.CompilerParams(vmem_limit_bytes=VMEM_LIMIT),
        cost_estimate=pl.CostEstimate(
            flops=10 * length * length * part_width, bytes_accessed=2 * length * width,
            transcendentals=length * length,
        ),
    )(qkv_rows, grad_heads, seg_row, seg_col)
    def token_rows(ctx, core):
        return lax.dynamic_slice_in_dim(grad_qkv_part, (2 * ctx + core) * half, half, 0)

    first_sent = chip_sum_rows(
        token_rows(1 - ctx_place, 1 - core_place), token_rows(1 - ctx_place, core_place), qkv_part
    )
    first_kept = chip_sum_rows(
        token_rows(ctx_place, 1 - core_place), token_rows(ctx_place, core_place), qkv_part
    )
    first_sent, late_part = lax.optimization_barrier((first_sent, grad_qkv_part))
    first_got = swap(first_sent, "ctx")
    grad_qkv_weight = dot(normed_all, late_part, 0, 0).astype(jnp.bfloat16)
    first_got, first_kept, grad_qkv_weight, kept_out, got_out, mlp_across, mlp_pair = (
        lax.optimization_barrier(
            (first_got, first_kept, grad_qkv_weight, kept_out, got_out, mlp_across, mlp_pair)
        )
    )
    grad_qkv_sum = row_major(scatter_rows(grad_qkv_weight)).astype(jnp.float32)
    own_rows = lax.dynamic_slice_in_dim(grad_qkv_sum, ctx_place * drow, drow, 0)
    sent_rows = swap(
        lax.dynamic_slice_in_dim(grad_qkv_sum, (1 - ctx_place) * drow, drow, 0).astype(
            jnp.bfloat16
        ),
        "ctx",
    ).astype(jnp.float32)
    grad_qkv_out = jnp.concatenate(
        [
            part.reshape(drow, 3, part_width)
            for part in ordered(ctx_place, own_rows, sent_rows)
        ],
        axis=2,
    )
    nothing = jnp.zeros_like(bias_sums)
    grad_qv_bias = jnp.concatenate(ordered(ctx_place, bias_sums, nothing), axis=1)

    def by_owner(vector):
        return vector.reshape(owners, 1, drow)

    def row_block(array, first):
        rows, lanes = array.shape[1:]
        return jnp.pad(
            array, ((0, 0), (first, small_rows - first - rows), (0, LANES - lanes))
        )

    def small_work(gated, chip_sum):
        up_rows_sum, down_rows, grad_up_bias, mlp_pair, mlp_across, kept_out, got_out = gated
        ffn_rows = jnp.stack([up_rows_sum, down_rows]).reshape(2, 2, drow, part_hidden)
        ffn_kept, ffn_sent = ordered(ctx_place, ffn_rows[:, 0], ffn_rows[:, 1])
        ffn_got = swap(ffn_sent, "ctx")
        half_inputs = lax.dynamic_slice_in_dim(inputs, core_place * half, half, 0)
        half_grad = chip_sum.astype(jnp.float32)
        unused, gain_share, shift_share = normalize_back(half_inputs, gain_one, half_grad)
        up_bias_rows = grad_up_bias.reshape(up_rows // 2, HD)
        up_bias_rows = jnp.concatenate(
            ordered(ctx_place, up_bias_rows, jnp.zeros_like(up_bias_rows))
        )
        small_grads = row_block(
            up_bias_rows.reshape(up_rows, owners, hrow).transpose(1, 0, 2), 16
        ) + row_block(grad_qv_bias.reshape(qv_rows, owners, hrow).transpose(1, 0, 2), 8)
        for place, vector in enumerate(
            (
                gain_share,
                shift_share,
                grad_gain_two,
                grad_shift_two,
                grad_out_bias,
                grad_down_bias,
            )
        ):
            small_grads = small_grads + row_block(by_owner(vector), place)
        small_sums = jnp.sum(
            lax.all_to_all(small_grads, ("fsdp", "ctx"), 0, 0, tiled=True), axis=0
        )
        mlp_total = pair_sum(mlp_pair, mlp_across)
        return (small_sums, ffn_kept, mlp_total, pair_sum(kept_out, got_out)), ffn_got

    first_pair = pair_sum(first_kept, first_got)
    first_pair, gated = lax.optimization_barrier(
        (
            first_pair,
            (up_rows_sum, down_rows, grad_up_bias, mlp_pair, mlp_across, kept_out, got_out),
        )
    )
    first_across = swap(first_pair, "tp", CHIP)
    done, ffn_got = small_work(gated, first_pair)
    first_across, done = lax.optimization_barrier((first_across, done))
    small_sums, ffn_kept, mlp_total, out_pairs = done
    grad_out_weight = row_major(scatter_rows(out_pairs))
    first_total = pair_sum(first_pair, first_across)
    first_sum = jnp.concatenate(
        ordered(core_place, first_total, swap(first_total, "tp", CORE))
    )
    grad_up, grad_down = jnp.concatenate(ordered(ctx_place, ffn_kept, ffn_got), axis=2)
    mlp_sum = jnp.concatenate(ordered(core_place, mlp_total, swap(mlp_total, "tp", CORE)))
    finished = middle + (mlp_sum.astype(jnp.float32) + down_bias)
    grad_inputs_norm, unused, unused = normalize_back(
        inputs, gain_one, first_sum.astype(jnp.float32)
    )
    grad_inputs = grad_middle + grad_inputs_norm
    share = small_sums[:2]
    share = share + swap(share, "tp", CORE)
    share = share + swap(share, "tp", CHIP)
    gain_one_sum, shift_one_sum = share[0, :drow], share[1, :drow]
    vector_sums = small_sums[:8, :drow]
    up_bias_sum = small_sums[16 : 16 + up_rows, :hrow]
    qv_bias_sum = small_sums[8 : 8 + qv_rows, :hrow].reshape(2, heads_local, hrow)

    return (
        finished.astype(jnp.bfloat16)[None],
        grad_inputs[None],
        grad_qkv_out,
        qv_bias_sum,
        grad_out_weight.T.astype(jnp.float32),
        vector_sums[4],
        grad_up.astype(jnp.float32),
        up_bias_sum,
        grad_down.T.astype(jnp.float32),
        vector_sums[5],
        gain_one_sum,
        shift_one_sum,
        vector_sums[2],
        vector_sums[3],
    )


def solution(mesh):
    placed = (
        P("fsdp", "ctx", None),
        P("fsdp", None),
        P(("fsdp", "ctx"), None, "tp"),
        P(None, "tp", ("fsdp", "ctx")),
        P("tp", ("fsdp", "ctx")),
        P(("fsdp", "ctx")),
        P(("fsdp", "ctx"), "tp"),
        P("tp", ("fsdp", "ctx")),
        P("tp", ("fsdp", "ctx")),
        P(("fsdp", "ctx")),
        P(("fsdp", "ctx")),
        P(("fsdp", "ctx")),
        P(("fsdp", "ctx")),
        P(("fsdp", "ctx")),
        P("fsdp", "ctx", None),
    )
    return jax.shard_map(
        local,
        mesh=mesh,
        in_specs=placed,
        out_specs=(
            P("fsdp", "ctx", None),
            P("fsdp", "ctx", None),
            P(("fsdp", "ctx"), None, "tp"),
            P(None, "tp", ("fsdp", "ctx")),
            P("tp", ("fsdp", "ctx")),
            P(("fsdp", "ctx")),
            P(("fsdp", "ctx"), "tp"),
            P("tp", ("fsdp", "ctx")),
            P("tp", ("fsdp", "ctx")),
            P(("fsdp", "ctx")),
            P(("fsdp", "ctx")),
            P(("fsdp", "ctx")),
            P(("fsdp", "ctx")),
            P(("fsdp", "ctx")),
        ),
        check_vma=False,
    )
```

```python
import functools

import jax
import jax.numpy as jnp
from jax import lax
from jax.experimental import pallas as pl
from jax.experimental.layout import Layout, with_layout_constraint
from jax.experimental.pallas import tpu as pltpu
from jax.sharding import PartitionSpec as P

HD = 64
LANES = 128
CORE = 1
CHIP = 2
VMEM_LIMIT = 16 * 1024 * 1024

epsilon = 1e-05
negative = -1e30


def swap(array, axis, mask=1):
    devices = lax.axis_size(axis)
    return lax.ppermute(array, axis, [(i, i ^ mask) for i in range(devices)])


def ordered(place, own, other):
    return jnp.where(place == 0, own, other), jnp.where(place == 0, other, own)


def gather_fsdp(block):
    devices = lax.axis_size("fsdp")
    return lax.all_to_all(
        jnp.broadcast_to(block[None], (devices,) + block.shape), "fsdp", 0, 0, tiled=True
    )


def gather_rows(block):
    return lax.all_gather(block, "fsdp", axis=0, tiled=True)


def row_major(array):
    return with_layout_constraint(array, Layout(tuple(range(array.ndim))))


def sum_tp(part_of, rows, core_place, work=None, gated=()):
    half = rows // 2
    sent = swap(part_of((1 - core_place) * half, half).astype(jnp.bfloat16), "tp", CORE)
    kept = part_of(core_place * half, half)
    chip_sum = (kept + sent.astype(jnp.float32)).astype(jnp.bfloat16)
    chip_sum, gated = lax.optimization_barrier((chip_sum, gated))
    across = swap(chip_sum, "tp", CHIP)
    done, free = work(gated, chip_sum) if work else ((), ())
    across, done = lax.optimization_barrier((across, done))
    total = (chip_sum.astype(jnp.float32) + across.astype(jnp.float32)).astype(jnp.bfloat16)
    summed = jnp.concatenate(ordered(core_place, total, swap(total, "tp", CORE)), axis=0)
    return summed, done, free


def other_tokens(rows, core_place):
    half = rows.shape[0] // 2
    got = swap(lax.dynamic_slice_in_dim(rows, core_place * half, half, 0), "ctx")
    return got, swap(got, "tp", CORE)


def chip_sum_rows(sent, kept, right):
    sent = swap(dot(sent, right, 1, 1).astype(jnp.bfloat16), "tp", CORE)
    return (dot(kept, right, 1, 1) + sent.astype(jnp.float32)).astype(jnp.bfloat16)


def chip_parts(own, other, right, core_place):
    half = own.shape[0] // 2
    return (
        chip_sum_rows(
            lax.dynamic_slice_in_dim(own, (1 - core_place) * half, half, 0),
            lax.dynamic_slice_in_dim(own, core_place * half, half, 0),
            right,
        ),
        chip_sum_rows(other[half:], other[:half], right),
    )


def weight_product(wide, narrow, ctx_place):
    devices = lax.axis_size("fsdp")
    rows = wide.shape[1] // (devices * 2)
    product = dot(wide, narrow, 0, 0).astype(jnp.bfloat16).reshape(devices, 2, rows, -1)
    return tuple(
        part.reshape(devices * rows, -1)
        for part in ordered(ctx_place, product[:, 0], product[:, 1])
    )


def pair_sum(kept, sent):
    return (kept.astype(jnp.float32) + sent.astype(jnp.float32)).astype(jnp.bfloat16)


def scatter_rows(array):
    return lax.psum_scatter(array, "fsdp", scatter_dimension=0, tiled=True)


def normalize(matrix, factor, offset):
    average = jnp.mean(matrix, axis=-1, keepdims=True)
    centered = matrix - average
    spread = jnp.mean(centered * centered, axis=-1, keepdims=True)
    return centered * lax.rsqrt(spread + epsilon) * factor + offset


def normalize_back(matrix, factor, grad):
    average = jnp.mean(matrix, axis=-1, keepdims=True)
    centered = matrix - average
    spread = jnp.mean(centered * centered, axis=-1, keepdims=True)
    inverse = lax.rsqrt(spread + epsilon)
    xhat = centered * inverse
    scaled = grad * factor
    mean_scaled = jnp.mean(scaled, axis=-1, keepdims=True)
    mean_product = jnp.mean(scaled * xhat, axis=-1, keepdims=True)
    grad_in = inverse * (scaled - mean_scaled - xhat * mean_product)
    return grad_in, jnp.sum(grad * xhat, axis=0), jnp.sum(grad, axis=0)


def gelu_tanh(inputs):
    cubed_vals = inputs * inputs * inputs
    return 0.5 * inputs * (1.0 + jnp.tanh(0.7978845608028654 * (inputs + 0.044715 * cubed_vals)))


def dot(left, right, left_dim, right_dim):
    return lax.dot_general(
        left, right, (((left_dim,), (right_dim,)), ((), ())), preferred_element_type=jnp.float32
    )


def head_masks(shape):
    lane = lax.broadcasted_iota(jnp.int32, shape, 1)
    return [(lane // HD) == head for head in range(shape[1] // HD)]


def attend_kernel(
    rows, drow, scale,
    tokens_ref, packs_ref, vectors_ref, bias_ref, seg_row_ref, seg_col_ref,
    normed_ref, qkv_ref, attended_ref, weight_ref, out_ref,
):
    length = tokens_ref.shape[0]
    part = attended_ref.shape[1]
    for owner in range(packs_ref.shape[0]):
        for kind in range(3):
            weight_ref[owner * drow : (owner + 1) * drow, kind * part : (kind + 1) * part] = (
                packs_ref[owner, kind * drow : (kind + 1) * drow, :]
            )
        for side in range(2):
            first = packs_ref.shape[1] - (2 - side) * drow
            out_ref[owner * drow : (owner + 1) * drow, side * part : (side + 1) * part] = (
                packs_ref[owner, first : first + drow, :]
            )
    masks = head_masks((rows, part))
    for block in range(length // rows):
        here = slice(block * rows, (block + 1) * rows)
        seen = (block + 1) * rows
        inputs = tokens_ref[here, :].astype(jnp.float32)
        centered = inputs - jnp.mean(inputs, axis=-1, keepdims=True)
        spread = jnp.mean(centered * centered, axis=-1, keepdims=True)
        normed = (
            centered * lax.rsqrt(spread + epsilon) * vectors_ref[0:1, :] + vectors_ref[1:2, :]
        ).astype(jnp.bfloat16)
        normed_ref[here, :] = normed
        projected = dot(normed, weight_ref[...], 1, 0) + bias_ref[...]
        qkv_ref[here, :] = projected.astype(jnp.bfloat16)
        queries = qkv_ref[here, :part]
        key_rows = qkv_ref[:seen, part : 2 * part]
        value_rows = qkv_ref[:seen, 2 * part :]
        query_index = block * rows + lax.broadcasted_iota(jnp.int32, (rows, seen), 0)
        key_index = lax.broadcasted_iota(jnp.int32, (rows, seen), 1)
        allowed = (seg_col_ref[here, :] == seg_row_ref[:, :seen]) & (key_index <= query_index)
        result = jnp.zeros((rows, part), jnp.float32)
        for mask in masks:
            scores = dot(jnp.where(mask, queries, 0), key_rows, 1, 1) * scale
            scores = jnp.where(allowed, scores, negative)
            weights = jnp.exp(scores - jnp.max(scores, axis=-1, keepdims=True))
            probs = weights * (1.0 / jnp.sum(weights, axis=-1, keepdims=True))
            result = jnp.where(mask, dot(probs.astype(jnp.bfloat16), value_rows, 1, 0), result)
        attended_ref[here, :] = result.astype(jnp.bfloat16)


def attend_back_kernel(
    rows, scale,
    qkv_ref, grad_ref, seg_row_ref, seg_col_ref,
    out_ref, sums_ref,
    key_sum, value_sum,
):
    length, part = grad_ref.shape
    masks = head_masks((rows, part))
    key_sum[...] = jnp.zeros_like(key_sum)
    value_sum[...] = jnp.zeros_like(value_sum)
    query_total = jnp.zeros((1, part), jnp.float32)
    for block in range(length // rows):
        here = slice(block * rows, (block + 1) * rows)
        seen = (block + 1) * rows
        queries = qkv_ref[here, :part]
        grads = grad_ref[here, :]
        key_rows = qkv_ref[:seen, part : 2 * part]
        value_rows = qkv_ref[:seen, 2 * part :]
        query_index = block * rows + lax.broadcasted_iota(jnp.int32, (seen, rows), 1)
        key_index = lax.broadcasted_iota(jnp.int32, (seen, rows), 0)
        allowed = (seg_col_ref[:seen, :] == seg_row_ref[:, here]) & (key_index <= query_index)
        grad_query = jnp.zeros((rows, part), jnp.float32)
        for mask in masks:
            head_queries = jnp.where(mask, queries, 0)
            head_grads = jnp.where(mask, grads, 0)
            scores = dot(key_rows, head_queries, 1, 1) * scale
            scores = jnp.where(allowed, scores, negative)
            weights = jnp.exp(scores - jnp.max(scores, axis=0, keepdims=True))
            probs = weights * (1.0 / jnp.sum(weights, axis=0, keepdims=True))
            value_sum[:seen, :] += dot(probs.astype(jnp.bfloat16), head_grads, 1, 0)
            grad_probs = dot(value_rows, head_grads, 1, 1)
            inner = jnp.sum(probs * grad_probs, axis=0, keepdims=True)
            grad_scores = (probs * (grad_probs - inner)).astype(jnp.bfloat16)
            key_sum[:seen, :] += dot(grad_scores, head_queries, 1, 0)
            grad_query = jnp.where(mask, dot(grad_scores, key_rows, 0, 0), grad_query)
        grad_query = (grad_query * scale).astype(jnp.bfloat16)
        out_ref[here, :part] = grad_query
        query_total += jnp.sum(grad_query.astype(jnp.float32), axis=0, keepdims=True)
    grad_values = value_sum[...].astype(jnp.bfloat16)
    out_ref[:, part : 2 * part] = (key_sum[...] * scale).astype(jnp.bfloat16)
    out_ref[:, 2 * part :] = grad_values
    sums_ref[0:1, :] = query_total
    sums_ref[1:2, :] = jnp.sum(grad_values.astype(jnp.float32), axis=0, keepdims=True)


def local(
    tokens,
    segments,
    w_qkv,
    b_qv,
    w_out,
    b_out,
    w_up,
    b_up,
    w_down,
    b_down,
    attngain,
    attnshift,
    mlpgain,
    mlpshift,
    cotangent,
):
    fsdp = lax.axis_size("fsdp")
    owners = fsdp * 2
    ctx_place = lax.axis_index("ctx")
    core_place = lax.axis_index("tp") % 2
    block_len, width = tokens.shape[1:]
    length = segments.shape[1]
    local_width = w_qkv.shape[2]
    part_width = local_width // 2
    part_heads = part_width // HD
    heads_local = local_width // HD
    drow = w_qkv.shape[0]
    hrow = b_qv.shape[2]
    score_scale = 1.0 / HD**0.5

    by_kind = jnp.transpose(w_qkv, (1, 0, 2))
    weight_rows = 3 * drow * part_width // LANES
    own_weight = lax.dynamic_slice_in_dim(by_kind, ctx_place * part_width, part_width, 2)
    sent_weight = lax.dynamic_slice_in_dim(by_kind, (1 - ctx_place) * part_width, part_width, 2)
    small_rows = 32
    up_rows = b_up.shape[0]
    qv_rows = b_qv.shape[0] * b_qv.shape[1]

    def padded(array, first):
        array = array.reshape(-1, array.shape[-1])
        rows, lanes = array.shape
        return jnp.pad(array, ((first, small_rows - first - rows), (0, LANES - lanes)))

    small = padded(b_up, 16) + padded(b_qv, 8)
    for place, vector in enumerate((attngain, attnshift, mlpgain, mlpshift, b_out, b_down)):
        small = small + padded(vector, place)
    out_turned = w_out.T
    small = jnp.concatenate([small, out_turned[:, :part_width], out_turned[:, part_width:]])
    own_pack = jnp.concatenate([own_weight.reshape(weight_rows, LANES), small])
    other_pack = swap(
        jnp.concatenate([sent_weight.reshape(weight_rows, LANES), small]), "ctx"
    )
    own_tokens, w_up, w_down, other_pack = lax.optimization_barrier(
        (tokens[0], w_up, w_down, other_pack)
    )
    half = block_len // 2
    other_block = jnp.concatenate(ordered(core_place, *other_tokens(own_tokens, core_place)))
    all_tokens = jnp.concatenate(ordered(ctx_place, own_tokens, other_block))

    part_hidden = w_up.shape[1] // 2
    own_ffn = jnp.concatenate([w_up, row_major(w_down.T)])
    sent_ffn = lax.dynamic_slice_in_dim(own_ffn, (1 - ctx_place) * part_hidden, part_hidden, 1)
    own_ffn = lax.dynamic_slice_in_dim(own_ffn, ctx_place * part_hidden, part_hidden, 1)
    ffn_pair = jnp.stack(ordered(ctx_place, own_ffn, swap(sent_ffn, "ctx")))
    all_tokens, own_grad = lax.optimization_barrier((all_tokens, cotangent[0]))
    grad_got, grad_turned = other_tokens(own_grad, core_place)

    both_packs = jnp.stack(ordered(ctx_place, own_pack, other_pack))
    packs = gather_fsdp(both_packs)
    up_full = gather_rows(ffn_pair[:, :drow].reshape(-1, part_hidden))
    down_full = gather_rows(ffn_pair[:, drow:].reshape(-1, part_hidden))
    packs = packs.reshape(owners, -1, LANES)
    smalls = packs[:, weight_rows : weight_rows + small_rows].astype(jnp.float32)
    first_vectors = smalls[:, :8, :drow].transpose(1, 0, 2).reshape(8, width)
    qv_bias = (
        smalls[:, 8 : 8 + qv_rows, :hrow].transpose(1, 0, 2).reshape(2, local_width)
    )
    qv_bias_part = lax.dynamic_slice_in_dim(qv_bias, ctx_place * part_width, part_width, 1)
    qkv_bias = jnp.concatenate(
        [qv_bias_part[0], jnp.zeros((part_width,), jnp.float32), qv_bias_part[1]]
    )[None]

    seg_row = segments
    seg_col = segments.reshape(length, 1)
    rows = min(256, length)
    normed_all, qkv_rows, attended_part, qkv_part, out_full = pl.pallas_call(
        functools.partial(attend_kernel, rows, drow, score_scale),
        out_shape=(
            jax.ShapeDtypeStruct((length, width), jnp.bfloat16),
            jax.ShapeDtypeStruct((length, 3 * part_width), jnp.bfloat16),
            jax.ShapeDtypeStruct((length, part_width), jnp.bfloat16),
            jax.ShapeDtypeStruct((width, 3 * part_width), jnp.bfloat16),
            jax.ShapeDtypeStruct((width, local_width), jnp.bfloat16),
        ),
        compiler_params=pltpu.CompilerParams(vmem_limit_bytes=VMEM_LIMIT),
        cost_estimate=pl.CostEstimate(
            flops=2 * length * width * 3 * part_width, bytes_accessed=8 * length * width,
            transcendentals=length * length,
        ),
    )(all_tokens, packs, first_vectors, qkv_bias, seg_row, seg_col)

    def to_tokens(array):
        kept = lax.dynamic_slice_in_dim(array, ctx_place * block_len, block_len, 0)
        sent = swap(
            lax.dynamic_slice_in_dim(array, (1 - ctx_place) * block_len, block_len, 0), "ctx"
        )
        return ordered(ctx_place, kept, sent)

    attended = to_tokens(attended_part)
    attended, grad_got, grad_turned = lax.optimization_barrier((attended, grad_got, grad_turned))
    attended = jnp.concatenate(attended, axis=1)
    inputs = own_tokens.astype(jnp.float32)

    def out_part(start, count):
        return dot(lax.dynamic_slice_in_dim(attended, start, count, 0), out_full, 1, 1)

    def small_vectors(gated, unused):
        smalls, up_full = gated
        vectors = smalls[:, :8, :drow].transpose(1, 0, 2).reshape(8, width)
        up_bias = lax.dynamic_slice_in_dim(
            smalls[:, 16 : 16 + up_rows, :hrow], ctx_place * (up_rows // 2), up_rows // 2, 1
        )
        up_bias = up_bias.transpose(1, 0, 2).reshape(1, -1)
        return (vectors, up_bias, up_full), ()

    attn_sum, (vectors, up_bias_part, up_full), unused = sum_tp(
        out_part, block_len, core_place, small_vectors, (smalls, up_full)
    )
    gain_one, shift_one, gain_two, shift_two, out_bias, down_bias = (vectors[i] for i in range(6))
    middle = inputs + (attn_sum.astype(jnp.float32) + out_bias)
    normed_two = normalize(middle, gain_two, shift_two).astype(jnp.bfloat16)
    def hidden(rows):
        return dot(rows, up_full, 1, 0) + up_bias_part

    def hidden_grad(pre, grads):
        grad_activated = dot(grads, down_full, 1, 0)
        value, gelu_pull = jax.vjp(gelu_tanh, pre)
        return gelu_pull(grad_activated)[0].astype(jnp.bfloat16)

    half_rows = lax.dynamic_slice_in_dim(normed_two, core_place * half, half, 0)
    half_rows, late_normed = lax.optimization_barrier((half_rows, normed_two))
    got = swap(half_rows, "ctx")
    own_pre = hidden(late_normed)
    own_active = gelu_tanh(own_pre).astype(jnp.bfloat16)
    other_grad = jnp.concatenate([grad_got, grad_turned])
    got, own_pre, own_active, other_grad, down_full = lax.optimization_barrier(
        (got, own_pre, own_active, other_grad, down_full)
    )
    other_normed = jnp.concatenate([got, swap(got, "tp", CORE)])
    own_hidden = hidden_grad(own_pre, own_grad)
    other_pre = hidden(other_normed)
    other_active = gelu_tanh(other_pre).astype(jnp.bfloat16)
    other_hidden = hidden_grad(other_pre, other_grad)

    up_kept, up_sent = chip_parts(own_hidden, other_hidden, up_full, core_place)
    up_sent, own_active, other_active, own_hidden, other_hidden = lax.optimization_barrier(
        (up_sent, own_active, other_active, own_hidden, other_hidden)
    )
    up_got = swap(up_sent, "ctx")
    up_product = (
        dot(normed_two, own_hidden, 0, 0) + dot(other_normed, other_hidden, 0, 0)
    ).astype(jnp.bfloat16)
    mlp_kept, mlp_sent = chip_parts(own_active, other_active, down_full, core_place)
    up_got, up_product, mlp_kept, mlp_sent = lax.optimization_barrier(
        (up_got, up_product, mlp_kept, mlp_sent)
    )
    up_rows_sum = row_major(scatter_rows(up_product))
    up_pair = pair_sum(up_kept, up_got)
    up_pair, own_active, other_active, own_hidden, other_hidden, own_grad, mlp_sent = (
        lax.optimization_barrier(
            (up_pair, own_active, other_active, own_hidden, other_hidden, own_grad, mlp_sent)
        )
    )
    up_across = swap(up_pair, "tp", CHIP)
    mlp_got = swap(mlp_sent, "ctx")
    down_product = (
        dot(own_grad, own_active, 0, 0) + dot(other_grad, other_active, 0, 0)
    ).astype(jnp.bfloat16)
    grad_up_bias = jnp.sum(own_hidden.astype(jnp.float32), axis=0) + jnp.sum(
        other_hidden.astype(jnp.float32), axis=0
    )
    grad_down_bias = jnp.sum(own_grad.astype(jnp.float32), axis=0)
    up_across, mlp_got, down_product, grad_up_bias, grad_down_bias = lax.optimization_barrier(
        (up_across, mlp_got, down_product, grad_up_bias, grad_down_bias)
    )
    down_rows = row_major(scatter_rows(down_product))
    up_total = pair_sum(up_pair, up_across)
    grad_normed_two = jnp.concatenate(
        ordered(core_place, up_total, swap(up_total, "tp", CORE))
    ).astype(jnp.float32)
    grad_out = own_grad.astype(jnp.float32)
    grad_middle_norm, grad_gain_two, grad_shift_two = normalize_back(
        middle, gain_two, grad_normed_two
    )
    grad_middle = grad_out + grad_middle_norm
    grad_branch_low = grad_middle.astype(jnp.bfloat16)
    grad_out_bias = jnp.sum(grad_branch_low.astype(jnp.float32), axis=0)
    grad_attended_low = dot(grad_branch_low, out_full, 1, 0).astype(jnp.bfloat16)
    own_cols = lax.dynamic_slice_in_dim(grad_attended_low, ctx_place * part_width, part_width, 1)
    sent_cols = lax.dynamic_slice_in_dim(
        grad_attended_low, (1 - ctx_place) * part_width, part_width, 1
    )
    sent_cols, late_branch, mlp_got, mlp_kept = lax.optimization_barrier(
        (sent_cols, grad_branch_low, mlp_got, mlp_kept)
    )
    got_cols = swap(sent_cols, "ctx")
    mlp_pair = pair_sum(mlp_kept, mlp_got)
    mlp_across = swap(mlp_pair, "tp", CHIP)
    kept_out, sent_out = weight_product(late_branch, attended, ctx_place)
    got_cols, kept_out, sent_out = lax.optimization_barrier((got_cols, kept_out, sent_out))
    got_out = swap(sent_out, "ctx")
    grad_heads = jnp.concatenate(ordered(ctx_place, own_cols, got_cols))
    grad_qkv_part, bias_sums = pl.pallas_call(
        functools.partial(attend_back_kernel, rows, score_scale),
        out_shape=(
            jax.ShapeDtypeStruct((length, 3 * part_width), jnp.bfloat16),
            jax.ShapeDtypeStruct((2, part_width), jnp.float32),
        ),
        scratch_shapes=[
            pltpu.VMEM((length, part_width), jnp.float32),
            pltpu.VMEM((length, part_width), jnp.float32),
        ],
        compiler_params=pltpu.CompilerParams(vmem_limit_bytes=VMEM_LIMIT),
        cost_estimate=pl.CostEstimate(
            flops=10 * length * length * part_width, bytes_accessed=2 * length * width,
            transcendentals=length * length,
        ),
    )(qkv_rows, grad_heads, seg_row, seg_col)
    def token_rows(ctx, core):
        return lax.dynamic_slice_in_dim(grad_qkv_part, (2 * ctx + core) * half, half, 0)

    first_sent = chip_sum_rows(
        token_rows(1 - ctx_place, 1 - core_place), token_rows(1 - ctx_place, core_place), qkv_part
    )
    first_kept = chip_sum_rows(
        token_rows(ctx_place, 1 - core_place), token_rows(ctx_place, core_place), qkv_part
    )
    first_sent, late_part, got_out = lax.optimization_barrier(
        (first_sent, grad_qkv_part, got_out)
    )
    first_got = swap(first_sent, "ctx")
    grad_qkv_weight = dot(normed_all, late_part, 0, 0).astype(jnp.bfloat16)
    first_got, first_kept, kept_out, got_out, mlp_across, mlp_pair = lax.optimization_barrier(
        (first_got, first_kept, kept_out, got_out, mlp_across, mlp_pair)
    )
    grad_qkv_sum = row_major(scatter_rows(grad_qkv_weight)).astype(jnp.float32)
    own_rows = lax.dynamic_slice_in_dim(grad_qkv_sum, ctx_place * drow, drow, 0)
    sent_rows = swap(
        lax.dynamic_slice_in_dim(grad_qkv_sum, (1 - ctx_place) * drow, drow, 0).astype(
            jnp.bfloat16
        ),
        "ctx",
    ).astype(jnp.float32)
    grad_qkv_out = jnp.concatenate(
        [
            part.reshape(drow, 3, part_width)
            for part in ordered(ctx_place, own_rows, sent_rows)
        ],
        axis=2,
    )
    nothing = jnp.zeros_like(bias_sums)
    grad_qv_bias = jnp.concatenate(ordered(ctx_place, bias_sums, nothing), axis=1)

    def by_owner(vector):
        return vector.reshape(owners, 1, drow)

    def row_block(array, first):
        rows, lanes = array.shape[1:]
        return jnp.pad(
            array, ((0, 0), (first, small_rows - first - rows), (0, LANES - lanes))
        )

    def small_work(gated, chip_sum):
        up_rows_sum, down_rows, grad_up_bias, mlp_pair, mlp_across, kept_out, got_out = gated
        ffn_rows = jnp.stack([up_rows_sum, down_rows]).reshape(2, 2, drow, part_hidden)
        ffn_kept, ffn_sent = ordered(ctx_place, ffn_rows[:, 0], ffn_rows[:, 1])
        ffn_got = swap(ffn_sent, "ctx")
        half_inputs = lax.dynamic_slice_in_dim(inputs, core_place * half, half, 0)
        half_grad = chip_sum.astype(jnp.float32)
        unused, gain_share, shift_share = normalize_back(half_inputs, gain_one, half_grad)
        up_bias_rows = grad_up_bias.reshape(up_rows // 2, HD)
        up_bias_rows = jnp.concatenate(
            ordered(ctx_place, up_bias_rows, jnp.zeros_like(up_bias_rows))
        )
        small_grads = row_block(
            up_bias_rows.reshape(up_rows, owners, hrow).transpose(1, 0, 2), 16
        ) + row_block(grad_qv_bias.reshape(qv_rows, owners, hrow).transpose(1, 0, 2), 8)
        for place, vector in enumerate(
            (
                gain_share,
                shift_share,
                grad_gain_two,
                grad_shift_two,
                grad_out_bias,
                grad_down_bias,
            )
        ):
            small_grads = small_grads + row_block(by_owner(vector), place)
        small_sums = jnp.sum(
            lax.all_to_all(small_grads, ("fsdp", "ctx"), 0, 0, tiled=True), axis=0
        )
        mlp_total = pair_sum(mlp_pair, mlp_across)
        return (small_sums, ffn_kept, mlp_total, pair_sum(kept_out, got_out)), ffn_got

    first_pair = pair_sum(first_kept, first_got)
    first_pair, gated = lax.optimization_barrier(
        (
            first_pair,
            (up_rows_sum, down_rows, grad_up_bias, mlp_pair, mlp_across, kept_out, got_out),
        )
    )
    first_across = swap(first_pair, "tp", CHIP)
    done, ffn_got = small_work(gated, first_pair)
    first_across, done = lax.optimization_barrier((first_across, done))
    small_sums, ffn_kept, mlp_total, out_pairs = done
    grad_out_weight = row_major(scatter_rows(out_pairs))
    first_total = pair_sum(first_pair, first_across)
    first_sum = jnp.concatenate(
        ordered(core_place, first_total, swap(first_total, "tp", CORE))
    )
    grad_up, grad_down = jnp.concatenate(ordered(ctx_place, ffn_kept, ffn_got), axis=2)
    mlp_sum = jnp.concatenate(ordered(core_place, mlp_total, swap(mlp_total, "tp", CORE)))
    finished = middle + (mlp_sum.astype(jnp.float32) + down_bias)
    grad_inputs_norm, unused, unused = normalize_back(
        inputs, gain_one, first_sum.astype(jnp.float32)
    )
    grad_inputs = grad_middle + grad_inputs_norm
    share = small_sums[:2]
    share = share + swap(share, "tp", CORE)
    share = share + swap(share, "tp", CHIP)
    gain_one_sum, shift_one_sum = share[0, :drow], share[1, :drow]
    vector_sums = small_sums[:8, :drow]
    up_bias_sum = small_sums[16 : 16 + up_rows, :hrow]
    qv_bias_sum = small_sums[8 : 8 + qv_rows, :hrow].reshape(2, heads_local, hrow)

    return (
        finished.astype(jnp.bfloat16)[None],
        grad_inputs[None],
        grad_qkv_out,
        qv_bias_sum,
        grad_out_weight.T.astype(jnp.float32),
        vector_sums[4],
        grad_up.astype(jnp.float32),
        up_bias_sum,
        grad_down.T.astype(jnp.float32),
        vector_sums[5],
        gain_one_sum,
        shift_one_sum,
        vector_sums[2],
        vector_sums[3],
    )


def solution(mesh):
    placed = (
        P("fsdp", "ctx", None),
        P("fsdp", None),
        P(("fsdp", "ctx"), None, "tp"),
        P(None, "tp", ("fsdp", "ctx")),
        P("tp", ("fsdp", "ctx")),
        P(("fsdp", "ctx")),
        P(("fsdp", "ctx"), "tp"),
        P("tp", ("fsdp", "ctx")),
        P("tp", ("fsdp", "ctx")),
        P(("fsdp", "ctx")),
        P(("fsdp", "ctx")),
        P(("fsdp", "ctx")),
        P(("fsdp", "ctx")),
        P(("fsdp", "ctx")),
        P("fsdp", "ctx", None),
    )
    return jax.shard_map(
        local,
        mesh=mesh,
        in_specs=placed,
        out_specs=(
            P("fsdp", "ctx", None),
            P("fsdp", "ctx", None),
            P(("fsdp", "ctx"), None, "tp"),
            P(None, "tp", ("fsdp", "ctx")),
            P("tp", ("fsdp", "ctx")),
            P(("fsdp", "ctx")),
            P(("fsdp", "ctx"), "tp"),
            P("tp", ("fsdp", "ctx")),
            P("tp", ("fsdp", "ctx")),
            P(("fsdp", "ctx")),
            P(("fsdp", "ctx")),
            P(("fsdp", "ctx")),
            P(("fsdp", "ctx")),
            P(("fsdp", "ctx")),
        ),
        check_vma=False,
    )
```

```python
import functools

import jax
import jax.numpy as jnp
from jax import lax
from jax.experimental import pallas as pl
from jax.experimental.layout import Layout, with_layout_constraint
from jax.experimental.pallas import tpu as pltpu
from jax.sharding import PartitionSpec as P

HD = 64
LANES = 128
CORE = 1
CHIP = 2
VMEM_LIMIT = 16 * 1024 * 1024

epsilon = 1e-05
negative = -1e30


def swap(array, axis, mask=1):
    devices = lax.axis_size(axis)
    return lax.ppermute(array, axis, [(i, i ^ mask) for i in range(devices)])


def ordered(place, own, other):
    return jnp.where(place == 0, own, other), jnp.where(place == 0, other, own)


def gather_fsdp(block):
    devices = lax.axis_size("fsdp")
    return lax.all_to_all(
        jnp.broadcast_to(block[None], (devices,) + block.shape), "fsdp", 0, 0, tiled=True
    )


def gather_rows(block):
    return lax.all_gather(block, "fsdp", axis=0, tiled=True)


def row_major(array):
    return with_layout_constraint(array, Layout(tuple(range(array.ndim))))


def sum_tp(part_of, rows, core_place, work=None, gated=()):
    half = rows // 2
    sent = swap(part_of((1 - core_place) * half, half).astype(jnp.bfloat16), "tp", CORE)
    kept = part_of(core_place * half, half)
    chip_sum = (kept + sent.astype(jnp.float32)).astype(jnp.bfloat16)
    chip_sum, gated = lax.optimization_barrier((chip_sum, gated))
    across = swap(chip_sum, "tp", CHIP)
    done, free = work(gated, chip_sum) if work else ((), ())
    across, done = lax.optimization_barrier((across, done))
    total = (chip_sum.astype(jnp.float32) + across.astype(jnp.float32)).astype(jnp.bfloat16)
    summed = jnp.concatenate(ordered(core_place, total, swap(total, "tp", CORE)), axis=0)
    return summed, done, free


def other_tokens(rows, core_place):
    half = rows.shape[0] // 2
    got = swap(lax.dynamic_slice_in_dim(rows, core_place * half, half, 0), "ctx")
    return got, swap(got, "tp", CORE)


def chip_sum_rows(sent, kept, right):
    sent = swap(dot(sent, right, 1, 1).astype(jnp.bfloat16), "tp", CORE)
    return (dot(kept, right, 1, 1) + sent.astype(jnp.float32)).astype(jnp.bfloat16)


def chip_parts(own, other, right, core_place):
    half = own.shape[0] // 2
    return (
        chip_sum_rows(
            lax.dynamic_slice_in_dim(own, (1 - core_place) * half, half, 0),
            lax.dynamic_slice_in_dim(own, core_place * half, half, 0),
            right,
        ),
        chip_sum_rows(other[half:], other[:half], right),
    )


def weight_product(wide, narrow, ctx_place):
    devices = lax.axis_size("fsdp")
    rows = wide.shape[1] // (devices * 2)
    product = dot(wide, narrow, 0, 0).astype(jnp.bfloat16).reshape(devices, 2, rows, -1)
    return tuple(
        part.reshape(devices * rows, -1)
        for part in ordered(ctx_place, product[:, 0], product[:, 1])
    )


def pair_sum(kept, sent):
    return (kept.astype(jnp.float32) + sent.astype(jnp.float32)).astype(jnp.bfloat16)


def scatter_rows(array):
    return lax.psum_scatter(array, "fsdp", scatter_dimension=0, tiled=True)


def normalize(matrix, factor, offset):
    average = jnp.mean(matrix, axis=-1, keepdims=True)
    centered = matrix - average
    spread = jnp.mean(centered * centered, axis=-1, keepdims=True)
    return centered * lax.rsqrt(spread + epsilon) * factor + offset


def normalize_back(matrix, factor, grad):
    average = jnp.mean(matrix, axis=-1, keepdims=True)
    centered = matrix - average
    spread = jnp.mean(centered * centered, axis=-1, keepdims=True)
    inverse = lax.rsqrt(spread + epsilon)
    xhat = centered * inverse
    scaled = grad * factor
    mean_scaled = jnp.mean(scaled, axis=-1, keepdims=True)
    mean_product = jnp.mean(scaled * xhat, axis=-1, keepdims=True)
    grad_in = inverse * (scaled - mean_scaled - xhat * mean_product)
    return grad_in, jnp.sum(grad * xhat, axis=0), jnp.sum(grad, axis=0)


def gelu_tanh(inputs):
    cubed_vals = inputs * inputs * inputs
    return 0.5 * inputs * (1.0 + jnp.tanh(0.7978845608028654 * (inputs + 0.044715 * cubed_vals)))


def dot(left, right, left_dim, right_dim):
    return lax.dot_general(
        left, right, (((left_dim,), (right_dim,)), ((), ())), preferred_element_type=jnp.float32
    )


def head_masks(shape):
    lane = lax.broadcasted_iota(jnp.int32, shape, 1)
    return [(lane // HD) == head for head in range(shape[1] // HD)]


def attend_kernel(
    rows, drow, scale,
    tokens_ref, packs_ref, vectors_ref, bias_ref, seg_row_ref, seg_col_ref,
    normed_ref, qkv_ref, attended_ref, weight_ref, out_ref,
):
    length = tokens_ref.shape[0]
    part = attended_ref.shape[1]
    for owner in range(packs_ref.shape[0]):
        for kind in range(3):
            weight_ref[owner * drow : (owner + 1) * drow, kind * part : (kind + 1) * part] = (
                packs_ref[owner, kind * drow : (kind + 1) * drow, :]
            )
        for side in range(2):
            first = packs_ref.shape[1] - (2 - side) * drow
            out_ref[owner * drow : (owner + 1) * drow, side * part : (side + 1) * part] = (
                packs_ref[owner, first : first + drow, :]
            )
    masks = head_masks((rows, part))
    for block in range(length // rows):
        here = slice(block * rows, (block + 1) * rows)
        seen = (block + 1) * rows
        inputs = tokens_ref[here, :].astype(jnp.float32)
        centered = inputs - jnp.mean(inputs, axis=-1, keepdims=True)
        spread = jnp.mean(centered * centered, axis=-1, keepdims=True)
        normed = (
            centered * lax.rsqrt(spread + epsilon) * vectors_ref[0:1, :] + vectors_ref[1:2, :]
        ).astype(jnp.bfloat16)
        normed_ref[here, :] = normed
        projected = dot(normed, weight_ref[...], 1, 0) + bias_ref[...]
        qkv_ref[here, :] = projected.astype(jnp.bfloat16)
        queries = qkv_ref[here, :part]
        key_rows = qkv_ref[:seen, part : 2 * part]
        value_rows = qkv_ref[:seen, 2 * part :]
        query_index = block * rows + lax.broadcasted_iota(jnp.int32, (rows, seen), 0)
        key_index = lax.broadcasted_iota(jnp.int32, (rows, seen), 1)
        allowed = (seg_col_ref[here, :] == seg_row_ref[:, :seen]) & (key_index <= query_index)
        result = jnp.zeros((rows, part), jnp.float32)
        for mask in masks:
            scores = dot(jnp.where(mask, queries, 0), key_rows, 1, 1) * scale
            scores = jnp.where(allowed, scores, negative)
            weights = jnp.exp(scores - jnp.max(scores, axis=-1, keepdims=True))
            probs = weights * (1.0 / jnp.sum(weights, axis=-1, keepdims=True))
            result = jnp.where(mask, dot(probs.astype(jnp.bfloat16), value_rows, 1, 0), result)
        attended_ref[here, :] = result.astype(jnp.bfloat16)


def attend_back_kernel(
    rows, scale,
    qkv_ref, grad_ref, seg_row_ref, seg_col_ref,
    out_ref, sums_ref,
    key_sum, value_sum,
):
    length, part = grad_ref.shape
    masks = head_masks((rows, part))
    key_sum[...] = jnp.zeros_like(key_sum)
    value_sum[...] = jnp.zeros_like(value_sum)
    query_total = jnp.zeros((1, part), jnp.float32)
    for block in range(length // rows):
        here = slice(block * rows, (block + 1) * rows)
        seen = (block + 1) * rows
        queries = qkv_ref[here, :part]
        grads = grad_ref[here, :]
        key_rows = qkv_ref[:seen, part : 2 * part]
        value_rows = qkv_ref[:seen, 2 * part :]
        query_index = block * rows + lax.broadcasted_iota(jnp.int32, (seen, rows), 1)
        key_index = lax.broadcasted_iota(jnp.int32, (seen, rows), 0)
        allowed = (seg_col_ref[:seen, :] == seg_row_ref[:, here]) & (key_index <= query_index)
        grad_query = jnp.zeros((rows, part), jnp.float32)
        for mask in masks:
            head_queries = jnp.where(mask, queries, 0)
            head_grads = jnp.where(mask, grads, 0)
            scores = dot(key_rows, head_queries, 1, 1) * scale
            scores = jnp.where(allowed, scores, negative)
            weights = jnp.exp(scores - jnp.max(scores, axis=0, keepdims=True))
            probs = weights * (1.0 / jnp.sum(weights, axis=0, keepdims=True))
            value_sum[:seen, :] += dot(probs.astype(jnp.bfloat16), head_grads, 1, 0)
            grad_probs = dot(value_rows, head_grads, 1, 1)
            inner = jnp.sum(probs * grad_probs, axis=0, keepdims=True)
            grad_scores = (probs * (grad_probs - inner)).astype(jnp.bfloat16)
            key_sum[:seen, :] += dot(grad_scores, head_queries, 1, 0)
            grad_query = jnp.where(mask, dot(grad_scores, key_rows, 0, 0), grad_query)
        grad_query = (grad_query * scale).astype(jnp.bfloat16)
        out_ref[here, :part] = grad_query
        query_total += jnp.sum(grad_query.astype(jnp.float32), axis=0, keepdims=True)
    grad_values = value_sum[...].astype(jnp.bfloat16)
    out_ref[:, part : 2 * part] = (key_sum[...] * scale).astype(jnp.bfloat16)
    out_ref[:, 2 * part :] = grad_values
    sums_ref[0:1, :] = query_total
    sums_ref[1:2, :] = jnp.sum(grad_values.astype(jnp.float32), axis=0, keepdims=True)


def local(
    tokens,
    segments,
    w_qkv,
    b_qv,
    w_out,
    b_out,
    w_up,
    b_up,
    w_down,
    b_down,
    attngain,
    attnshift,
    mlpgain,
    mlpshift,
    cotangent,
):
    fsdp = lax.axis_size("fsdp")
    owners = fsdp * 2
    ctx_place = lax.axis_index("ctx")
    core_place = lax.axis_index("tp") % 2
    block_len, width = tokens.shape[1:]
    length = segments.shape[1]
    local_width = w_qkv.shape[2]
    part_width = local_width // 2
    part_heads = part_width // HD
    heads_local = local_width // HD
    drow = w_qkv.shape[0]
    hrow = b_qv.shape[2]
    score_scale = 1.0 / HD**0.5

    by_kind = jnp.transpose(w_qkv, (1, 0, 2))
    weight_rows = 3 * drow * part_width // LANES
    own_weight = lax.dynamic_slice_in_dim(by_kind, ctx_place * part_width, part_width, 2)
    sent_weight = lax.dynamic_slice_in_dim(by_kind, (1 - ctx_place) * part_width, part_width, 2)
    small_rows = 32
    up_rows = b_up.shape[0]
    qv_rows = b_qv.shape[0] * b_qv.shape[1]

    def padded(array, first):
        array = array.reshape(-1, array.shape[-1])
        rows, lanes = array.shape
        return jnp.pad(array, ((first, small_rows - first - rows), (0, LANES - lanes)))

    small = padded(b_up, 16) + padded(b_qv, 8)
    for place, vector in enumerate((attngain, attnshift, mlpgain, mlpshift, b_out, b_down)):
        small = small + padded(vector, place)
    out_turned = w_out.T
    small = jnp.concatenate([small, out_turned[:, :part_width], out_turned[:, part_width:]])
    own_pack = jnp.concatenate([own_weight.reshape(weight_rows, LANES), small])
    other_pack = swap(
        jnp.concatenate([sent_weight.reshape(weight_rows, LANES), small]), "ctx"
    )
    own_tokens, w_up, w_down, other_pack = lax.optimization_barrier(
        (tokens[0], w_up, w_down, other_pack)
    )
    half = block_len // 2
    other_block = jnp.concatenate(ordered(core_place, *other_tokens(own_tokens, core_place)))
    all_tokens = jnp.concatenate(ordered(ctx_place, own_tokens, other_block))

    part_hidden = w_up.shape[1] // 2
    own_ffn = jnp.concatenate([w_up, row_major(w_down.T)])
    sent_ffn = lax.dynamic_slice_in_dim(own_ffn, (1 - ctx_place) * part_hidden, part_hidden, 1)
    own_ffn = lax.dynamic_slice_in_dim(own_ffn, ctx_place * part_hidden, part_hidden, 1)
    ffn_pair = jnp.stack(ordered(ctx_place, own_ffn, swap(sent_ffn, "ctx")))
    all_tokens, own_grad = lax.optimization_barrier((all_tokens, cotangent[0]))
    grad_got, grad_turned = other_tokens(own_grad, core_place)

    both_packs = jnp.stack(ordered(ctx_place, own_pack, other_pack))
    packs = gather_fsdp(both_packs)
    packs, ffn_pair = lax.optimization_barrier((packs, ffn_pair))
    up_full = gather_rows(ffn_pair[:, :drow].reshape(-1, part_hidden))
    down_full = gather_rows(ffn_pair[:, drow:].reshape(-1, part_hidden))
    packs = packs.reshape(owners, -1, LANES)
    smalls = packs[:, weight_rows : weight_rows + small_rows].astype(jnp.float32)
    first_vectors = smalls[:, :8, :drow].transpose(1, 0, 2).reshape(8, width)
    qv_bias = (
        smalls[:, 8 : 8 + qv_rows, :hrow].transpose(1, 0, 2).reshape(2, local_width)
    )
    qv_bias_part = lax.dynamic_slice_in_dim(qv_bias, ctx_place * part_width, part_width, 1)
    qkv_bias = jnp.concatenate(
        [qv_bias_part[0], jnp.zeros((part_width,), jnp.float32), qv_bias_part[1]]
    )[None]

    seg_row = segments
    seg_col = segments.reshape(length, 1)
    rows = min(256, length)
    normed_all, qkv_rows, attended_part, qkv_part, out_full = pl.pallas_call(
        functools.partial(attend_kernel, rows, drow, score_scale),
        out_shape=(
            jax.ShapeDtypeStruct((length, width), jnp.bfloat16),
            jax.ShapeDtypeStruct((length, 3 * part_width), jnp.bfloat16),
            jax.ShapeDtypeStruct((length, part_width), jnp.bfloat16),
            jax.ShapeDtypeStruct((width, 3 * part_width), jnp.bfloat16),
            jax.ShapeDtypeStruct((width, local_width), jnp.bfloat16),
        ),
        compiler_params=pltpu.CompilerParams(vmem_limit_bytes=VMEM_LIMIT),
        cost_estimate=pl.CostEstimate(
            flops=2 * length * width * 3 * part_width, bytes_accessed=8 * length * width,
            transcendentals=length * length,
        ),
    )(all_tokens, packs, first_vectors, qkv_bias, seg_row, seg_col)

    def to_tokens(array):
        kept = lax.dynamic_slice_in_dim(array, ctx_place * block_len, block_len, 0)
        sent = swap(
            lax.dynamic_slice_in_dim(array, (1 - ctx_place) * block_len, block_len, 0), "ctx"
        )
        return ordered(ctx_place, kept, sent)

    attended = to_tokens(attended_part)
    attended, up_full, grad_got, grad_turned = lax.optimization_barrier(
        (attended, up_full, grad_got, grad_turned)
    )
    attended = jnp.concatenate(attended, axis=1)
    inputs = own_tokens.astype(jnp.float32)

    def out_part(start, count):
        return dot(lax.dynamic_slice_in_dim(attended, start, count, 0), out_full, 1, 1)

    def small_vectors(gated, unused):
        smalls = gated
        vectors = smalls[:, :8, :drow].transpose(1, 0, 2).reshape(8, width)
        up_bias = lax.dynamic_slice_in_dim(
            smalls[:, 16 : 16 + up_rows, :hrow], ctx_place * (up_rows // 2), up_rows // 2, 1
        )
        up_bias = up_bias.transpose(1, 0, 2).reshape(1, -1)
        return (vectors, up_bias, down_full), ()

    attn_sum, (vectors, up_bias_part, down_full), unused = sum_tp(
        out_part, block_len, core_place, small_vectors, smalls
    )
    gain_one, shift_one, gain_two, shift_two, out_bias, down_bias = (vectors[i] for i in range(6))
    middle = inputs + (attn_sum.astype(jnp.float32) + out_bias)
    normed_two = normalize(middle, gain_two, shift_two).astype(jnp.bfloat16)
    def hidden(rows):
        return dot(rows, up_full, 1, 0) + up_bias_part

    def hidden_grad(pre, grads):
        grad_activated = dot(grads, down_full, 1, 0)
        value, gelu_pull = jax.vjp(gelu_tanh, pre)
        return gelu_pull(grad_activated)[0].astype(jnp.bfloat16)

    half_rows = lax.dynamic_slice_in_dim(normed_two, core_place * half, half, 0)
    half_rows, late_normed = lax.optimization_barrier((half_rows, normed_two))
    got = swap(half_rows, "ctx")
    own_pre = hidden(late_normed)
    own_active = gelu_tanh(own_pre).astype(jnp.bfloat16)
    other_grad = jnp.concatenate([grad_got, grad_turned])
    own_hidden = hidden_grad(own_pre, own_grad)
    got, own_hidden, own_active, other_grad = lax.optimization_barrier(
        (got, own_hidden, own_active, other_grad)
    )
    other_normed = jnp.concatenate([got, swap(got, "tp", CORE)])
    other_pre = hidden(other_normed)
    other_active = gelu_tanh(other_pre).astype(jnp.bfloat16)
    other_hidden = hidden_grad(other_pre, other_grad)

    up_kept, up_sent = chip_parts(own_hidden, other_hidden, up_full, core_place)
    up_sent, own_active, other_active, own_hidden, other_hidden = lax.optimization_barrier(
        (up_sent, own_active, other_active, own_hidden, other_hidden)
    )
    up_got = swap(up_sent, "ctx")
    up_product = (
        dot(normed_two, own_hidden, 0, 0) + dot(other_normed, other_hidden, 0, 0)
    ).astype(jnp.bfloat16)
    mlp_kept, mlp_sent = chip_parts(own_active, other_active, down_full, core_place)
    up_got, up_product, mlp_kept, mlp_sent = lax.optimization_barrier(
        (up_got, up_product, mlp_kept, mlp_sent)
    )
    up_rows_sum = row_major(scatter_rows(up_product))
    up_pair = pair_sum(up_kept, up_got)
    up_pair, own_active, other_active, own_hidden, other_hidden, own_grad, mlp_sent = (
        lax.optimization_barrier(
            (up_pair, own_active, other_active, own_hidden, other_hidden, own_grad, mlp_sent)
        )
    )
    up_across = swap(up_pair, "tp", CHIP)
    mlp_got = swap(mlp_sent, "ctx")
    down_product = (
        dot(own_grad, own_active, 0, 0) + dot(other_grad, other_active, 0, 0)
    ).astype(jnp.bfloat16)
    grad_up_bias = jnp.sum(own_hidden.astype(jnp.float32), axis=0) + jnp.sum(
        other_hidden.astype(jnp.float32), axis=0
    )
    grad_down_bias = jnp.sum(own_grad.astype(jnp.float32), axis=0)
    up_across, mlp_got, down_product, grad_up_bias, grad_down_bias = lax.optimization_barrier(
        (up_across, mlp_got, down_product, grad_up_bias, grad_down_bias)
    )
    down_rows = row_major(scatter_rows(down_product))
    up_total = pair_sum(up_pair, up_across)
    grad_normed_two = jnp.concatenate(
        ordered(core_place, up_total, swap(up_total, "tp", CORE))
    ).astype(jnp.float32)
    grad_out = own_grad.astype(jnp.float32)
    grad_middle_norm, grad_gain_two, grad_shift_two = normalize_back(
        middle, gain_two, grad_normed_two
    )
    grad_middle = grad_out + grad_middle_norm
    grad_branch_low = grad_middle.astype(jnp.bfloat16)
    grad_out_bias = jnp.sum(grad_branch_low.astype(jnp.float32), axis=0)
    grad_attended_low = dot(grad_branch_low, out_full, 1, 0).astype(jnp.bfloat16)
    own_cols = lax.dynamic_slice_in_dim(grad_attended_low, ctx_place * part_width, part_width, 1)
    sent_cols = lax.dynamic_slice_in_dim(
        grad_attended_low, (1 - ctx_place) * part_width, part_width, 1
    )
    sent_cols, late_branch, mlp_got, mlp_kept = lax.optimization_barrier(
        (sent_cols, grad_branch_low, mlp_got, mlp_kept)
    )
    got_cols = swap(sent_cols, "ctx")
    mlp_pair = pair_sum(mlp_kept, mlp_got)
    mlp_across = swap(mlp_pair, "tp", CHIP)
    kept_out, sent_out = weight_product(late_branch, attended, ctx_place)
    got_cols, kept_out, sent_out = lax.optimization_barrier((got_cols, kept_out, sent_out))
    grad_heads = jnp.concatenate(ordered(ctx_place, own_cols, got_cols))
    grad_qkv_part, bias_sums = pl.pallas_call(
        functools.partial(attend_back_kernel, rows, score_scale),
        out_shape=(
            jax.ShapeDtypeStruct((length, 3 * part_width), jnp.bfloat16),
            jax.ShapeDtypeStruct((2, part_width), jnp.float32),
        ),
        scratch_shapes=[
            pltpu.VMEM((length, part_width), jnp.float32),
            pltpu.VMEM((length, part_width), jnp.float32),
        ],
        compiler_params=pltpu.CompilerParams(vmem_limit_bytes=VMEM_LIMIT),
        cost_estimate=pl.CostEstimate(
            flops=10 * length * length * part_width, bytes_accessed=2 * length * width,
            transcendentals=length * length,
        ),
    )(qkv_rows, grad_heads, seg_row, seg_col)
    def token_rows(ctx, core):
        return lax.dynamic_slice_in_dim(grad_qkv_part, (2 * ctx + core) * half, half, 0)

    first_sent = chip_sum_rows(
        token_rows(1 - ctx_place, 1 - core_place), token_rows(1 - ctx_place, core_place), qkv_part
    )
    first_kept = chip_sum_rows(
        token_rows(ctx_place, 1 - core_place), token_rows(ctx_place, core_place), qkv_part
    )
    first_sent, late_part = lax.optimization_barrier((first_sent, grad_qkv_part))
    first_got = swap(first_sent, "ctx")
    grad_qkv_weight = dot(normed_all, late_part, 0, 0).astype(jnp.bfloat16)
    first_got, first_kept, sent_out, mlp_across, mlp_pair = lax.optimization_barrier(
        (first_got, first_kept, sent_out, mlp_across, mlp_pair)
    )
    got_out = swap(sent_out, "ctx")
    grad_qkv_sum = row_major(scatter_rows(grad_qkv_weight)).astype(jnp.float32)
    own_rows = lax.dynamic_slice_in_dim(grad_qkv_sum, ctx_place * drow, drow, 0)
    sent_rows = swap(
        lax.dynamic_slice_in_dim(grad_qkv_sum, (1 - ctx_place) * drow, drow, 0).astype(
            jnp.bfloat16
        ),
        "ctx",
    ).astype(jnp.float32)
    grad_qkv_out = jnp.concatenate(
        [
            part.reshape(drow, 3, part_width)
            for part in ordered(ctx_place, own_rows, sent_rows)
        ],
        axis=2,
    )
    nothing = jnp.zeros_like(bias_sums)
    grad_qv_bias = jnp.concatenate(ordered(ctx_place, bias_sums, nothing), axis=1)

    def by_owner(vector):
        return vector.reshape(owners, 1, drow)

    def row_block(array, first):
        rows, lanes = array.shape[1:]
        return jnp.pad(
            array, ((0, 0), (first, small_rows - first - rows), (0, LANES - lanes))
        )

    def small_work(gated, chip_sum):
        up_rows_sum, down_rows, grad_up_bias, mlp_pair, mlp_across, kept_out = gated
        ffn_rows = jnp.stack([up_rows_sum, down_rows]).reshape(2, 2, drow, part_hidden)
        ffn_kept, ffn_sent = ordered(ctx_place, ffn_rows[:, 0], ffn_rows[:, 1])
        ffn_got = swap(ffn_sent, "ctx")
        half_inputs = lax.dynamic_slice_in_dim(inputs, core_place * half, half, 0)
        half_grad = chip_sum.astype(jnp.float32)
        unused, gain_share, shift_share = normalize_back(half_inputs, gain_one, half_grad)
        up_bias_rows = grad_up_bias.reshape(up_rows // 2, HD)
        up_bias_rows = jnp.concatenate(
            ordered(ctx_place, up_bias_rows, jnp.zeros_like(up_bias_rows))
        )
        small_grads = row_block(
            up_bias_rows.reshape(up_rows, owners, hrow).transpose(1, 0, 2), 16
        ) + row_block(grad_qv_bias.reshape(qv_rows, owners, hrow).transpose(1, 0, 2), 8)
        for place, vector in enumerate(
            (
                gain_share,
                shift_share,
                grad_gain_two,
                grad_shift_two,
                grad_out_bias,
                grad_down_bias,
            )
        ):
            small_grads = small_grads + row_block(by_owner(vector), place)
        small_sums = jnp.sum(
            lax.all_to_all(small_grads, ("fsdp", "ctx"), 0, 0, tiled=True), axis=0
        )
        mlp_total = pair_sum(mlp_pair, mlp_across)
        return (small_sums, ffn_kept, mlp_total, pair_sum(kept_out, got_out)), ffn_got

    first_pair = pair_sum(first_kept, first_got)
    first_pair, gated = lax.optimization_barrier(
        (
            first_pair,
            (up_rows_sum, down_rows, grad_up_bias, mlp_pair, mlp_across, kept_out),
        )
    )
    first_across = swap(first_pair, "tp", CHIP)
    done, ffn_got = small_work(gated, first_pair)
    first_across, done = lax.optimization_barrier((first_across, done))
    small_sums, ffn_kept, mlp_total, out_pairs = done
    grad_out_weight = row_major(scatter_rows(out_pairs))
    first_total = pair_sum(first_pair, first_across)
    first_sum = jnp.concatenate(
        ordered(core_place, first_total, swap(first_total, "tp", CORE))
    )
    grad_up, grad_down = jnp.concatenate(ordered(ctx_place, ffn_kept, ffn_got), axis=2)
    mlp_sum = jnp.concatenate(ordered(core_place, mlp_total, swap(mlp_total, "tp", CORE)))
    finished = middle + (mlp_sum.astype(jnp.float32) + down_bias)
    grad_inputs_norm, unused, unused = normalize_back(
        inputs, gain_one, first_sum.astype(jnp.float32)
    )
    grad_inputs = grad_middle + grad_inputs_norm
    share = small_sums[:2]
    share = share + swap(share, "tp", CORE)
    share = share + swap(share, "tp", CHIP)
    gain_one_sum, shift_one_sum = share[0, :drow], share[1, :drow]
    vector_sums = small_sums[:8, :drow]
    up_bias_sum = small_sums[16 : 16 + up_rows, :hrow]
    qv_bias_sum = small_sums[8 : 8 + qv_rows, :hrow].reshape(2, heads_local, hrow)

    return (
        finished.astype(jnp.bfloat16)[None],
        grad_inputs[None],
        grad_qkv_out,
        qv_bias_sum,
        grad_out_weight.T.astype(jnp.float32),
        vector_sums[4],
        grad_up.astype(jnp.float32),
        up_bias_sum,
        grad_down.T.astype(jnp.float32),
        vector_sums[5],
        gain_one_sum,
        shift_one_sum,
        vector_sums[2],
        vector_sums[3],
    )


def solution(mesh):
    placed = (
        P("fsdp", "ctx", None),
        P("fsdp", None),
        P(("fsdp", "ctx"), None, "tp"),
        P(None, "tp", ("fsdp", "ctx")),
        P("tp", ("fsdp", "ctx")),
        P(("fsdp", "ctx")),
        P(("fsdp", "ctx"), "tp"),
        P("tp", ("fsdp", "ctx")),
        P("tp", ("fsdp", "ctx")),
        P(("fsdp", "ctx")),
        P(("fsdp", "ctx")),
        P(("fsdp", "ctx")),
        P(("fsdp", "ctx")),
        P(("fsdp", "ctx")),
        P("fsdp", "ctx", None),
    )
    return jax.shard_map(
        local,
        mesh=mesh,
        in_specs=placed,
        out_specs=(
            P("fsdp", "ctx", None),
            P("fsdp", "ctx", None),
            P(("fsdp", "ctx"), None, "tp"),
            P(None, "tp", ("fsdp", "ctx")),
            P("tp", ("fsdp", "ctx")),
            P(("fsdp", "ctx")),
            P(("fsdp", "ctx"), "tp"),
            P("tp", ("fsdp", "ctx")),
            P("tp", ("fsdp", "ctx")),
            P(("fsdp", "ctx")),
            P(("fsdp", "ctx")),
            P(("fsdp", "ctx")),
            P(("fsdp", "ctx")),
            P(("fsdp", "ctx")),
        ),
        check_vma=False,
    )
```

```python
import functools

import jax
import jax.numpy as jnp
from jax import lax
from jax.experimental import pallas as pl
from jax.experimental.layout import Layout, with_layout_constraint
from jax.experimental.pallas import tpu as pltpu
from jax.sharding import PartitionSpec as P

HD = 64
LANES = 128
CORE = 1
CHIP = 2
VMEM_LIMIT = 16 * 1024 * 1024

epsilon = 1e-05
negative = -1e30


def swap(array, axis, mask=1):
    devices = lax.axis_size(axis)
    return lax.ppermute(array, axis, [(i, i ^ mask) for i in range(devices)])


def ordered(place, own, other):
    return jnp.where(place == 0, own, other), jnp.where(place == 0, other, own)


def gather_fsdp(block):
    devices = lax.axis_size("fsdp")
    return lax.all_to_all(
        jnp.broadcast_to(block[None], (devices,) + block.shape), "fsdp", 0, 0, tiled=True
    )


def gather_rows(block):
    return lax.all_gather(block, "fsdp", axis=0, tiled=True)


def row_major(array):
    return with_layout_constraint(array, Layout(tuple(range(array.ndim))))


def sum_tp(part_of, rows, core_place, work=None, gated=()):
    half = rows // 2
    sent = swap(part_of((1 - core_place) * half, half).astype(jnp.bfloat16), "tp", CORE)
    kept = part_of(core_place * half, half)
    chip_sum = (kept + sent.astype(jnp.float32)).astype(jnp.bfloat16)
    chip_sum, gated = lax.optimization_barrier((chip_sum, gated))
    across = swap(chip_sum, "tp", CHIP)
    done, free = work(gated, chip_sum) if work else ((), ())
    across, done = lax.optimization_barrier((across, done))
    total = (chip_sum.astype(jnp.float32) + across.astype(jnp.float32)).astype(jnp.bfloat16)
    summed = jnp.concatenate(ordered(core_place, total, swap(total, "tp", CORE)), axis=0)
    return summed, done, free


def other_tokens(rows, core_place):
    half = rows.shape[0] // 2
    got = swap(lax.dynamic_slice_in_dim(rows, core_place * half, half, 0), "ctx")
    return got, swap(got, "tp", CORE)


def chip_sum_rows(sent, kept, right):
    sent = swap(dot(sent, right, 1, 1).astype(jnp.bfloat16), "tp", CORE)
    return (dot(kept, right, 1, 1) + sent.astype(jnp.float32)).astype(jnp.bfloat16)


def chip_parts(own, other, right, core_place):
    half = own.shape[0] // 2
    return (
        chip_sum_rows(
            lax.dynamic_slice_in_dim(own, (1 - core_place) * half, half, 0),
            lax.dynamic_slice_in_dim(own, core_place * half, half, 0),
            right,
        ),
        chip_sum_rows(other[half:], other[:half], right),
    )


def weight_product(wide, narrow, ctx_place):
    devices = lax.axis_size("fsdp")
    rows = wide.shape[1] // (devices * 2)
    product = dot(wide, narrow, 0, 0).astype(jnp.bfloat16).reshape(devices, 2, rows, -1)
    return tuple(
        part.reshape(devices * rows, -1)
        for part in ordered(ctx_place, product[:, 0], product[:, 1])
    )


def pair_sum(kept, sent):
    return (kept.astype(jnp.float32) + sent.astype(jnp.float32)).astype(jnp.bfloat16)


def scatter_rows(array):
    return lax.psum_scatter(array, "fsdp", scatter_dimension=0, tiled=True)


def normalize(matrix, factor, offset):
    average = jnp.mean(matrix, axis=-1, keepdims=True)
    centered = matrix - average
    spread = jnp.mean(centered * centered, axis=-1, keepdims=True)
    return centered * lax.rsqrt(spread + epsilon) * factor + offset


def normalize_back(matrix, factor, grad):
    average = jnp.mean(matrix, axis=-1, keepdims=True)
    centered = matrix - average
    spread = jnp.mean(centered * centered, axis=-1, keepdims=True)
    inverse = lax.rsqrt(spread + epsilon)
    xhat = centered * inverse
    scaled = grad * factor
    mean_scaled = jnp.mean(scaled, axis=-1, keepdims=True)
    mean_product = jnp.mean(scaled * xhat, axis=-1, keepdims=True)
    grad_in = inverse * (scaled - mean_scaled - xhat * mean_product)
    return grad_in, jnp.sum(grad * xhat, axis=0), jnp.sum(grad, axis=0)


def gelu_tanh(inputs):
    cubed_vals = inputs * inputs * inputs
    return 0.5 * inputs * (1.0 + jnp.tanh(0.7978845608028654 * (inputs + 0.044715 * cubed_vals)))


def dot(left, right, left_dim, right_dim):
    return lax.dot_general(
        left, right, (((left_dim,), (right_dim,)), ((), ())), preferred_element_type=jnp.float32
    )


def head_masks(shape):
    lane = lax.broadcasted_iota(jnp.int32, shape, 1)
    return [(lane // HD) == head for head in range(shape[1] // HD)]


def attend_kernel(
    rows, drow, scale,
    tokens_ref, packs_ref, vectors_ref, bias_ref, seg_row_ref, seg_col_ref,
    normed_ref, qkv_ref, attended_ref, weight_ref, out_ref,
):
    length = tokens_ref.shape[0]
    part = attended_ref.shape[1]
    for owner in range(packs_ref.shape[0]):
        for kind in range(3):
            weight_ref[owner * drow : (owner + 1) * drow, kind * part : (kind + 1) * part] = (
                packs_ref[owner, kind * drow : (kind + 1) * drow, :]
            )
        for side in range(2):
            first = packs_ref.shape[1] - (2 - side) * drow
            out_ref[owner * drow : (owner + 1) * drow, side * part : (side + 1) * part] = (
                packs_ref[owner, first : first + drow, :]
            )
    masks = head_masks((rows, part))
    for block in range(length // rows):
        here = slice(block * rows, (block + 1) * rows)
        seen = (block + 1) * rows
        inputs = tokens_ref[here, :].astype(jnp.float32)
        centered = inputs - jnp.mean(inputs, axis=-1, keepdims=True)
        spread = jnp.mean(centered * centered, axis=-1, keepdims=True)
        normed = (
            centered * lax.rsqrt(spread + epsilon) * vectors_ref[0:1, :] + vectors_ref[1:2, :]
        ).astype(jnp.bfloat16)
        normed_ref[here, :] = normed
        projected = dot(normed, weight_ref[...], 1, 0) + bias_ref[...]
        qkv_ref[here, :] = projected.astype(jnp.bfloat16)
        queries = qkv_ref[here, :part]
        key_rows = qkv_ref[:seen, part : 2 * part]
        value_rows = qkv_ref[:seen, 2 * part :]
        query_index = block * rows + lax.broadcasted_iota(jnp.int32, (rows, seen), 0)
        key_index = lax.broadcasted_iota(jnp.int32, (rows, seen), 1)
        allowed = (seg_col_ref[here, :] == seg_row_ref[:, :seen]) & (key_index <= query_index)
        result = jnp.zeros((rows, part), jnp.float32)
        for mask in masks:
            scores = dot(jnp.where(mask, queries, 0), key_rows, 1, 1) * scale
            scores = jnp.where(allowed, scores, negative)
            weights = jnp.exp(scores - jnp.max(scores, axis=-1, keepdims=True))
            probs = weights * (1.0 / jnp.sum(weights, axis=-1, keepdims=True))
            result = jnp.where(mask, dot(probs.astype(jnp.bfloat16), value_rows, 1, 0), result)
        attended_ref[here, :] = result.astype(jnp.bfloat16)


def attend_back_kernel(
    rows, scale,
    qkv_ref, grad_ref, seg_row_ref, seg_col_ref,
    out_ref, sums_ref,
    key_sum, value_sum,
):
    length, part = grad_ref.shape
    masks = head_masks((rows, part))
    key_sum[...] = jnp.zeros_like(key_sum)
    value_sum[...] = jnp.zeros_like(value_sum)
    query_total = jnp.zeros((1, part), jnp.float32)
    for block in range(length // rows):
        here = slice(block * rows, (block + 1) * rows)
        seen = (block + 1) * rows
        queries = qkv_ref[here, :part]
        grads = grad_ref[here, :]
        key_rows = qkv_ref[:seen, part : 2 * part]
        value_rows = qkv_ref[:seen, 2 * part :]
        query_index = block * rows + lax.broadcasted_iota(jnp.int32, (seen, rows), 1)
        key_index = lax.broadcasted_iota(jnp.int32, (seen, rows), 0)
        allowed = (seg_col_ref[:seen, :] == seg_row_ref[:, here]) & (key_index <= query_index)
        grad_query = jnp.zeros((rows, part), jnp.float32)
        for mask in masks:
            head_queries = jnp.where(mask, queries, 0)
            head_grads = jnp.where(mask, grads, 0)
            scores = dot(key_rows, head_queries, 1, 1) * scale
            scores = jnp.where(allowed, scores, negative)
            weights = jnp.exp(scores - jnp.max(scores, axis=0, keepdims=True))
            probs = weights * (1.0 / jnp.sum(weights, axis=0, keepdims=True))
            value_sum[:seen, :] += dot(probs.astype(jnp.bfloat16), head_grads, 1, 0)
            grad_probs = dot(value_rows, head_grads, 1, 1)
            inner = jnp.sum(probs * grad_probs, axis=0, keepdims=True)
            grad_scores = (probs * (grad_probs - inner)).astype(jnp.bfloat16)
            key_sum[:seen, :] += dot(grad_scores, head_queries, 1, 0)
            grad_query = jnp.where(mask, dot(grad_scores, key_rows, 0, 0), grad_query)
        grad_query = (grad_query * scale).astype(jnp.bfloat16)
        out_ref[here, :part] = grad_query
        query_total += jnp.sum(grad_query.astype(jnp.float32), axis=0, keepdims=True)
    grad_values = value_sum[...].astype(jnp.bfloat16)
    out_ref[:, part : 2 * part] = (key_sum[...] * scale).astype(jnp.bfloat16)
    out_ref[:, 2 * part :] = grad_values
    sums_ref[0:1, :] = query_total
    sums_ref[1:2, :] = jnp.sum(grad_values.astype(jnp.float32), axis=0, keepdims=True)


def local(
    tokens,
    segments,
    w_qkv,
    b_qv,
    w_out,
    b_out,
    w_up,
    b_up,
    w_down,
    b_down,
    attngain,
    attnshift,
    mlpgain,
    mlpshift,
    cotangent,
):
    fsdp = lax.axis_size("fsdp")
    owners = fsdp * 2
    ctx_place = lax.axis_index("ctx")
    core_place = lax.axis_index("tp") % 2
    block_len, width = tokens.shape[1:]
    length = segments.shape[1]
    local_width = w_qkv.shape[2]
    part_width = local_width // 2
    part_heads = part_width // HD
    heads_local = local_width // HD
    drow = w_qkv.shape[0]
    hrow = b_qv.shape[2]
    score_scale = 1.0 / HD**0.5

    by_kind = jnp.transpose(w_qkv, (1, 0, 2))
    weight_rows = 3 * drow * part_width // LANES
    own_weight = lax.dynamic_slice_in_dim(by_kind, ctx_place * part_width, part_width, 2)
    sent_weight = lax.dynamic_slice_in_dim(by_kind, (1 - ctx_place) * part_width, part_width, 2)
    small_rows = 32
    up_rows = b_up.shape[0]
    qv_rows = b_qv.shape[0] * b_qv.shape[1]

    def padded(array, first):
        array = array.reshape(-1, array.shape[-1])
        rows, lanes = array.shape
        return jnp.pad(array, ((first, small_rows - first - rows), (0, LANES - lanes)))

    small = padded(b_up, 16) + padded(b_qv, 8)
    for place, vector in enumerate((attngain, attnshift, mlpgain, mlpshift, b_out, b_down)):
        small = small + padded(vector, place)
    out_turned = w_out.T
    small = jnp.concatenate([small, out_turned[:, :part_width], out_turned[:, part_width:]])
    own_pack = jnp.concatenate([own_weight.reshape(weight_rows, LANES), small])
    other_pack = swap(
        jnp.concatenate([sent_weight.reshape(weight_rows, LANES), small]), "ctx"
    )
    own_tokens, w_up, w_down, other_pack = lax.optimization_barrier(
        (tokens[0], w_up, w_down, other_pack)
    )
    half = block_len // 2
    other_block = jnp.concatenate(ordered(core_place, *other_tokens(own_tokens, core_place)))
    all_tokens = jnp.concatenate(ordered(ctx_place, own_tokens, other_block))

    part_hidden = w_up.shape[1] // 2
    own_ffn = jnp.concatenate([w_up, row_major(w_down.T)])
    sent_ffn = lax.dynamic_slice_in_dim(own_ffn, (1 - ctx_place) * part_hidden, part_hidden, 1)
    own_ffn = lax.dynamic_slice_in_dim(own_ffn, ctx_place * part_hidden, part_hidden, 1)
    ffn_pair = jnp.stack(ordered(ctx_place, own_ffn, swap(sent_ffn, "ctx")))
    all_tokens, own_grad = lax.optimization_barrier((all_tokens, cotangent[0]))
    grad_got, grad_turned = other_tokens(own_grad, core_place)

    both_packs = jnp.stack(ordered(ctx_place, own_pack, other_pack))
    packs = gather_fsdp(both_packs)
    packs, down_pair = lax.optimization_barrier((packs, ffn_pair[:, drow:]))
    up_full = gather_rows(ffn_pair[:, :drow].reshape(-1, part_hidden))
    down_full = gather_rows(down_pair.reshape(-1, part_hidden))
    packs = packs.reshape(owners, -1, LANES)
    smalls = packs[:, weight_rows : weight_rows + small_rows].astype(jnp.float32)
    first_vectors = smalls[:, :8, :drow].transpose(1, 0, 2).reshape(8, width)
    qv_bias = (
        smalls[:, 8 : 8 + qv_rows, :hrow].transpose(1, 0, 2).reshape(2, local_width)
    )
    qv_bias_part = lax.dynamic_slice_in_dim(qv_bias, ctx_place * part_width, part_width, 1)
    qkv_bias = jnp.concatenate(
        [qv_bias_part[0], jnp.zeros((part_width,), jnp.float32), qv_bias_part[1]]
    )[None]

    seg_row = segments
    seg_col = segments.reshape(length, 1)
    rows = min(256, length)
    normed_all, qkv_rows, attended_part, qkv_part, out_full = pl.pallas_call(
        functools.partial(attend_kernel, rows, drow, score_scale),
        out_shape=(
            jax.ShapeDtypeStruct((length, width), jnp.bfloat16),
            jax.ShapeDtypeStruct((length, 3 * part_width), jnp.bfloat16),
            jax.ShapeDtypeStruct((length, part_width), jnp.bfloat16),
            jax.ShapeDtypeStruct((width, 3 * part_width), jnp.bfloat16),
            jax.ShapeDtypeStruct((width, local_width), jnp.bfloat16),
        ),
        compiler_params=pltpu.CompilerParams(vmem_limit_bytes=VMEM_LIMIT),
        cost_estimate=pl.CostEstimate(
            flops=2 * length * width * 3 * part_width, bytes_accessed=8 * length * width,
            transcendentals=length * length,
        ),
    )(all_tokens, packs, first_vectors, qkv_bias, seg_row, seg_col)

    def to_tokens(array):
        kept = lax.dynamic_slice_in_dim(array, ctx_place * block_len, block_len, 0)
        sent = swap(
            lax.dynamic_slice_in_dim(array, (1 - ctx_place) * block_len, block_len, 0), "ctx"
        )
        return ordered(ctx_place, kept, sent)

    attended = to_tokens(attended_part)
    attended, up_full, grad_got, grad_turned = lax.optimization_barrier(
        (attended, up_full, grad_got, grad_turned)
    )
    attended = jnp.concatenate(attended, axis=1)
    inputs = own_tokens.astype(jnp.float32)

    def out_part(start, count):
        return dot(lax.dynamic_slice_in_dim(attended, start, count, 0), out_full, 1, 1)

    def small_vectors(gated, unused):
        smalls = gated
        vectors = smalls[:, :8, :drow].transpose(1, 0, 2).reshape(8, width)
        up_bias = lax.dynamic_slice_in_dim(
            smalls[:, 16 : 16 + up_rows, :hrow], ctx_place * (up_rows // 2), up_rows // 2, 1
        )
        up_bias = up_bias.transpose(1, 0, 2).reshape(1, -1)
        return (vectors, up_bias, down_full), ()

    attn_sum, (vectors, up_bias_part, down_full), unused = sum_tp(
        out_part, block_len, core_place, small_vectors, smalls
    )
    gain_one, shift_one, gain_two, shift_two, out_bias, down_bias = (vectors[i] for i in range(6))
    middle = inputs + (attn_sum.astype(jnp.float32) + out_bias)
    normed_two = normalize(middle, gain_two, shift_two).astype(jnp.bfloat16)
    def hidden(rows):
        return dot(rows, up_full, 1, 0) + up_bias_part

    def hidden_grad(pre, grads):
        grad_activated = dot(grads, down_full, 1, 0)
        value, gelu_pull = jax.vjp(gelu_tanh, pre)
        return gelu_pull(grad_activated)[0].astype(jnp.bfloat16)

    half_rows = lax.dynamic_slice_in_dim(normed_two, core_place * half, half, 0)
    half_rows, late_normed = lax.optimization_barrier((half_rows, normed_two))
    got = swap(half_rows, "ctx")
    own_pre = hidden(late_normed)
    own_active = gelu_tanh(own_pre).astype(jnp.bfloat16)
    other_grad = jnp.concatenate([grad_got, grad_turned])
    own_hidden = hidden_grad(own_pre, own_grad)
    got, own_hidden, own_active, other_grad = lax.optimization_barrier(
        (got, own_hidden, own_active, other_grad)
    )
    other_normed = jnp.concatenate([got, swap(got, "tp", CORE)])
    other_pre = hidden(other_normed)
    other_active = gelu_tanh(other_pre).astype(jnp.bfloat16)
    other_hidden = hidden_grad(other_pre, other_grad)

    up_kept, up_sent = chip_parts(own_hidden, other_hidden, up_full, core_place)
    up_sent, own_active, other_active, own_hidden, other_hidden = lax.optimization_barrier(
        (up_sent, own_active, other_active, own_hidden, other_hidden)
    )
    up_got = swap(up_sent, "ctx")
    up_product = (
        dot(normed_two, own_hidden, 0, 0) + dot(other_normed, other_hidden, 0, 0)
    ).astype(jnp.bfloat16)
    mlp_kept, mlp_sent = chip_parts(own_active, other_active, down_full, core_place)
    up_got, up_product, mlp_kept, mlp_sent = lax.optimization_barrier(
        (up_got, up_product, mlp_kept, mlp_sent)
    )
    up_rows_sum = row_major(scatter_rows(up_product))
    up_pair = pair_sum(up_kept, up_got)
    up_pair, own_active, other_active, own_hidden, other_hidden, own_grad, mlp_sent = (
        lax.optimization_barrier(
            (up_pair, own_active, other_active, own_hidden, other_hidden, own_grad, mlp_sent)
        )
    )
    up_across = swap(up_pair, "tp", CHIP)
    mlp_got = swap(mlp_sent, "ctx")
    down_product = (
        dot(own_grad, own_active, 0, 0) + dot(other_grad, other_active, 0, 0)
    ).astype(jnp.bfloat16)
    grad_up_bias = jnp.sum(own_hidden.astype(jnp.float32), axis=0) + jnp.sum(
        other_hidden.astype(jnp.float32), axis=0
    )
    grad_down_bias = jnp.sum(own_grad.astype(jnp.float32), axis=0)
    up_across, mlp_got, down_product, grad_up_bias, grad_down_bias = lax.optimization_barrier(
        (up_across, mlp_got, down_product, grad_up_bias, grad_down_bias)
    )
    down_rows = row_major(scatter_rows(down_product))
    up_total = pair_sum(up_pair, up_across)
    grad_normed_two = jnp.concatenate(
        ordered(core_place, up_total, swap(up_total, "tp", CORE))
    ).astype(jnp.float32)
    grad_out = own_grad.astype(jnp.float32)
    grad_middle_norm, grad_gain_two, grad_shift_two = normalize_back(
        middle, gain_two, grad_normed_two
    )
    grad_middle = grad_out + grad_middle_norm
    grad_branch_low = grad_middle.astype(jnp.bfloat16)
    grad_out_bias = jnp.sum(grad_branch_low.astype(jnp.float32), axis=0)
    grad_attended_low = dot(grad_branch_low, out_full, 1, 0).astype(jnp.bfloat16)
    own_cols = lax.dynamic_slice_in_dim(grad_attended_low, ctx_place * part_width, part_width, 1)
    sent_cols = lax.dynamic_slice_in_dim(
        grad_attended_low, (1 - ctx_place) * part_width, part_width, 1
    )
    sent_cols, late_branch, mlp_got, mlp_kept = lax.optimization_barrier(
        (sent_cols, grad_branch_low, mlp_got, mlp_kept)
    )
    got_cols = swap(sent_cols, "ctx")
    mlp_pair = pair_sum(mlp_kept, mlp_got)
    mlp_across = swap(mlp_pair, "tp", CHIP)
    kept_out, sent_out = weight_product(late_branch, attended, ctx_place)
    got_cols, kept_out, sent_out = lax.optimization_barrier((got_cols, kept_out, sent_out))
    grad_heads = jnp.concatenate(ordered(ctx_place, own_cols, got_cols))
    grad_qkv_part, bias_sums = pl.pallas_call(
        functools.partial(attend_back_kernel, rows, score_scale),
        out_shape=(
            jax.ShapeDtypeStruct((length, 3 * part_width), jnp.bfloat16),
            jax.ShapeDtypeStruct((2, part_width), jnp.float32),
        ),
        scratch_shapes=[
            pltpu.VMEM((length, part_width), jnp.float32),
            pltpu.VMEM((length, part_width), jnp.float32),
        ],
        compiler_params=pltpu.CompilerParams(vmem_limit_bytes=VMEM_LIMIT),
        cost_estimate=pl.CostEstimate(
            flops=10 * length * length * part_width, bytes_accessed=2 * length * width,
            transcendentals=length * length,
        ),
    )(qkv_rows, grad_heads, seg_row, seg_col)
    def token_rows(ctx, core):
        return lax.dynamic_slice_in_dim(grad_qkv_part, (2 * ctx + core) * half, half, 0)

    first_sent = chip_sum_rows(
        token_rows(1 - ctx_place, 1 - core_place), token_rows(1 - ctx_place, core_place), qkv_part
    )
    first_kept = chip_sum_rows(
        token_rows(ctx_place, 1 - core_place), token_rows(ctx_place, core_place), qkv_part
    )
    first_sent, late_part = lax.optimization_barrier((first_sent, grad_qkv_part))
    first_got = swap(first_sent, "ctx")
    grad_qkv_weight = dot(normed_all, late_part, 0, 0).astype(jnp.bfloat16)
    first_got, first_kept, sent_out, mlp_across, mlp_pair = lax.optimization_barrier(
        (first_got, first_kept, sent_out, mlp_across, mlp_pair)
    )
    got_out = swap(sent_out, "ctx")
    grad_qkv_sum = row_major(scatter_rows(grad_qkv_weight)).astype(jnp.float32)
    own_rows = lax.dynamic_slice_in_dim(grad_qkv_sum, ctx_place * drow, drow, 0)
    sent_rows = swap(
        lax.dynamic_slice_in_dim(grad_qkv_sum, (1 - ctx_place) * drow, drow, 0).astype(
            jnp.bfloat16
        ),
        "ctx",
    ).astype(jnp.float32)
    grad_qkv_out = jnp.concatenate(
        [
            part.reshape(drow, 3, part_width)
            for part in ordered(ctx_place, own_rows, sent_rows)
        ],
        axis=2,
    )
    nothing = jnp.zeros_like(bias_sums)
    grad_qv_bias = jnp.concatenate(ordered(ctx_place, bias_sums, nothing), axis=1)

    def by_owner(vector):
        return vector.reshape(owners, 1, drow)

    def row_block(array, first):
        rows, lanes = array.shape[1:]
        return jnp.pad(
            array, ((0, 0), (first, small_rows - first - rows), (0, LANES - lanes))
        )

    def small_work(gated, chip_sum):
        up_rows_sum, down_rows, grad_up_bias, mlp_pair, mlp_across, kept_out = gated
        ffn_rows = jnp.stack([up_rows_sum, down_rows]).reshape(2, 2, drow, part_hidden)
        ffn_kept, ffn_sent = ordered(ctx_place, ffn_rows[:, 0], ffn_rows[:, 1])
        ffn_got = swap(ffn_sent, "ctx")
        half_inputs = lax.dynamic_slice_in_dim(inputs, core_place * half, half, 0)
        half_grad = chip_sum.astype(jnp.float32)
        unused, gain_share, shift_share = normalize_back(half_inputs, gain_one, half_grad)
        up_bias_rows = grad_up_bias.reshape(up_rows // 2, HD)
        up_bias_rows = jnp.concatenate(
            ordered(ctx_place, up_bias_rows, jnp.zeros_like(up_bias_rows))
        )
        small_grads = row_block(
            up_bias_rows.reshape(up_rows, owners, hrow).transpose(1, 0, 2), 16
        ) + row_block(grad_qv_bias.reshape(qv_rows, owners, hrow).transpose(1, 0, 2), 8)
        for place, vector in enumerate(
            (
                gain_share,
                shift_share,
                grad_gain_two,
                grad_shift_two,
                grad_out_bias,
                grad_down_bias,
            )
        ):
            small_grads = small_grads + row_block(by_owner(vector), place)
        small_sums = jnp.sum(
            lax.all_to_all(small_grads, ("fsdp", "ctx"), 0, 0, tiled=True), axis=0
        )
        mlp_total = pair_sum(mlp_pair, mlp_across)
        return (small_sums, ffn_kept, mlp_total, pair_sum(kept_out, got_out)), ffn_got

    first_pair = pair_sum(first_kept, first_got)
    first_pair, gated = lax.optimization_barrier(
        (
            first_pair,
            (up_rows_sum, down_rows, grad_up_bias, mlp_pair, mlp_across, kept_out),
        )
    )
    first_across = swap(first_pair, "tp", CHIP)
    done, ffn_got = small_work(gated, first_pair)
    first_across, done = lax.optimization_barrier((first_across, done))
    small_sums, ffn_kept, mlp_total, out_pairs = done
    grad_out_weight = jnp.sum(
        lax.all_to_all(
            out_pairs.reshape(fsdp, drow, local_width), "fsdp", 0, 0, tiled=True
        ).astype(jnp.float32),
        axis=0,
    )
    first_total = pair_sum(first_pair, first_across)
    first_sum = jnp.concatenate(
        ordered(core_place, first_total, swap(first_total, "tp", CORE))
    )
    grad_up, grad_down = jnp.concatenate(ordered(ctx_place, ffn_kept, ffn_got), axis=2)
    mlp_sum = jnp.concatenate(ordered(core_place, mlp_total, swap(mlp_total, "tp", CORE)))
    finished = middle + (mlp_sum.astype(jnp.float32) + down_bias)
    grad_inputs_norm, unused, unused = normalize_back(
        inputs, gain_one, first_sum.astype(jnp.float32)
    )
    grad_inputs = grad_middle + grad_inputs_norm
    share = small_sums[:2]
    share = share + swap(share, "tp", CORE)
    share = share + swap(share, "tp", CHIP)
    gain_one_sum, shift_one_sum = share[0, :drow], share[1, :drow]
    vector_sums = small_sums[:8, :drow]
    up_bias_sum = small_sums[16 : 16 + up_rows, :hrow]
    qv_bias_sum = small_sums[8 : 8 + qv_rows, :hrow].reshape(2, heads_local, hrow)

    return (
        finished.astype(jnp.bfloat16)[None],
        grad_inputs[None],
        grad_qkv_out,
        qv_bias_sum,
        grad_out_weight.T,
        vector_sums[4],
        grad_up.astype(jnp.float32),
        up_bias_sum,
        grad_down.T.astype(jnp.float32),
        vector_sums[5],
        gain_one_sum,
        shift_one_sum,
        vector_sums[2],
        vector_sums[3],
    )


def solution(mesh):
    placed = (
        P("fsdp", "ctx", None),
        P("fsdp", None),
        P(("fsdp", "ctx"), None, "tp"),
        P(None, "tp", ("fsdp", "ctx")),
        P("tp", ("fsdp", "ctx")),
        P(("fsdp", "ctx")),
        P(("fsdp", "ctx"), "tp"),
        P("tp", ("fsdp", "ctx")),
        P("tp", ("fsdp", "ctx")),
        P(("fsdp", "ctx")),
        P(("fsdp", "ctx")),
        P(("fsdp", "ctx")),
        P(("fsdp", "ctx")),
        P(("fsdp", "ctx")),
        P("fsdp", "ctx", None),
    )
    return jax.shard_map(
        local,
        mesh=mesh,
        in_specs=placed,
        out_specs=(
            P("fsdp", "ctx", None),
            P("fsdp", "ctx", None),
            P(("fsdp", "ctx"), None, "tp"),
            P(None, "tp", ("fsdp", "ctx")),
            P("tp", ("fsdp", "ctx")),
            P(("fsdp", "ctx")),
            P(("fsdp", "ctx"), "tp"),
            P("tp", ("fsdp", "ctx")),
            P("tp", ("fsdp", "ctx")),
            P(("fsdp", "ctx")),
            P(("fsdp", "ctx")),
            P(("fsdp", "ctx")),
            P(("fsdp", "ctx")),
            P(("fsdp", "ctx")),
        ),
        check_vma=False,
    )
```
